256 devices in a mesh: gx: 16 (over x, z_hi), gy: 16 (over y, z_lo, core).
Axes of the slice: x: 4, y: 4, z: 8 (z_hi: 4, z_lo: 2; z = z_hi * 2 + z_lo), core: 2. Of those that a mesh axis runs over, the one named last changes fastest.
Arguments:
- right_side: float32 [3, 128, 512, 128], P(None, 'gx', 'gy'), may hold values from -6 to 6
- classes: int32 [128, 512, 128], P('gx', 'gy'), may hold values from 0 to 15
- table: float32 [16], replicated, may hold values from 0.05 to 4
Outputs:
- correction: float32 [3, 128, 512, 128], P(None, 'gx', 'gy')
The draws below stay inside these ranges and needn't reach their ends.
All inputs are finite; a program needn't handle non-finite values.
Results may differ from the reference program's by a relative error of at most 0.000026.
Values sent between devices are 32-bit elements; how exact they have to be, the bound alone decides.
A program may use at most 64 MiB of HBM per device.

```python
import math
import jax
import jax.numpy as jnp
from jax import lax

NZ = 128
EDGE_SWEEPS = 4
NODE_SWEEPS = 4
COARSE_SWEEPS = 8
CLASSES = 16
NX = 128
NY = 512


def draw_right_side(key, part):
    key = jax.random.fold_in(key, 11)
    shape = (3, NX, NY, NZ)
    return jnp.clip(jax.random.normal(key, shape, jnp.float32), -6.0, 6.0)


def set_ends(entries, rng, least, high):
    place = [jax.random.randint(jax.random.fold_in(rng, axis), (), 0, length) for axis, length in enumerate(entries.shape)]
    longest = entries.shape.index(max(entries.shape))
    next_to = place[:longest] + [(place[longest] + 1) % entries.shape[longest]] + place[longest + 1:]
    return entries.at[tuple(place)].set(least).at[tuple(next_to)].set(high)


def setup_inputs(seed: int = 0) -> dict:
    splits = jax.random.split(jax.random.key(seed), 4)
    right_side = draw_right_side(jax.random.fold_in(splits[3], 71), 0)
    classes = set_ends(jax.random.randint(splits[1], (NX, NY, NZ), 0, CLASSES), jax.random.fold_in(splits[1], 1), 0, CLASSES - 1).astype(jnp.int32)
    table = jnp.clip(jnp.exp(jax.random.uniform(splits[2], (CLASSES,), jnp.float32, math.log(0.05), math.log(4.0))), 0.05, 4.0)
    return dict(right_side=right_side, classes=classes, table=table)


edge_top = 20.0
node_top = 48.0
coarse_top = 96.0


def ahead(field, axis):
    count = field.shape[axis]
    tail = jnp.zeros_like(lax.slice_in_dim(field, 0, 1, axis=axis))
    return jnp.concatenate([lax.slice_in_dim(field, 1, count, axis=axis), tail], axis=axis)


def behind(field, axis):
    count = field.shape[axis]
    head = jnp.zeros_like(lax.slice_in_dim(field, 0, 1, axis=axis))
    return jnp.concatenate([head, lax.slice_in_dim(field, 0, count - 1, axis=axis)], axis=axis)


def forward(field, axis):
    return ahead(field, axis) - field


def adjoint(field, axis):
    return behind(field, axis) - field


def curl(edges):
    return jnp.stack([forward(edges[2], 1) - forward(edges[1], 2),
                      forward(edges[0], 2) - forward(edges[2], 0),
                      forward(edges[1], 0) - forward(edges[0], 1)])


def curl_adjoint(faces):
    return jnp.stack([adjoint(faces[2], 1) - adjoint(faces[1], 2),
                      adjoint(faces[0], 2) - adjoint(faces[2], 0),
                      adjoint(faces[1], 0) - adjoint(faces[0], 1)])


def gradient(nodes):
    return jnp.stack([forward(nodes, 0), forward(nodes, 1), forward(nodes, 2)])


def divergence(edges):
    return adjoint(edges[0], 0) + adjoint(edges[1], 1) + adjoint(edges[2], 2)


def chebyshev(apply, rhs, top, ratio, count, need_residual):
    low = top / ratio
    center = 0.5 * (top + low)
    radius = 0.5 * (top - low)
    sharp = center / radius
    rho = 1.0 / sharp
    update = rhs / center
    result = update
    residual = rhs
    if count > 1 or need_residual:
        residual = rhs - apply(update)
    for turn in range(1, count):
        rho_next = 1.0 / (2.0 * sharp - rho)
        update = (rho_next * rho) * update + (2.0 * rho_next / radius) * residual
        result = result + update
        if turn + 1 < count or need_residual:
            residual = residual - apply(update)
        rho = rho_next
    return result, residual


def lower_pad(field, axis):
    head = jnp.zeros_like(lax.slice_in_dim(field, 0, 1, axis=axis))
    return jnp.concatenate([head, field], axis=axis)


def upper_pad(field, axis):
    tail = jnp.zeros_like(lax.slice_in_dim(field, 0, 1, axis=axis))
    return jnp.concatenate([field, tail], axis=axis)


def reduce_pairs(field, axis):
    count = field.shape[axis]
    lower = lax.slice_in_dim(field, 0, 1, axis=axis)
    even = lax.slice_in_dim(field, 1, count, 2, axis=axis)
    odd = lax.slice_in_dim(field, 2, count, 2, axis=axis)
    before = jnp.concatenate([lower, lax.slice_in_dim(odd, 0, odd.shape[axis] - 1, axis=axis)], axis=axis)
    return even + 0.5 * (odd + before)


def spread_pairs(field, axis):
    count = field.shape[axis]
    own = lax.slice_in_dim(field, 0, count - 1, axis=axis)
    upper = lax.slice_in_dim(field, 1, count, axis=axis)
    middle = 0.5 * (own + upper)
    joined = jnp.stack([own, middle], axis=axis + 1)
    shape = list(own.shape)
    shape[axis] = shape[axis] * 2
    return joined.reshape(shape)


def block_mean(field):
    a_len, b_len, c_len = field.shape
    return field.reshape(a_len // 2, 2, b_len // 2, 2, c_len // 2, 2).mean(axis=(1, 3, 5))


def reference(right_side, classes, table):
    sigma = table[classes]

    def apply_edges(edges):
        return curl_adjoint(curl(edges)) + sigma[None] * edges

    edge_smooth, edge_residual = chebyshev(apply_edges, right_side, edge_top, 30.0, EDGE_SWEEPS, True)
    nodal_rhs = -divergence(edge_residual)

    def apply_nodes(nodes):
        return -divergence(sigma[None] * gradient(nodes))

    node_smooth, node_residual = chebyshev(apply_nodes, nodal_rhs, node_top, 30.0, NODE_SWEEPS, True)
    reduced = reduce_pairs(lower_pad(node_residual, 2), 2)
    reduced = reduce_pairs(lower_pad(reduced, 0), 0)
    coarse_rhs = reduce_pairs(lower_pad(reduced, 1), 1)
    coarse_sigma = block_mean(sigma)

    def apply_coarse(nodes):
        return -2.0 * divergence(coarse_sigma[None] * gradient(nodes))

    coarse_answer, spare = chebyshev(apply_coarse, coarse_rhs, coarse_top, 100.0, COARSE_SWEEPS, False)
    fine = spread_pairs(upper_pad(coarse_answer, 0), 0)
    fine = spread_pairs(upper_pad(fine, 1), 1)
    fine = spread_pairs(upper_pad(fine, 2), 2)
    return edge_smooth + gradient(node_smooth + fine)
```

```python
import functools

import jax
import jax.numpy as jnp
from jax import lax
from jax.experimental import pallas as pl
from jax.experimental.pallas import tpu as pltpu
from jax.sharding import PartitionSpec as P

MESH = pl.DeviceIdType.MESH
ROWS = 48


def coefficients(top, ratio, count):
    low = top / ratio
    center = 0.5 * (top + low)
    radius = 0.5 * (top - low)
    sharp = center / radius
    rho = 1.0 / sharp
    steps = []
    for _ in range(1, count):
        rho_next = 1.0 / (2.0 * sharp - rho)
        steps.append((rho_next * rho, 2.0 * rho_next / radius))
        rho = rho_next
    return 1.0 / center, steps


def roll(value, shift, axis):
    return pltpu.roll(value, shift % value.shape[axis], axis)


def kernel(nx, ny, rhs, classes, table, out, base, kinds, sig, upd, res, acc,
           pack_dn, pack_up, got_dn, got_up, nod, node_sum, red, cs_main, cs_dn, cs_up,
           cf_main, cf_dn, cf_up, cm_one, g_one, g_two, s_one, s_two, fine,
           sem_in, send, recv, far_send, far_recv, x2_send, x2_recv, cs_send, cs_recv, x3_send, x3_recv):
    gx, gy = lax.axis_index("gx"), lax.axis_index("gy")
    first_x, last_x, first_y, last_y = gx == 0, gx == nx - 1, gy == 0, gy == ny - 1

    def at(dx, dy):
        return (lax.rem(gx + dx + nx, nx), lax.rem(gy + dy + ny, ny))

    near = [(1, 0), (-1, 0), (0, 1), (0, -1), (1, 1), (1, -1), (-1, 1), (-1, -1)]
    distant = [(2, 0), (-2, 0), (2, 1), (2, -1), (-2, 1), (-2, -1)]

    def remote(source, target, sems, index, where):
        return pltpu.make_async_remote_copy(
            src_ref=source, dst_ref=target, send_sem=sems[0].at[index], recv_sem=sems[1].at[index],
            device_id=at(*where), device_id_type=MESH)

    barrier = pltpu.get_barrier_semaphore()
    for where in near + distant:
        pl.semaphore_signal(barrier, inc=1, device_id=at(*where), device_id_type=MESH)
    load_rhs = pltpu.make_async_copy(rhs, base.at[:, 3:11, 0:32], sem_in.at[0])
    load_kinds = pltpu.make_async_copy(classes, kinds, sem_in.at[1])
    load_rhs.start()
    load_kinds.start()

    load_kinds.wait()
    values = [table[k] for k in range(16)]
    for x in range(8):
        code = kinds[x]
        level = values
        for bit in range(4):
            flag = (code & (1 << bit)) != 0
            level = [jnp.where(flag, level[2 * i + 1], level[2 * i]) for i in range(len(level) // 2)]
        sig[x + 4, 0:32] = level[0]
    load_rhs.wait()

    pl.semaphore_wait(barrier, len(near + distant))
    x1 = (send, recv)
    first = [
        remote(base.at[:, 8:11, 0:32], base.at[:, 0:3, 0:32], x1, 0, (1, 0)),
        remote(base.at[:, 3:6, 0:32], base.at[:, 11:14, 0:32], x1, 1, (-1, 0)),
    ]
    for copy in first:
        copy.start()

    sub = lax.broadcasted_iota(jnp.int32, (8, 128), 0)
    lower = sub < 4
    for x in range(8):
        ux, uy, uz = (base[c, x + 3, 0:8] for c in range(3))
        sg = sig[x + 4, 0:8]
        pack_dn[x, 0] = jnp.where(lower, ux, roll(uy, 4, 0))
        pack_dn[x, 1] = jnp.where(lower, uz, roll(sg, 4, 0))
        ux, uy, uz = (base[c, x + 3, 24:32] for c in range(3))
        sg = sig[x + 4, 24:32]
        pack_up[x, 0] = jnp.where(lower, roll(uy, 4, 0), ux)
        pack_up[x, 1] = jnp.where(lower, roll(sg, 4, 0), uz)
    for x in range(8):
        pack_up[8, 0, x:x + 1] = sig[x + 4, 27:28]
    pack_up[8, 1] = jnp.zeros((8, 128), jnp.float32)

    second = [
        remote(pack_dn.at[0:3], got_dn.at[12:15], x1, 2, (-1, -1)),
        remote(pack_up.at[0:3], got_up.at[13:16], x1, 3, (-1, 1)),
        remote(pack_dn.at[5:8], got_dn.at[9:12], x1, 4, (1, -1)),
        remote(pack_up.at[4:8], got_up.at[9:13], x1, 5, (1, 1)),
        remote(pack_dn, got_dn.at[0:8], x1, 6, (0, -1)),
        remote(pack_up, got_up.at[0:9], x1, 7, (0, 1)),
        remote(sig.at[10:12, 0:32], sig.at[2:4, 0:32], x1, 8, (1, 0)),
        remote(sig.at[4:6, 0:32], sig.at[12:14, 0:32], x1, 9, (-1, 0)),
    ]
    for copy in second:
        copy.start()
    far = (far_send, far_recv)
    later = [
        remote(sig.at[8:10, 0:32], sig.at[0:2, 0:32], far, 0, (1, 0)),
        remote(sig.at[6:7, 0:32], sig.at[14:15, 0:32], far, 1, (-1, 0)),
    ]
    for copy in later:
        copy.start()

    lane = lax.broadcasted_iota(jnp.int32, (ROWS, 128), 1)
    row = lax.broadcasted_iota(jnp.int32, (ROWS, 128), 0)
    lane_end, lane_start = lane == 127, lane == 0
    f32 = lambda flag: flag.astype(jnp.float32)
    keep_hi, keep_lo = 1.0 - f32(last_y), 1.0 - f32(first_y)
    row_mask = jnp.where(row < 32, 1.0, jnp.where(row < 40, keep_hi, keep_lo))
    row_zero = (row[0:8] == 0) & first_y

    def next_z(f):
        return jnp.where(lane_end, 0.0, roll(f, -1, 1))

    def prev_z(f):
        return jnp.where(lane_start, 0.0, roll(f, 1, 1))

    def next_y(f):
        return roll(f, -1, 0)

    def prev_y(f):
        return roll(f, 1, 0)

    def prev_y_inside(f):
        moved = roll(f, 1, 0)
        return jnp.concatenate([jnp.where(row_zero, 0.0, moved[0:8]), moved[8:]], axis=0)

    fine_z = lax.broadcasted_iota(jnp.int32, (256, 128), 0)
    packed_z = lax.broadcasted_iota(jnp.int32, (256, 128), 1)
    half = fine_z // 128 == packed_z // 64
    apart = (fine_z % 128) - 2 * (packed_z % 64)
    mean_z = jnp.where(half & ((apart == 0) | (apart == 1)), 0.125, 0.0)
    rest_z = jnp.where(half, jnp.where(apart == 0, 1.0, jnp.where(jnp.abs(apart) == 1, 0.5, 0.0)), 0.0)
    dot = functools.partial(jnp.dot, precision=lax.Precision.HIGHEST, preferred_element_type=jnp.float32)

    for x in range(4):
        red[x, 8:40] = sig[2 * x + 4, 0:32] + sig[2 * x + 5, 0:32]
    pairs = [red[x, pl.ds(8, 16, stride=2)] + red[x, pl.ds(9, 16, stride=2)] for x in range(4)]
    wide = jnp.concatenate(
        [jnp.concatenate([p[0:8] for p in pairs], axis=0), jnp.concatenate([p[8:16] for p in pairs], axis=0)], axis=1)
    coarse = 2.0 * dot(wide, mean_z)
    for x in range(4):
        cs_main[7 + x] = coarse[8 * x:8 * x + 8]

    plane_x = lax.broadcasted_iota(jnp.int32, (19, 8, 128), 0) - 7 + 4 * gx
    plane_ok = (plane_x >= 0) & (plane_x < 4 * nx)
    left3 = lax.broadcasted_iota(jnp.int32, (19, 8, 128), 2) < 64
    cm_one[0] = jnp.where(plane_ok, 1.0, 0.0)
    cm_one[1] = jnp.where(plane_ok, jnp.where(left3, keep_hi, keep_lo), 0.0)

    for copy in first + second:
        copy.wait()

    def spot_dn(x):
        return x if 0 <= x < 8 else (12 + x if x < 0 else 4 + x)

    def spot_up(x):
        return x if 0 <= x < 8 else (13 + x if x < 0 else 5 + x)

    zero_tile = jnp.zeros((8, 128), jnp.float32)
    for x in range(-4, 11):
        if x > -4:
            a, b = got_dn[spot_dn(x), 0], got_dn[spot_dn(x), 1]
            base[0, x + 3, 32:40] = a * keep_hi
            base[1, x + 3, 32:40] = roll(a, 4, 0) * keep_hi
            base[2, x + 3, 32:40] = b * keep_hi
            sig[x + 4, 32:40] = roll(b, 4, 0) * keep_hi
        else:
            sig[x + 4, 32:40] = zero_tile
        a, b = got_up[spot_up(x), 0], got_up[spot_up(x), 1]
        if x > -4:
            base[0, x + 3, 40:48] = a * keep_lo
            base[1, x + 3, 40:48] = roll(a, 4, 0) * keep_lo
            base[2, x + 3, 40:48] = b * keep_lo
        sg = roll(b, 4, 0)
        if 0 <= x < 8:
            sg = jnp.where(sub == 3, got_up[8, 0, x:x + 1], sg)
        sig[x + 4, 40:48] = sg * keep_lo

    @pl.when(first_x)
    def _():
        base[:, 0:3] = jnp.zeros((3, 3, ROWS, 128), jnp.float32)
        sig[2:4] = jnp.zeros((2, ROWS, 128), jnp.float32)

    @pl.when(last_x)
    def _():
        base[:, 11:14] = jnp.zeros((3, 3, ROWS, 128), jnp.float32)
        sig[12:14] = jnp.zeros((2, ROWS, 128), jnp.float32)

    keep_left, keep_right = 1.0 - f32(first_x), 1.0 - f32(last_x)

    def side(x):
        return keep_left if x < 0 else (keep_right if x > 7 else None)

    inv, steps = coefficients(20.0, 30.0, 4)
    nodal_prev = None
    for turn, (c_old, c_res) in enumerate(steps):
        lo, hi = -2 + turn, 9 - turn
        get = (lambda c, x: base[c, x + 3]) if turn == 0 else (lambda c, x: upd[c, x + 2])
        scaled = row_mask * c_res
        before = None
        here = [get(c, lo - 1) for c in range(3)]
        for x in range(lo - 1, hi + 1):
            after = [None if (c == 0 and x == hi) else get(c, x + 1) for c in range(3)]
            ux, uy, uz = here
            cy = (next_z(ux) - ux) - (after[2] - uz)
            cz = (after[1] - uy) - (next_y(ux) - ux)
            if x == -1:
                cy, cz = cy * keep_left, cz * keep_left
            if x >= lo:
                cx = (next_y(uz) - uz) - (next_z(uy) - uy)
                sg = sig[x + 4]
                applied = [
                    (prev_y_inside(cz) - cz) - (prev_z(cy) - cy) + sg * ux,
                    (prev_z(cx) - cx) - (before[1] - cz) + sg * uy,
                    (before[0] - cy) - (prev_y_inside(cx) - cx) + sg * uz,
                ]
                weight = scaled if side(x) is None else scaled * side(x)
                left = []
                for c in range(3):
                    if turn == 0:
                        u = here[c] * inv
                        r = here[c] - applied[c] * inv
                    else:
                        u = here[c]
                        r = res[c, x + 2] - applied[c]
                    new = c_old * u + weight * r
                    if turn < 2:
                        upd[c, x + 2] = new
                        res[c, x + 2] = r
                        if 0 <= x < 8:
                            acc[c, x] = u + new if turn == 0 else acc[c, x] + new
                    else:
                        answer = acc[c, x] + new
                        acc[c, x] = answer
                        left.append(base[c, x + 3] - sg * answer)
                if turn == 2:
                    rx, ry, rz = left
                    total = (ry - prev_y(ry)) + (rz - prev_z(rz)) + rx
                    nod[x + 5, 0:32] = (total if nodal_prev is None else total - nodal_prev)[0:32]
                    nodal_prev = rx
                    if x == 7:
                        nod[13, 0:32] = rx[0:32]
            before = (cy, cz)
            here = after

    x2 = (x2_send, x2_recv)
    swap = [
        remote(nod.at[9:14, 0:32], nod.at[0:5, 0:32], x2, 0, (1, 0)),
        remote(nod.at[5:9, 0:32], nod.at[14:18, 0:32], x2, 1, (-1, 0)),
        remote(nod.at[9:14, 24:32], nod.at[0:5, 40:48], x2, 2, (1, 1)),
        remote(nod.at[9:14, 0:8], nod.at[0:5, 32:40], x2, 3, (1, -1)),
        remote(nod.at[5:9, 24:32], nod.at[14:18, 40:48], x2, 4, (-1, 1)),
        remote(nod.at[5:9, 0:8], nod.at[14:18, 32:40], x2, 5, (-1, -1)),
        remote(nod.at[5:14, 24:32], nod.at[5:14, 40:48], x2, 6, (0, 1)),
        remote(nod.at[5:14, 0:8], nod.at[5:14, 32:40], x2, 7, (0, -1)),
    ]
    for copy in swap:
        copy.start()

    csem = (cs_send, cs_recv)

    def spread(main, dn, up, sems, own, count):
        block = main.at[own:own + count]
        span = {1: own - count, -1: own + count}
        copies = []
        for k, dx in enumerate((1, -1)):
            spot = span[dx]
            copies.append(remote(block, main.at[spot:spot + count], sems, 6 * k, (dx, 0)))
            copies.append(remote(block, dn.at[spot:spot + count], sems, 6 * k + 1, (dx, -1)))
            copies.append(remote(block, up.at[spot:spot + count], sems, 6 * k + 2, (dx, 1)))
        far_low, far_high = main.at[own + 1:own + count], main.at[own:own + 4]
        size = count - 1
        end = own + 2 * count
        copies.append(remote(far_low, main.at[0:size], sems, 3, (2, 0)))
        copies.append(remote(far_low, dn.at[0:size], sems, 4, (2, -1)))
        copies.append(remote(far_low, up.at[0:size], sems, 5, (2, 1)))
        copies.append(remote(far_high, main.at[end:end + 4], sems, 9, (-2, 0)))
        copies.append(remote(far_high, dn.at[end:end + 4], sems, 10, (-2, -1)))
        copies.append(remote(far_high, up.at[end:end + 4], sems, 11, (-2, 1)))
        copies.append(remote(block, dn.at[own:own + count], sems, 12, (0, -1)))
        copies.append(remote(block, up.at[own:own + count], sems, 13, (0, 1)))
        return copies

    cs_copies = spread(cs_main, cs_dn, cs_up, csem, 7, 4)
    for copy in cs_copies:
        copy.start()

    for copy in later + swap:
        copy.wait()

    @pl.when(first_x)
    def _():
        nod[0:5] = jnp.zeros((5, ROWS, 128), jnp.float32)
        sig[0:2] = jnp.zeros((2, ROWS, 128), jnp.float32)

    @pl.when(last_x)
    def _():
        sig[14:15] = jnp.zeros((1, ROWS, 128), jnp.float32)

    nod[5] = nod[5] - nod[4]
    nod[14] = nod[14] - nod[13]

    @pl.when(last_x)
    def _():
        nod[14:18] = jnp.zeros((4, ROWS, 128), jnp.float32)

    @pl.when(first_y)
    def _():
        nod[:, 40:48] = jnp.zeros((18, 8, 128), jnp.float32)

    @pl.when(last_y)
    def _():
        nod[:, 32:40] = jnp.zeros((18, 8, 128), jnp.float32)

    def place(x):
        return x + 4 if x < 0 else (x + 5 if x < 8 else x + 6)

    inv, steps = coefficients(48.0, 30.0, 4)
    steps = steps + [None]
    nupd, nres = upd.at[0], res.at[0]
    planes = []
    for turn, step in enumerate(steps):
        lo, hi = -3 + turn, 10 - turn
        get = (lambda x: nod[place(x)]) if turn == 0 else (lambda x: nupd[x + 3])
        here = get(lo - 1)
        before = None
        for x in range(lo - 1, hi + 1):
            after = get(x + 1)
            sg = sig[x + 4]
            flux_x = sg * (after - here)
            if x >= lo:
                flux_y = sg * (next_y(here) - here)
                flux_z = sg * (next_z(here) - here)
                applied = (flux_x - before) + (flux_y - prev_y(flux_y)) + (flux_z - prev_z(flux_z))
                if turn == 0:
                    u = here * inv
                    r = here - applied * inv
                else:
                    u = here
                    r = nres[x + 3] - applied
                if step is not None:
                    weight = row_mask * step[1]
                    weight = weight if side(x) is None else weight * side(x)
                    new = step[0] * u + weight * r
                    nupd[x + 3] = new
                    nres[x + 3] = r
                    if 0 <= x < 9:
                        node_sum[x] = u + new if turn == 0 else node_sum[x] + new
                else:
                    planes.append(r)
                    if x % 2 == 1:
                        total = planes[x - 1] + 0.5 * planes[x]
                        if x > 1:
                            total = total + 0.5 * planes[x - 2]
                        red[x // 2, 8:40] = total[0:32]
                        red[x // 2, 0:8] = total[40:48] * keep_lo
                    if x == 7:
                        red[4, 8:40] = 0.5 * r[0:32]
                        red[4, 0:8] = 0.5 * r[40:48] * keep_lo
            before = flux_x
            here = after

    thin = [red[x, pl.ds(8, 16, stride=2)] + 0.5 * (red[x, pl.ds(9, 16, stride=2)] + red[x, pl.ds(7, 16, stride=2)])
            for x in range(5)]
    wide = jnp.concatenate(
        [jnp.concatenate([p[0:8] for p in thin], axis=0), jnp.concatenate([p[8:16] for p in thin], axis=0)], axis=1)
    coarse = dot(wide, rest_z)
    for x in range(5):
        cf_main[9 + x] = coarse[8 * x:8 * x + 8]
    cf_copies = spread(cf_main, cf_dn, cf_up, (x3_send, x3_recv), 9, 5)
    for copy in cf_copies:
        copy.start()
    for copy in cs_copies:
        copy.wait()

    left = lax.broadcasted_iota(jnp.int32, (8, 128), 1) < 64
    for x in range(19):
        s_one[x] = cs_main[x] * cm_one[0, x]
        s_two[x] = jnp.where(left, cs_dn[x], cs_up[x]) * cm_one[1, x]

    for copy in cf_copies:
        copy.wait()

    def joined(i):
        return cf_main[i], jnp.where(left, cf_dn[i], cf_up[i])

    where_plane = [0, 1, 2, 4, 5, 6, 7, 9, 10, 11, 12, 14, 15, 16, 17, 19, 20, 21, 22]
    extra = {-4: (3, gx > 1), 0: (8, gx > 0), 4: (13, None), 8: (18, None)}
    for x in range(-7, 12):
        one, two = joined(where_plane[x + 7])
        if x in extra:
            spot, valid = extra[x]
            add_one, add_two = joined(spot)
            scale = 1.0 if valid is None else f32(valid)
            one, two = one + scale * add_one, two + scale * add_two
        g_one[x + 7] = one * cm_one[0, x + 7]
        g_two[x + 7] = two * cm_one[1, x + 7]

    inv, steps = coefficients(96.0, 100.0, 8)

    def lanes3(n):
        return lax.broadcasted_iota(jnp.int32, (n, 8, 128), 2)

    def swapped(one, two, first_side):
        turn_one, turn_two = roll(one, 64, 2), roll(two, 64, 2)
        pick = lanes3(one.shape[0]) < 64
        if first_side:
            return jnp.where(pick, turn_one, turn_two), jnp.where(pick, turn_two, turn_one)
        return jnp.where(pick, turn_two, turn_one), jnp.where(pick, turn_one, turn_two)

    def coarse_next_y(one, two):
        seam_one, seam_two = swapped(one, two, True)
        top = lax.broadcasted_iota(jnp.int32, one.shape, 1) == 0
        return roll(jnp.where(top, seam_one, one), -1, 1), roll(jnp.where(top, seam_two, two), -1, 1)

    def coarse_prev_y(one, two):
        seam_one, seam_two = swapped(one, two, False)
        bottom = lax.broadcasted_iota(jnp.int32, one.shape, 1) == 7
        return roll(jnp.where(bottom, seam_one, one), 1, 1), roll(jnp.where(bottom, seam_two, two), 1, 1)

    def coarse_next_z(f):
        return jnp.where(lanes3(f.shape[0]) % 64 == 63, 0.0, roll(f, -1, 2))

    def coarse_prev_z(f):
        return jnp.where(lanes3(f.shape[0]) % 64 == 0, 0.0, roll(f, 1, 2))

    f_one, f_two = g_one[...], g_two[...]
    r_one = r_two = None
    answer = None
    low = -7
    for turn, (c_old, c_res) in enumerate(steps):
        n = f_one.shape[0]
        sg_one, sg_two = s_one[low + 7:low + 7 + n], s_two[low + 7:low + 7 + n]
        x_one = sg_one[:-1] * (f_one[1:] - f_one[:-1])
        x_two = sg_two[:-1] * (f_two[1:] - f_two[:-1])
        mid_one, mid_two = f_one[1:-1], f_two[1:-1]
        in_one, in_two = sg_one[1:-1], sg_two[1:-1]
        up_one, up_two = coarse_next_y(mid_one, mid_two)
        y_one, y_two = in_one * (up_one - mid_one), in_two * (up_two - mid_two)
        back_one, back_two = coarse_prev_y(y_one, y_two)
        results = []
        for f, x_flux, y_flux, y_back, s in (
            (mid_one, x_one, y_one, back_one, in_one), (mid_two, x_two, y_two, back_two, in_two)):
            z_flux = s * (coarse_next_z(f) - f)
            results.append((x_flux[1:] - x_flux[:-1]) + (y_flux - y_back) + (z_flux - coarse_prev_z(z_flux)))
        low += 1
        if turn == 0:
            r_one, r_two = mid_one - results[0] * inv, mid_two - results[1] * inv
            mid_one, mid_two = mid_one * inv, mid_two * inv
            answer = [mid_one[6:11], mid_two[6:11]]
        else:
            r_one, r_two = r_one[1:-1] - results[0], r_two[1:-1] - results[1]
        n -= 2
        f_one = c_old * mid_one + c_res * (cm_one[0, low + 7:low + 7 + n] * r_one)
        f_two = c_old * mid_two + c_res * (cm_one[1, low + 7:low + 7 + n] * r_two)
        answer = [answer[0] + f_one[-low:5 - low], answer[1] + f_two[-low:5 - low]]

    coarse_k = lax.broadcasted_iota(jnp.int32, (128, 256), 0)
    fine_k = lax.broadcasted_iota(jnp.int32, (128, 256), 1)
    same = coarse_k // 64 == fine_k // 128
    apart = (fine_k % 128) - 2 * (coarse_k % 64)
    grow = jnp.where(same, jnp.where(apart == 0, 1.0, jnp.where(jnp.abs(apart) == 1, 0.5, 0.0)), 0.0)
    body = dot(answer[0].reshape(40, 128), grow)
    edge = dot(answer[1].reshape(40, 128), grow[:, 0:128])
    for x in range(5):
        fine[x, 0:8] = body[8 * x:8 * x + 8, 0:128]
        fine[x, 8:16] = body[8 * x:8 * x + 8, 128:256]
        fine[x, 16:24] = edge[8 * x:8 * x + 8]

    own, nxt = None, None
    half_rows = []
    for x in range(5):
        a, b = fine[x, 0:16], fine[x, 1:17]
        red[x, pl.ds(0, 16, stride=2)] = a
        red[x, pl.ds(1, 16, stride=2)] = 0.5 * (a + b)
        red[x, 32:40] = fine[x, 16:24]
    for x in range(9):
        value = red[x // 2] if x % 2 == 0 else 0.5 * (red[x // 2] + red[x // 2 + 1])
        node_sum[x, 0:40] = node_sum[x, 0:40] + value
    keep_next = [keep_hi, keep_right]
    for x in range(8):
        here = node_sum[x, 0:32]
        after = node_sum[x + 1, 0:32]
        if x == 7:
            after = after * keep_right
        shifted = roll(node_sum[x], -1, 0)[0:32]
        last = (row[0:32] == 31) & last_y
        shifted = jnp.where(last, 0.0, shifted)
        out[0, x] = acc[0, x, 0:32] + (after - here)
        out[1, x] = acc[1, x, 0:32] + (shifted - here)
        out[2, x] = acc[2, x, 0:32] + (jnp.where(lane_end[0:32], 0.0, roll(here, -1, 1)) - here)


def solution(mesh):
    nx, ny = mesh.shape["gx"], mesh.shape["gy"]
    f32 = jnp.float32
    dma = pltpu.SemaphoreType.DMA

    def shards(right_side, classes, table):
        return pl.pallas_call(
            functools.partial(kernel, nx, ny),
            out_shape=jax.ShapeDtypeStruct(right_side.shape, f32),
            in_specs=[pl.BlockSpec(memory_space=pl.ANY), pl.BlockSpec(memory_space=pl.ANY),
                      pl.BlockSpec(memory_space=pltpu.SMEM)],
            out_specs=pl.BlockSpec(memory_space=pltpu.VMEM),
            scratch_shapes=[
                pltpu.VMEM((3, 14, ROWS, 128), f32),
                pltpu.VMEM((8, 32, 128), jnp.int32),
                pltpu.VMEM((16, ROWS, 128), f32),
                pltpu.VMEM((3, 14, ROWS, 128), f32),
                pltpu.VMEM((3, 14, ROWS, 128), f32),
                pltpu.VMEM((3, 8, ROWS, 128), f32),
                pltpu.VMEM((8, 2, 8, 128), f32),
                pltpu.VMEM((9, 2, 8, 128), f32),
                pltpu.VMEM((15, 2, 8, 128), f32),
                pltpu.VMEM((16, 2, 8, 128), f32),
                pltpu.VMEM((18, ROWS, 128), f32),
                pltpu.VMEM((9, ROWS, 128), f32),
                pltpu.VMEM((5, 40, 128), f32),
                pltpu.VMEM((19, 8, 128), f32),
                pltpu.VMEM((19, 8, 128), f32),
                pltpu.VMEM((19, 8, 128), f32),
                pltpu.VMEM((23, 8, 128), f32),
                pltpu.VMEM((23, 8, 128), f32),
                pltpu.VMEM((23, 8, 128), f32),
                pltpu.VMEM((2, 19, 8, 128), f32),
                pltpu.VMEM((19, 8, 128), f32),
                pltpu.VMEM((19, 8, 128), f32),
                pltpu.VMEM((19, 8, 128), f32),
                pltpu.VMEM((19, 8, 128), f32),
                pltpu.VMEM((5, 24, 128), f32),
                dma((2,)), dma((10,)), dma((10,)), dma((2,)), dma((2,)), dma((8,)), dma((8,)),
                dma((14,)), dma((14,)), dma((14,)), dma((14,)),
            ],
            compiler_params=pltpu.CompilerParams(
                collective_id=0, has_side_effects=True, vmem_limit_bytes=40 * 2**20),
            name="cycle",
        )(right_side, classes, table)

    return jax.shard_map(
        shards,
        mesh=mesh,
        in_specs=(P(None, "gx", "gy", None), P("gx", "gy", None), P()),
        out_specs=P(None, "gx", "gy", None),
        check_vma=False,
    )
```

```python
import functools

import jax
import jax.numpy as jnp
from jax import lax
from jax.experimental import pallas as pl
from jax.experimental.pallas import tpu as pltpu
from jax.sharding import PartitionSpec as P

MESH = pl.DeviceIdType.MESH
ROWS = 48


def coefficients(top, ratio, count):
    low = top / ratio
    center = 0.5 * (top + low)
    radius = 0.5 * (top - low)
    sharp = center / radius
    rho = 1.0 / sharp
    steps = []
    for _ in range(1, count):
        rho_next = 1.0 / (2.0 * sharp - rho)
        steps.append((rho_next * rho, 2.0 * rho_next / radius))
        rho = rho_next
    return 1.0 / center, steps


def roll(value, shift, axis):
    return pltpu.roll(value, shift % value.shape[axis], axis)


def kernel(nx, ny, rhs, classes, table, out, base, kinds, sig, upd, res, acc,
           pack_dn, pack_up, got_dn, got_up, nod, node_sum, red, cs_main, cs_pack, cs_got, cs_far,
           cf_main, cf_pack, cf_got, cf_far, values_in, cm_one, g_one, g_two, s_one, s_two, fine,
           sem_in, send, recv, far_send, far_recv, x2_send, x2_recv, cs_send, cs_recv, x3_send, x3_recv):
    gx, gy = lax.axis_index("gx"), lax.axis_index("gy")
    first_x, last_x, first_y, last_y = gx == 0, gx == nx - 1, gy == 0, gy == ny - 1

    def at(dx, dy):
        return (lax.rem(gx + dx + nx, nx), lax.rem(gy + dy + ny, ny))

    near = [(1, 0), (-1, 0), (0, 1), (0, -1), (1, 1), (1, -1), (-1, 1), (-1, -1)]
    distant = [(2, 0), (-2, 0), (2, 1), (2, -1), (-2, 1), (-2, -1)]

    def remote(source, target, sems, index, where):
        return pltpu.make_async_remote_copy(
            src_ref=source, dst_ref=target, send_sem=sems[0].at[index], recv_sem=sems[1].at[index],
            device_id=at(*where), device_id_type=MESH)

    barrier = pltpu.get_barrier_semaphore()
    for where in near + distant:
        pl.semaphore_signal(barrier, inc=1, device_id=at(*where), device_id_type=MESH)
    loads = [
        pltpu.make_async_copy(table, values_in, sem_in.at[2]),
        pltpu.make_async_copy(classes, kinds, sem_in.at[1]),
        pltpu.make_async_copy(rhs, base.at[:, 3:11, 0:32], sem_in.at[0]),
    ]
    for copy in loads:
        copy.start()

    pl.semaphore_wait(barrier, len(near + distant))
    x1 = (send, recv)
    first = [
        remote(rhs.at[:, 5:8], base.at[:, 0:3, 0:32], x1, 0, (1, 0)),
        remote(rhs.at[1:3, 0:3], base.at[1:3, 11:14, 0:32], x1, 1, (-1, 0)),
        remote(rhs.at[0:1, 0:2], base.at[0:1, 11:13, 0:32], x1, 10, (-1, 0)),
    ]
    for copy in first:
        copy.start()
    for copy in loads:
        copy.wait()

    values = [values_in[k] for k in range(16)]
    for x in range(8):
        code = kinds[x]
        level = values
        for bit in range(4):
            flag = (code & (1 << bit)) != 0
            level = [jnp.where(flag, level[2 * i + 1], level[2 * i]) for i in range(len(level) // 2)]
        sig[x + 4, 0:32] = level[0]

    sub = lax.broadcasted_iota(jnp.int32, (8, 128), 0)
    lower = sub < 4
    for x in range(8):
        ux, uy, uz = (base[c, x + 3, 0:8] for c in range(3))
        sg = sig[x + 4, 0:8]
        pack_dn[x, 0] = jnp.where(lower, ux, roll(uy, 4, 0))
        pack_dn[x, 1] = jnp.where(lower, uz, roll(sg, 4, 0))
        ux, uy, uz = (base[c, x + 3, 24:32] for c in range(3))
        sg = sig[x + 4, 24:32]
        pack_up[x, 0] = jnp.where(lower, roll(uy, 4, 0), ux)
        pack_up[x, 1] = jnp.where(lower, roll(sg, 4, 0), uz)
    for x in range(8):
        pack_up[8, 0, x:x + 1] = sig[x + 4, 27:28]
    pack_up[8, 1] = jnp.zeros((8, 128), jnp.float32)

    second = [
        remote(pack_dn.at[0:3], got_dn.at[12:15], x1, 2, (-1, -1)),
        remote(pack_up.at[0:3], got_up.at[13:16], x1, 3, (-1, 1)),
        remote(pack_dn.at[5:8], got_dn.at[9:12], x1, 4, (1, -1)),
        remote(pack_up.at[4:8], got_up.at[9:13], x1, 5, (1, 1)),
        remote(pack_dn, got_dn.at[0:8], x1, 6, (0, -1)),
        remote(pack_up, got_up.at[0:9], x1, 7, (0, 1)),
        remote(sig.at[10:12, 0:32], sig.at[2:4, 0:32], x1, 8, (1, 0)),
        remote(sig.at[4:6, 0:32], sig.at[12:14, 0:32], x1, 9, (-1, 0)),
    ]
    for copy in second:
        copy.start()
    far = (far_send, far_recv)
    later = [
        remote(sig.at[8:10, 0:32], sig.at[0:2, 0:32], far, 0, (1, 0)),
        remote(sig.at[6:7, 0:32], sig.at[14:15, 0:32], far, 1, (-1, 0)),
    ]
    for copy in later:
        copy.start()

    lane = lax.broadcasted_iota(jnp.int32, (ROWS, 128), 1)
    row = lax.broadcasted_iota(jnp.int32, (ROWS, 128), 0)
    lane_end, lane_start = lane == 127, lane == 0
    f32 = lambda flag: flag.astype(jnp.float32)
    keep_hi, keep_lo = 1.0 - f32(last_y), 1.0 - f32(first_y)
    row_mask = jnp.where(row < 32, 1.0, jnp.where(row < 40, keep_hi, keep_lo))
    row_zero = (row[0:8] == 0) & first_y

    def next_z(f):
        return jnp.where(lane_end, 0.0, roll(f, -1, 1))

    def prev_z(f):
        return jnp.where(lane_start, 0.0, roll(f, 1, 1))

    def next_y(f):
        return roll(f, -1, 0)

    def prev_y(f):
        return roll(f, 1, 0)

    def prev_y_inside(f):
        moved = roll(f, 1, 0)
        return jnp.concatenate([jnp.where(row_zero, 0.0, moved[0:8]), moved[8:]], axis=0)

    fine_z = lax.broadcasted_iota(jnp.int32, (256, 128), 0)
    packed_z = lax.broadcasted_iota(jnp.int32, (256, 128), 1)
    half = fine_z // 128 == packed_z // 64
    apart = (fine_z % 128) - 2 * (packed_z % 64)
    mean_z = jnp.where(half & ((apart == 0) | (apart == 1)), 0.125, 0.0)
    rest_z = jnp.where(half, jnp.where(apart == 0, 1.0, jnp.where(jnp.abs(apart) == 1, 0.5, 0.0)), 0.0)
    dot = functools.partial(jnp.dot, precision=lax.Precision.HIGHEST, preferred_element_type=jnp.float32)

    for x in range(4):
        red[x, 8:40] = sig[2 * x + 4, 0:32] + sig[2 * x + 5, 0:32]
    pairs = [red[x, pl.ds(8, 16, stride=2)] + red[x, pl.ds(9, 16, stride=2)] for x in range(4)]
    wide = jnp.concatenate(
        [jnp.concatenate([p[0:8] for p in pairs], axis=0), jnp.concatenate([p[8:16] for p in pairs], axis=0)], axis=1)
    coarse = 2.0 * dot(wide, mean_z)
    for x in range(4):
        cs_main[7 + x] = coarse[8 * x:8 * x + 8]

    plane_x = lax.broadcasted_iota(jnp.int32, (19, 8, 128), 0) - 7 + 4 * gx
    plane_ok = (plane_x >= 0) & (plane_x < 4 * nx)
    left3 = lax.broadcasted_iota(jnp.int32, (19, 8, 128), 2) < 64
    cm_one[0] = jnp.where(plane_ok, 1.0, 0.0)
    cm_one[1] = jnp.where(plane_ok, jnp.where(left3, keep_hi, keep_lo), 0.0)

    left = lax.broadcasted_iota(jnp.int32, (8, 128), 1) < 64

    def flip(tile):
        return roll(tile, 64, 1)

    def halves(a, b):
        if b is None:
            return a, flip(a)
        return jnp.where(left, a, flip(b)), jnp.where(left, flip(a), b)

    def unhalve(dn, up):
        return jnp.where(left, dn, flip(up)), jnp.where(left, flip(dn), up)

    def spread(main, pack, got, far_got, sems, own, count):
        tiles = [main[own + i] for i in range(count)] + [None]
        pairs = [halves(tiles[0], tiles[1]), halves(tiles[2], tiles[3])]
        odd = [halves(tiles[1], tiles[2]), halves(tiles[3], tiles[4])]
        if count == 5:
            pairs.append(halves(tiles[4], None))
        number = len(pairs)
        for i, (dn, up) in enumerate(pairs):
            pack[0, i] = dn
            pack[1, i] = up
        for i, (one, two) in enumerate((odd, pairs[:2])):
            pack[0, 3 + i] = jnp.where(lower, one[0], roll(two[0], 4, 0))
            pack[1, 3 + i] = jnp.where(lower, roll(one[1], 4, 0), two[1])
        block = main.at[own:own + count]
        size, end = count - 1, own + 2 * count
        copies = [
            remote(main.at[own + 1:own + count], main.at[0:size], sems, 0, (2, 0)),
            remote(main.at[own:own + 4], main.at[end:end + 4], sems, 1, (-2, 0)),
        ]
        for i, dx in enumerate((2, -2)):
            for j, dy in enumerate((-1, 1)):
                copies.append(remote(pack.at[j, 3 + i], far_got.at[i, j], sems, 2 + 2 * i + j, (dx, dy)))
        for i, dx in enumerate((1, -1, 0)):
            for j, dy in enumerate((-1, 1)):
                copies.append(remote(pack.at[j, 0:number], got.at[i, j, 0:number], sems, 6 + 2 * i + j, (dx, dy)))
        copies.append(remote(block, main.at[own - count:own], sems, 12, (1, 0)))
        copies.append(remote(block, main.at[own + count:own + 2 * count], sems, 13, (-1, 0)))
        for copy in copies:
            copy.start()
        return copies

    def received(got, far_got, number):
        planes = []
        for spot in (0, 2, 1):
            block = []
            for i in range(number):
                block += list(unhalve(got[spot, 0, i], got[spot, 1, i]))
            planes.append(block[:5] if number == 3 else block)
        sides = []
        for i in range(2):
            dn, up = far_got[i, 0], far_got[i, 1]
            sides.append(list(unhalve(dn, roll(up, 4, 0))) + list(unhalve(roll(dn, 4, 0), up)))
        return sides[0], planes[0], planes[1], planes[2], sides[1]

    for copy in first + second:
        copy.wait()
    cs_copies = spread(cs_main, cs_pack, cs_got, cs_far, (cs_send, cs_recv), 7, 4)

    def spot_dn(x):
        return x if 0 <= x < 8 else (12 + x if x < 0 else 4 + x)

    def spot_up(x):
        return x if 0 <= x < 8 else (13 + x if x < 0 else 5 + x)

    zero_tile = jnp.zeros((8, 128), jnp.float32)
    for x in range(-4, 11):
        if x > -4:
            a, b = got_dn[spot_dn(x), 0], got_dn[spot_dn(x), 1]
            base[0, x + 3, 32:40] = a * keep_hi
            base[1, x + 3, 32:40] = roll(a, 4, 0) * keep_hi
            base[2, x + 3, 32:40] = b * keep_hi
            sig[x + 4, 32:40] = roll(b, 4, 0) * keep_hi
        else:
            sig[x + 4, 32:40] = zero_tile
        a, b = got_up[spot_up(x), 0], got_up[spot_up(x), 1]
        if x > -4:
            base[0, x + 3, 40:48] = a * keep_lo
            base[1, x + 3, 40:48] = roll(a, 4, 0) * keep_lo
            base[2, x + 3, 40:48] = b * keep_lo
        sg = roll(b, 4, 0)
        if 0 <= x < 8:
            sg = jnp.where(sub == 3, got_up[8, 0, x:x + 1], sg)
        sig[x + 4, 40:48] = sg * keep_lo

    @pl.when(first_x)
    def _():
        base[:, 0:3] = jnp.zeros((3, 3, ROWS, 128), jnp.float32)
        sig[2:4] = jnp.zeros((2, ROWS, 128), jnp.float32)

    @pl.when(last_x)
    def _():
        base[:, 11:14] = jnp.zeros((3, 3, ROWS, 128), jnp.float32)
        sig[12:14] = jnp.zeros((2, ROWS, 128), jnp.float32)

    keep_left, keep_right = 1.0 - f32(first_x), 1.0 - f32(last_x)

    def side(x):
        return keep_left if x < 0 else (keep_right if x > 7 else None)

    inv, steps = coefficients(20.0, 30.0, 4)
    nodal_prev = None
    for turn, (c_old, c_res) in enumerate(steps):
        lo, hi = -2 + turn, 9 - turn
        get = (lambda c, x: base[c, x + 3]) if turn == 0 else (lambda c, x: upd[c, x + 2])
        scaled = row_mask * c_res
        before = None
        here = [get(c, lo - 1) for c in range(3)]
        for x in range(lo - 1, hi + 1):
            after = [None if (c == 0 and x == hi) else get(c, x + 1) for c in range(3)]
            ux, uy, uz = here
            cy = (next_z(ux) - ux) - (after[2] - uz)
            cz = (after[1] - uy) - (next_y(ux) - ux)
            if x == -1:
                cy, cz = cy * keep_left, cz * keep_left
            if x >= lo:
                cx = (next_y(uz) - uz) - (next_z(uy) - uy)
                sg = sig[x + 4]
                applied = [
                    (prev_y_inside(cz) - cz) - (prev_z(cy) - cy) + sg * ux,
                    (prev_z(cx) - cx) - (before[1] - cz) + sg * uy,
                    (before[0] - cy) - (prev_y_inside(cx) - cx) + sg * uz,
                ]
                weight = scaled if side(x) is None else scaled * side(x)
                rest = []
                for c in range(3):
                    if turn == 0:
                        u = here[c] * inv
                        r = here[c] - applied[c] * inv
                    else:
                        u = here[c]
                        r = res[c, x + 2] - applied[c]
                    new = c_old * u + weight * r
                    if turn < 2:
                        upd[c, x + 2] = new
                        res[c, x + 2] = r
                        if 0 <= x < 8:
                            acc[c, x] = u + new if turn == 0 else acc[c, x] + new
                    else:
                        answer = acc[c, x] + new
                        acc[c, x] = answer
                        rest.append(base[c, x + 3] - sg * answer)
                if turn == 2:
                    rx, ry, rz = rest
                    total = (ry - prev_y(ry)) + (rz - prev_z(rz)) + rx
                    nod[x + 5, 0:32] = (total if nodal_prev is None else total - nodal_prev)[0:32]
                    nodal_prev = rx
                    if x == 7:
                        nod[13, 0:32] = rx[0:32]
            before = (cy, cz)
            here = after

    x2 = (x2_send, x2_recv)
    swap = [
        remote(nod.at[9:14, 0:32], nod.at[0:5, 0:32], x2, 0, (1, 0)),
        remote(nod.at[5:9, 0:32], nod.at[14:18, 0:32], x2, 1, (-1, 0)),
        remote(nod.at[9:14, 24:32], nod.at[0:5, 40:48], x2, 2, (1, 1)),
        remote(nod.at[9:14, 0:8], nod.at[0:5, 32:40], x2, 3, (1, -1)),
        remote(nod.at[5:9, 24:32], nod.at[14:18, 40:48], x2, 4, (-1, 1)),
        remote(nod.at[5:9, 0:8], nod.at[14:18, 32:40], x2, 5, (-1, -1)),
        remote(nod.at[5:14, 24:32], nod.at[5:14, 40:48], x2, 6, (0, 1)),
        remote(nod.at[5:14, 0:8], nod.at[5:14, 32:40], x2, 7, (0, -1)),
    ]
    for copy in swap:
        copy.start()

    for copy in later + swap:
        copy.wait()

    @pl.when(first_x)
    def _():
        nod[0:5] = jnp.zeros((5, ROWS, 128), jnp.float32)
        sig[0:2] = jnp.zeros((2, ROWS, 128), jnp.float32)

    @pl.when(last_x)
    def _():
        sig[14:15] = jnp.zeros((1, ROWS, 128), jnp.float32)

    nod[5] = nod[5] - nod[4]
    nod[14] = nod[14] - nod[13]

    @pl.when(last_x)
    def _():
        nod[14:18] = jnp.zeros((4, ROWS, 128), jnp.float32)

    @pl.when(first_y)
    def _():
        nod[:, 40:48] = jnp.zeros((18, 8, 128), jnp.float32)

    @pl.when(last_y)
    def _():
        nod[:, 32:40] = jnp.zeros((18, 8, 128), jnp.float32)

    def place(x):
        return x + 4 if x < 0 else (x + 5 if x < 8 else x + 6)

    inv, steps = coefficients(48.0, 30.0, 4)
    steps = steps + [None]
    nupd, nres = upd.at[0], res.at[0]
    planes = []
    for turn, step in enumerate(steps):
        lo, hi = -3 + turn, 10 - turn
        get = (lambda x: nod[place(x)]) if turn == 0 else (lambda x: nupd[x + 3])
        here = get(lo - 1)
        before = None
        for x in range(lo - 1, hi + 1):
            after = get(x + 1)
            sg = sig[x + 4]
            flux_x = sg * (after - here)
            if x >= lo:
                flux_y = sg * (next_y(here) - here)
                flux_z = sg * (next_z(here) - here)
                applied = (flux_x - before) + (flux_y - prev_y(flux_y)) + (flux_z - prev_z(flux_z))
                if turn == 0:
                    u = here * inv
                    r = here - applied * inv
                else:
                    u = here
                    r = nres[x + 3] - applied
                if step is not None:
                    weight = row_mask * step[1]
                    weight = weight if side(x) is None else weight * side(x)
                    new = step[0] * u + weight * r
                    nupd[x + 3] = new
                    nres[x + 3] = r
                    if 0 <= x < 9:
                        node_sum[x] = u + new if turn == 0 else node_sum[x] + new
                else:
                    planes.append(r)
                    if x % 2 == 1:
                        total = planes[x - 1] + 0.5 * planes[x]
                        if x > 1:
                            total = total + 0.5 * planes[x - 2]
                        red[x // 2, 8:40] = total[0:32]
                        red[x // 2, 0:8] = total[40:48] * keep_lo
                    if x == 7:
                        red[4, 8:40] = 0.5 * r[0:32]
                        red[4, 0:8] = 0.5 * r[40:48] * keep_lo
            before = flux_x
            here = after

    thin = [red[x, pl.ds(8, 16, stride=2)] + 0.5 * (red[x, pl.ds(9, 16, stride=2)] + red[x, pl.ds(7, 16, stride=2)])
            for x in range(5)]
    wide = jnp.concatenate(
        [jnp.concatenate([p[0:8] for p in thin], axis=0), jnp.concatenate([p[8:16] for p in thin], axis=0)], axis=1)
    coarse = dot(wide, rest_z)
    for x in range(5):
        cf_main[9 + x] = coarse[8 * x:8 * x + 8]
    cf_copies = spread(cf_main, cf_pack, cf_got, cf_far, (x3_send, x3_recv), 9, 5)
    for copy in cs_copies:
        copy.wait()

    far_low, low_block, own_block, high_block, far_high = received(cs_got, cs_far, 2)
    halo = far_low[:3] + low_block + own_block + high_block + far_high
    for x in range(19):
        s_one[x] = cs_main[x] * cm_one[0, x]
        s_two[x] = halo[x] * cm_one[1, x]

    for copy in cf_copies:
        copy.wait()

    far_low, low_block, own_block, high_block, far_high = received(cf_got, cf_far, 3)
    halo = far_low + low_block + own_block + high_block + far_high
    where_plane = [0, 1, 2, 4, 5, 6, 7, 9, 10, 11, 12, 14, 15, 16, 17, 19, 20, 21, 22]
    extra = {-4: (3, gx > 1), 0: (8, gx > 0), 4: (13, None), 8: (18, None)}
    for x in range(-7, 12):
        one, two = cf_main[where_plane[x + 7]], halo[where_plane[x + 7]]
        if x in extra:
            spot, valid = extra[x]
            add_one, add_two = cf_main[spot], halo[spot]
            if valid is not None:
                add_one, add_two = add_one * f32(valid), add_two * f32(valid)
            one, two = one + add_one, two + add_two
        g_one[x + 7] = one * cm_one[0, x + 7]
        g_two[x + 7] = two * cm_one[1, x + 7]

    inv, steps = coefficients(96.0, 100.0, 8)

    def lanes3(n):
        return lax.broadcasted_iota(jnp.int32, (n, 8, 128), 2)

    def swapped(one, two, first_side):
        turn_one, turn_two = roll(one, 64, 2), roll(two, 64, 2)
        pick = lanes3(one.shape[0]) < 64
        if first_side:
            return jnp.where(pick, turn_one, turn_two), jnp.where(pick, turn_two, turn_one)
        return jnp.where(pick, turn_two, turn_one), jnp.where(pick, turn_one, turn_two)

    def coarse_next_y(one, two):
        seam_one, seam_two = swapped(one, two, True)
        top = lax.broadcasted_iota(jnp.int32, one.shape, 1) == 0
        return roll(jnp.where(top, seam_one, one), -1, 1), roll(jnp.where(top, seam_two, two), -1, 1)

    def coarse_prev_y(one, two):
        seam_one, seam_two = swapped(one, two, False)
        bottom = lax.broadcasted_iota(jnp.int32, one.shape, 1) == 7
        return roll(jnp.where(bottom, seam_one, one), 1, 1), roll(jnp.where(bottom, seam_two, two), 1, 1)

    def coarse_next_z(f):
        return jnp.where(lanes3(f.shape[0]) % 64 == 63, 0.0, roll(f, -1, 2))

    def coarse_prev_z(f):
        return jnp.where(lanes3(f.shape[0]) % 64 == 0, 0.0, roll(f, 1, 2))

    f_one, f_two = g_one[...], g_two[...]
    r_one = r_two = None
    answer = None
    low = -7
    for turn, (c_old, c_res) in enumerate(steps):
        n = f_one.shape[0]
        sg_one, sg_two = s_one[low + 7:low + 7 + n], s_two[low + 7:low + 7 + n]
        x_one = sg_one[:-1] * (f_one[1:] - f_one[:-1])
        x_two = sg_two[:-1] * (f_two[1:] - f_two[:-1])
        mid_one, mid_two = f_one[1:-1], f_two[1:-1]
        in_one, in_two = sg_one[1:-1], sg_two[1:-1]
        up_one, up_two = coarse_next_y(mid_one, mid_two)
        y_one, y_two = in_one * (up_one - mid_one), in_two * (up_two - mid_two)
        back_one, back_two = coarse_prev_y(y_one, y_two)
        results = []
        for f, x_flux, y_flux, y_back, s in (
            (mid_one, x_one, y_one, back_one, in_one), (mid_two, x_two, y_two, back_two, in_two)):
            z_flux = s * (coarse_next_z(f) - f)
            results.append((x_flux[1:] - x_flux[:-1]) + (y_flux - y_back) + (z_flux - coarse_prev_z(z_flux)))
        low += 1
        if turn == 0:
            r_one, r_two = mid_one - results[0] * inv, mid_two - results[1] * inv
            mid_one, mid_two = mid_one * inv, mid_two * inv
            answer = [mid_one[6:11], mid_two[6:11]]
        else:
            r_one, r_two = r_one[1:-1] - results[0], r_two[1:-1] - results[1]
        n -= 2
        f_one = c_old * mid_one + c_res * (cm_one[0, low + 7:low + 7 + n] * r_one)
        f_two = c_old * mid_two + c_res * (cm_one[1, low + 7:low + 7 + n] * r_two)
        answer = [answer[0] + f_one[-low:5 - low], answer[1] + f_two[-low:5 - low]]

    coarse_k = lax.broadcasted_iota(jnp.int32, (128, 256), 0)
    fine_k = lax.broadcasted_iota(jnp.int32, (128, 256), 1)
    same = coarse_k // 64 == fine_k // 128
    apart = (fine_k % 128) - 2 * (coarse_k % 64)
    grow = jnp.where(same, jnp.where(apart == 0, 1.0, jnp.where(jnp.abs(apart) == 1, 0.5, 0.0)), 0.0)
    body = dot(answer[0].reshape(40, 128), grow)
    edge = dot(answer[1].reshape(40, 128), grow[:, 0:128])
    for x in range(5):
        fine[x, 0:8] = body[8 * x:8 * x + 8, 0:128]
        fine[x, 8:16] = body[8 * x:8 * x + 8, 128:256]
        fine[x, 16:24] = edge[8 * x:8 * x + 8]

    own, nxt = None, None
    half_rows = []
    for x in range(5):
        a, b = fine[x, 0:16], fine[x, 1:17]
        red[x, pl.ds(0, 16, stride=2)] = a
        red[x, pl.ds(1, 16, stride=2)] = 0.5 * (a + b)
        red[x, 32:40] = fine[x, 16:24]
    for x in range(9):
        value = red[x // 2] if x % 2 == 0 else 0.5 * (red[x // 2] + red[x // 2 + 1])
        node_sum[x, 0:40] = node_sum[x, 0:40] + value
    keep_next = [keep_hi, keep_right]
    for x in range(8):
        here = node_sum[x, 0:32]
        after = node_sum[x + 1, 0:32]
        if x == 7:
            after = after * keep_right
        shifted = roll(node_sum[x], -1, 0)[0:32]
        last = (row[0:32] == 31) & last_y
        shifted = jnp.where(last, 0.0, shifted)
        out[0, x] = acc[0, x, 0:32] + (after - here)
        out[1, x] = acc[1, x, 0:32] + (shifted - here)
        out[2, x] = acc[2, x, 0:32] + (jnp.where(lane_end[0:32], 0.0, roll(here, -1, 1)) - here)


def solution(mesh):
    nx, ny = mesh.shape["gx"], mesh.shape["gy"]
    f32 = jnp.float32
    dma = pltpu.SemaphoreType.DMA

    def shards(right_side, classes, table):
        return pl.pallas_call(
            functools.partial(kernel, nx, ny),
            out_shape=jax.ShapeDtypeStruct(right_side.shape, f32),
            in_specs=[pl.BlockSpec(memory_space=pltpu.HBM)] * 3,
            out_specs=pl.BlockSpec(memory_space=pltpu.VMEM),
            scratch_shapes=[
                pltpu.VMEM((3, 14, ROWS, 128), f32),
                pltpu.VMEM((8, 32, 128), jnp.int32),
                pltpu.VMEM((16, ROWS, 128), f32),
                pltpu.VMEM((3, 14, ROWS, 128), f32),
                pltpu.VMEM((3, 14, ROWS, 128), f32),
                pltpu.VMEM((3, 8, ROWS, 128), f32),
                pltpu.VMEM((8, 2, 8, 128), f32),
                pltpu.VMEM((9, 2, 8, 128), f32),
                pltpu.VMEM((15, 2, 8, 128), f32),
                pltpu.VMEM((16, 2, 8, 128), f32),
                pltpu.VMEM((18, ROWS, 128), f32),
                pltpu.VMEM((9, ROWS, 128), f32),
                pltpu.VMEM((5, 40, 128), f32),
                pltpu.VMEM((19, 8, 128), f32),
                pltpu.VMEM((2, 5, 8, 128), f32),
                pltpu.VMEM((3, 2, 2, 8, 128), f32),
                pltpu.VMEM((2, 2, 8, 128), f32),
                pltpu.VMEM((23, 8, 128), f32),
                pltpu.VMEM((2, 5, 8, 128), f32),
                pltpu.VMEM((3, 2, 3, 8, 128), f32),
                pltpu.VMEM((2, 2, 8, 128), f32),
                pltpu.SMEM((16,), f32),
                pltpu.VMEM((2, 19, 8, 128), f32),
                pltpu.VMEM((19, 8, 128), f32),
                pltpu.VMEM((19, 8, 128), f32),
                pltpu.VMEM((19, 8, 128), f32),
                pltpu.VMEM((19, 8, 128), f32),
                pltpu.VMEM((5, 24, 128), f32),
                dma((3,)), dma((11,)), dma((11,)), dma((2,)), dma((2,)), dma((8,)), dma((8,)),
                dma((14,)), dma((14,)), dma((14,)), dma((14,)),
            ],
            compiler_params=pltpu.CompilerParams(
                collective_id=0, has_side_effects=True, vmem_limit_bytes=40 * 2**20),
            name="cycle",
        )(*(pltpu.with_memory_space_constraint(a, pltpu.HBM) for a in (right_side, classes, table)))

    return jax.shard_map(
        shards,
        mesh=mesh,
        in_specs=(P(None, "gx", "gy", None), P("gx", "gy", None), P()),
        out_specs=P(None, "gx", "gy", None),
        check_vma=False,
    )
```

```python
import functools

import jax
import jax.numpy as jnp
from jax import lax
from jax.experimental import pallas as pl
from jax.experimental.pallas import tpu as pltpu
from jax.sharding import PartitionSpec as P

MESH = pl.DeviceIdType.MESH
ROWS = 48


def coefficients(top, ratio, count):
    low = top / ratio
    center = 0.5 * (top + low)
    radius = 0.5 * (top - low)
    sharp = center / radius
    rho = 1.0 / sharp
    steps = []
    for _ in range(1, count):
        rho_next = 1.0 / (2.0 * sharp - rho)
        steps.append((rho_next * rho, 2.0 * rho_next / radius))
        rho = rho_next
    return 1.0 / center, steps


def roll(value, shift, axis):
    return pltpu.roll(value, shift % value.shape[axis], axis)


def kernel(nx, ny, rhs, classes, table, out, base, kinds, sig, upd, res, acc,
           pack_dn, pack_up, got_dn, got_up, nod, node_sum, red, cs_main, cs_pack, cs_got, cs_far,
           cf_main, cf_pack, cf_got, cf_far, values_in, cm_one, g_one, g_two, s_one, s_two, fine,
           sem_in, send, recv, far_send, far_recv, x2_send, x2_recv, cs_send, cs_recv, x3_send, x3_recv):
    gx, gy = lax.axis_index("gx"), lax.axis_index("gy")
    first_x, last_x, first_y, last_y = gx == 0, gx == nx - 1, gy == 0, gy == ny - 1

    def at(dx, dy):
        return (lax.rem(gx + dx + nx, nx), lax.rem(gy + dy + ny, ny))

    near = [(1, 1), (1, -1), (-1, 1), (-1, -1), (1, 0), (-1, 0), (0, 1), (0, -1)]

    def remote(source, target, sems, index, where):
        return pltpu.make_async_remote_copy(
            src_ref=source, dst_ref=target, send_sem=sems[0].at[index], recv_sem=sems[1].at[index],
            device_id=at(*where), device_id_type=MESH)

    barrier = pltpu.get_barrier_semaphore()
    for where in near:
        pl.semaphore_signal(barrier, inc=1, device_id=at(*where), device_id_type=MESH)
    loads = [
        pltpu.make_async_copy(table, values_in, sem_in.at[2]),
        pltpu.make_async_copy(classes, kinds, sem_in.at[1]),
        pltpu.make_async_copy(rhs, base.at[:, 3:11, 0:32], sem_in.at[0]),
    ]
    for copy in loads:
        copy.start()

    pl.semaphore_wait(barrier, len(near))
    x1 = (send, recv)
    first = [
        remote(rhs.at[:, 5:8], base.at[:, 0:3, 0:32], x1, 0, (1, 0)),
        remote(rhs.at[1:3, 0:3], base.at[1:3, 11:14, 0:32], x1, 1, (-1, 0)),
        remote(rhs.at[0:1, 0:2], base.at[0:1, 11:13, 0:32], x1, 10, (-1, 0)),
    ]
    for copy in first:
        copy.start()
    for copy in loads:
        copy.wait()

    values = [values_in[k] for k in range(16)]
    for x in range(8):
        code = kinds[x]
        level = values
        for bit in range(4):
            flag = (code & (1 << bit)) != 0
            level = [jnp.where(flag, level[2 * i + 1], level[2 * i]) for i in range(len(level) // 2)]
        sig[x + 4, 0:32] = level[0]

    sub = lax.broadcasted_iota(jnp.int32, (8, 128), 0)
    lower = sub < 4
    for x in range(8):
        ux, uy, uz = (base[c, x + 3, 0:8] for c in range(3))
        sg = sig[x + 4, 0:8]
        pack_dn[x, 0] = jnp.where(lower, ux, roll(uy, 4, 0))
        pack_dn[x, 1] = jnp.where(lower, uz, roll(sg, 4, 0))
        ux, uy, uz = (base[c, x + 3, 24:32] for c in range(3))
        sg = sig[x + 4, 24:32]
        pack_up[x, 0] = jnp.where(lower, roll(uy, 4, 0), ux)
        pack_up[x, 1] = jnp.where(lower, roll(sg, 4, 0), uz)
    for x in range(8):
        pack_up[8, 0, x:x + 1] = sig[x + 4, 27:28]
    pack_up[8, 1] = jnp.zeros((8, 128), jnp.float32)

    second = [
        remote(pack_dn.at[0:3], got_dn.at[12:15], x1, 2, (-1, -1)),
        remote(pack_up.at[0:3], got_up.at[13:16], x1, 3, (-1, 1)),
        remote(pack_dn.at[5:8], got_dn.at[9:12], x1, 4, (1, -1)),
        remote(pack_up.at[4:8], got_up.at[9:13], x1, 5, (1, 1)),
        remote(pack_dn, got_dn.at[0:8], x1, 6, (0, -1)),
        remote(pack_up, got_up.at[0:9], x1, 7, (0, 1)),
        remote(sig.at[10:12, 0:32], sig.at[2:4, 0:32], x1, 8, (1, 0)),
        remote(sig.at[4:6, 0:32], sig.at[12:14, 0:32], x1, 9, (-1, 0)),
    ]
    for copy in second:
        copy.start()
    far = (far_send, far_recv)
    later = [
        remote(sig.at[8:10, 0:32], sig.at[0:2, 0:32], far, 0, (1, 0)),
        remote(sig.at[6:7, 0:32], sig.at[14:15, 0:32], far, 1, (-1, 0)),
    ]

    lane = lax.broadcasted_iota(jnp.int32, (ROWS, 128), 1)
    row = lax.broadcasted_iota(jnp.int32, (ROWS, 128), 0)
    lane_end, lane_start = lane == 127, lane == 0
    f32 = lambda flag: flag.astype(jnp.float32)
    keep_hi, keep_lo = 1.0 - f32(last_y), 1.0 - f32(first_y)
    row_mask = jnp.where(row < 32, 1.0, jnp.where(row < 40, keep_hi, keep_lo))
    row_zero = (row[0:8] == 0) & first_y

    def next_z(f):
        return jnp.where(lane_end, 0.0, roll(f, -1, 1))

    def prev_z(f):
        return jnp.where(lane_start, 0.0, roll(f, 1, 1))

    def next_y(f):
        return roll(f, -1, 0)

    def prev_y(f):
        return roll(f, 1, 0)

    def prev_y_inside(f):
        moved = roll(f, 1, 0)
        return jnp.concatenate([jnp.where(row_zero, 0.0, moved[0:8]), moved[8:]], axis=0)

    fine_z = lax.broadcasted_iota(jnp.int32, (256, 128), 0)
    packed_z = lax.broadcasted_iota(jnp.int32, (256, 128), 1)
    half = fine_z // 128 == packed_z // 64
    apart = (fine_z % 128) - 2 * (packed_z % 64)
    mean_z = jnp.where(half & ((apart == 0) | (apart == 1)), 0.125, 0.0)
    rest_z = jnp.where(half, jnp.where(apart == 0, 1.0, jnp.where(jnp.abs(apart) == 1, 0.5, 0.0)), 0.0)
    dot = functools.partial(jnp.dot, precision=lax.Precision.HIGHEST, preferred_element_type=jnp.float32)

    for x in range(4):
        red[x, 8:40] = sig[2 * x + 4, 0:32] + sig[2 * x + 5, 0:32]
    pairs = [red[x, pl.ds(8, 16, stride=2)] + red[x, pl.ds(9, 16, stride=2)] for x in range(4)]
    wide = jnp.concatenate(
        [jnp.concatenate([p[0:8] for p in pairs], axis=0), jnp.concatenate([p[8:16] for p in pairs], axis=0)], axis=1)
    coarse = 2.0 * dot(wide, mean_z)
    for x in range(4):
        cs_main[7 + x] = coarse[8 * x:8 * x + 8]

    plane_x = lax.broadcasted_iota(jnp.int32, (19, 8, 128), 0) - 7 + 4 * gx
    plane_ok = (plane_x >= 0) & (plane_x < 4 * nx)
    left3 = lax.broadcasted_iota(jnp.int32, (19, 8, 128), 2) < 64
    cm_one[0] = jnp.where(plane_ok, 1.0, 0.0)
    cm_one[1] = jnp.where(plane_ok, jnp.where(left3, keep_hi, keep_lo), 0.0)

    left = lax.broadcasted_iota(jnp.int32, (8, 128), 1) < 64

    def flip(tile):
        return roll(tile, 64, 1)

    def halves(a, b):
        if b is None:
            return a, flip(a)
        return jnp.where(left, a, flip(b)), jnp.where(left, flip(a), b)

    def unhalve(dn, up):
        return jnp.where(left, dn, flip(up)), jnp.where(left, flip(dn), up)

    def spread(main, pack, got, far_got, sems, own, count):
        tiles = [main[own + i] for i in range(count)] + [None]
        pairs = [halves(tiles[0], tiles[1]), halves(tiles[2], tiles[3])]
        odd = [halves(tiles[1], tiles[2]), halves(tiles[3], tiles[4])]
        if count == 5:
            pairs.append(halves(tiles[4], None))
        number = len(pairs)
        for i, (dn, up) in enumerate(pairs):
            pack[0, i] = dn
            pack[1, i] = up
        for i, (one, two) in enumerate((odd, pairs[:2])):
            pack[0, 3 + i] = jnp.where(lower, one[0], roll(two[0], 4, 0))
            pack[1, 3 + i] = jnp.where(lower, roll(one[1], 4, 0), two[1])
        block = main.at[own:own + count]
        size, end = count - 1, own + 2 * count
        distant = [
            remote(main.at[own + 1:own + count], main.at[0:size], sems, 0, (2, 0)),
            remote(main.at[own:own + 4], main.at[end:end + 4], sems, 1, (-2, 0)),
        ]
        for i, dx in enumerate((2, -2)):
            for j, dy in enumerate((-1, 1)):
                distant.append(remote(pack.at[j, 3 + i], far_got.at[i, j], sems, 2 + 2 * i + j, (dx, dy)))
        close = []
        for i, dx in enumerate((1, -1, 0)):
            for j, dy in enumerate((-1, 1)):
                close.append(remote(pack.at[j, 0:number], got.at[i, j, 0:number], sems, 6 + 2 * i + j, (dx, dy)))
        close.append(remote(block, main.at[own - count:own], sems, 12, (1, 0)))
        close.append(remote(block, main.at[own + count:own + 2 * count], sems, 13, (-1, 0)))
        return distant, close

    def received(got, far_got, number):
        planes = []
        for spot in (0, 2, 1):
            block = []
            for i in range(number):
                block += list(unhalve(got[spot, 0, i], got[spot, 1, i]))
            planes.append(block[:5] if number == 3 else block)
        sides = []
        for i in range(2):
            dn, up = far_got[i, 0], far_got[i, 1]
            sides.append(list(unhalve(dn, roll(up, 4, 0))) + list(unhalve(roll(dn, 4, 0), up)))
        return sides[0], planes[0], planes[1], planes[2], sides[1]

    for copy in first + second:
        copy.wait()
    cs_distant, cs_close = spread(cs_main, cs_pack, cs_got, cs_far, (cs_send, cs_recv), 7, 4)
    for copy in later + cs_close:
        copy.start()

    def spot_dn(x):
        return x if 0 <= x < 8 else (12 + x if x < 0 else 4 + x)

    def spot_up(x):
        return x if 0 <= x < 8 else (13 + x if x < 0 else 5 + x)

    zero_tile = jnp.zeros((8, 128), jnp.float32)
    for x in range(-4, 11):
        if x > -4:
            a, b = got_dn[spot_dn(x), 0], got_dn[spot_dn(x), 1]
            base[0, x + 3, 32:40] = a * keep_hi
            base[1, x + 3, 32:40] = roll(a, 4, 0) * keep_hi
            base[2, x + 3, 32:40] = b * keep_hi
            sig[x + 4, 32:40] = roll(b, 4, 0) * keep_hi
        else:
            sig[x + 4, 32:40] = zero_tile
        a, b = got_up[spot_up(x), 0], got_up[spot_up(x), 1]
        if x > -4:
            base[0, x + 3, 40:48] = a * keep_lo
            base[1, x + 3, 40:48] = roll(a, 4, 0) * keep_lo
            base[2, x + 3, 40:48] = b * keep_lo
        sg = roll(b, 4, 0)
        if 0 <= x < 8:
            sg = jnp.where(sub == 3, got_up[8, 0, x:x + 1], sg)
        sig[x + 4, 40:48] = sg * keep_lo

    @pl.when(first_x)
    def _():
        base[:, 0:3] = jnp.zeros((3, 3, ROWS, 128), jnp.float32)
        sig[2:4] = jnp.zeros((2, ROWS, 128), jnp.float32)

    @pl.when(last_x)
    def _():
        base[:, 11:14] = jnp.zeros((3, 3, ROWS, 128), jnp.float32)
        sig[12:14] = jnp.zeros((2, ROWS, 128), jnp.float32)

    keep_left, keep_right = 1.0 - f32(first_x), 1.0 - f32(last_x)

    def side(x):
        return keep_left if x < 0 else (keep_right if x > 7 else None)

    inv, steps = coefficients(20.0, 30.0, 4)
    nodal_prev = None
    for turn, (c_old, c_res) in enumerate(steps):
        lo, hi = -2 + turn, 9 - turn
        get = (lambda c, x: base[c, x + 3]) if turn == 0 else (lambda c, x: upd[c, x + 2])
        scaled = row_mask * c_res
        before = None
        here = [get(c, lo - 1) for c in range(3)]
        for x in range(lo - 1, hi + 1):
            after = [None if (c == 0 and x == hi) else get(c, x + 1) for c in range(3)]
            ux, uy, uz = here
            cy = (next_z(ux) - ux) - (after[2] - uz)
            cz = (after[1] - uy) - (next_y(ux) - ux)
            if x == -1:
                cy, cz = cy * keep_left, cz * keep_left
            if x >= lo:
                cx = (next_y(uz) - uz) - (next_z(uy) - uy)
                sg = sig[x + 4]
                applied = [
                    (prev_y_inside(cz) - cz) - (prev_z(cy) - cy) + sg * ux,
                    (prev_z(cx) - cx) - (before[1] - cz) + sg * uy,
                    (before[0] - cy) - (prev_y_inside(cx) - cx) + sg * uz,
                ]
                weight = scaled if side(x) is None else scaled * side(x)
                rest = []
                for c in range(3):
                    if turn == 0:
                        u = here[c] * inv
                        r = here[c] - applied[c] * inv
                    else:
                        u = here[c]
                        r = res[c, x + 2] - applied[c]
                    new = c_old * u + weight * r
                    if turn < 2:
                        upd[c, x + 2] = new
                        res[c, x + 2] = r
                        if 0 <= x < 8:
                            acc[c, x] = u + new if turn == 0 else acc[c, x] + new
                    else:
                        answer = acc[c, x] + new
                        acc[c, x] = answer
                        rest.append(base[c, x + 3] - sg * answer)
                if turn == 2:
                    rx, ry, rz = rest
                    total = (ry - prev_y(ry)) + (rz - prev_z(rz)) + rx
                    nod[x + 5, 0:32] = (total if nodal_prev is None else total - nodal_prev)[0:32]
                    nodal_prev = rx
                    if x == 7:
                        nod[13, 0:32] = rx[0:32]
            before = (cy, cz)
            here = after

    x2 = (x2_send, x2_recv)
    swap = [
        remote(nod.at[9:14, 0:32], nod.at[0:5, 0:32], x2, 0, (1, 0)),
        remote(nod.at[5:9, 0:32], nod.at[14:18, 0:32], x2, 1, (-1, 0)),
        remote(nod.at[9:14, 24:32], nod.at[0:5, 40:48], x2, 2, (1, 1)),
        remote(nod.at[9:14, 0:8], nod.at[0:5, 32:40], x2, 3, (1, -1)),
        remote(nod.at[5:9, 24:32], nod.at[14:18, 40:48], x2, 4, (-1, 1)),
        remote(nod.at[5:9, 0:8], nod.at[14:18, 32:40], x2, 5, (-1, -1)),
        remote(nod.at[5:14, 24:32], nod.at[5:14, 40:48], x2, 6, (0, 1)),
        remote(nod.at[5:14, 0:8], nod.at[5:14, 32:40], x2, 7, (0, -1)),
    ]
    for copy in swap + cs_distant:
        copy.start()

    for copy in later + swap:
        copy.wait()

    @pl.when(first_x)
    def _():
        nod[0:5] = jnp.zeros((5, ROWS, 128), jnp.float32)
        sig[0:2] = jnp.zeros((2, ROWS, 128), jnp.float32)

    @pl.when(last_x)
    def _():
        sig[14:15] = jnp.zeros((1, ROWS, 128), jnp.float32)

    nod[5] = nod[5] - nod[4]
    nod[14] = nod[14] - nod[13]

    @pl.when(last_x)
    def _():
        nod[14:18] = jnp.zeros((4, ROWS, 128), jnp.float32)

    @pl.when(first_y)
    def _():
        nod[:, 40:48] = jnp.zeros((18, 8, 128), jnp.float32)

    @pl.when(last_y)
    def _():
        nod[:, 32:40] = jnp.zeros((18, 8, 128), jnp.float32)

    def place(x):
        return x + 4 if x < 0 else (x + 5 if x < 8 else x + 6)

    inv, steps = coefficients(48.0, 30.0, 4)
    steps = steps + [None]
    nupd, nres = upd.at[0], res.at[0]
    planes = []
    for turn, step in enumerate(steps):
        lo, hi = -3 + turn, 10 - turn
        get = (lambda x: nod[place(x)]) if turn == 0 else (lambda x: nupd[x + 3])
        here = get(lo - 1)
        before = None
        for x in range(lo - 1, hi + 1):
            after = get(x + 1)
            sg = sig[x + 4]
            flux_x = sg * (after - here)
            if x >= lo:
                flux_y = sg * (next_y(here) - here)
                flux_z = sg * (next_z(here) - here)
                applied = (flux_x - before) + (flux_y - prev_y(flux_y)) + (flux_z - prev_z(flux_z))
                if turn == 0:
                    u = here * inv
                    r = here - applied * inv
                else:
                    u = here
                    r = nres[x + 3] - applied
                if step is not None:
                    weight = row_mask * step[1]
                    weight = weight if side(x) is None else weight * side(x)
                    new = step[0] * u + weight * r
                    nupd[x + 3] = new
                    nres[x + 3] = r
                    if 0 <= x < 9:
                        node_sum[x] = u + new if turn == 0 else node_sum[x] + new
                else:
                    planes.append(r)
                    if x % 2 == 1:
                        total = planes[x - 1] + 0.5 * planes[x]
                        if x > 1:
                            total = total + 0.5 * planes[x - 2]
                        red[x // 2, 8:40] = total[0:32]
                        red[x // 2, 0:8] = total[40:48] * keep_lo
                    if x == 7:
                        red[4, 8:40] = 0.5 * r[0:32]
                        red[4, 0:8] = 0.5 * r[40:48] * keep_lo
            before = flux_x
            here = after

    thin = [red[x, pl.ds(8, 16, stride=2)] + 0.5 * (red[x, pl.ds(9, 16, stride=2)] + red[x, pl.ds(7, 16, stride=2)])
            for x in range(5)]
    wide = jnp.concatenate(
        [jnp.concatenate([p[0:8] for p in thin], axis=0), jnp.concatenate([p[8:16] for p in thin], axis=0)], axis=1)
    coarse = dot(wide, rest_z)
    for x in range(5):
        cf_main[9 + x] = coarse[8 * x:8 * x + 8]
    cf_distant, cf_close = spread(cf_main, cf_pack, cf_got, cf_far, (x3_send, x3_recv), 9, 5)
    for copy in cf_distant + cf_close:
        copy.start()
    for copy in cs_distant + cs_close:
        copy.wait()

    far_low, low_block, own_block, high_block, far_high = received(cs_got, cs_far, 2)
    halo = far_low[:3] + low_block + own_block + high_block + far_high
    for x in range(19):
        s_one[x] = cs_main[x] * cm_one[0, x]
        s_two[x] = halo[x] * cm_one[1, x]

    for copy in cf_distant + cf_close:
        copy.wait()

    far_low, low_block, own_block, high_block, far_high = received(cf_got, cf_far, 3)
    halo = far_low + low_block + own_block + high_block + far_high
    where_plane = [0, 1, 2, 4, 5, 6, 7, 9, 10, 11, 12, 14, 15, 16, 17, 19, 20, 21, 22]
    extra = {-4: (3, gx > 1), 0: (8, gx > 0), 4: (13, None), 8: (18, None)}
    for x in range(-7, 12):
        one, two = cf_main[where_plane[x + 7]], halo[where_plane[x + 7]]
        if x in extra:
            spot, valid = extra[x]
            add_one, add_two = cf_main[spot], halo[spot]
            if valid is not None:
                add_one, add_two = add_one * f32(valid), add_two * f32(valid)
            one, two = one + add_one, two + add_two
        g_one[x + 7] = one * cm_one[0, x + 7]
        g_two[x + 7] = two * cm_one[1, x + 7]

    inv, steps = coefficients(96.0, 100.0, 8)

    def lanes3(n):
        return lax.broadcasted_iota(jnp.int32, (n, 8, 128), 2)

    def swapped(one, two, first_side):
        turn_one, turn_two = roll(one, 64, 2), roll(two, 64, 2)
        pick = lanes3(one.shape[0]) < 64
        if first_side:
            return jnp.where(pick, turn_one, turn_two), jnp.where(pick, turn_two, turn_one)
        return jnp.where(pick, turn_two, turn_one), jnp.where(pick, turn_one, turn_two)

    def coarse_next_y(one, two):
        seam_one, seam_two = swapped(one, two, True)
        top = lax.broadcasted_iota(jnp.int32, one.shape, 1) == 0
        return roll(jnp.where(top, seam_one, one), -1, 1), roll(jnp.where(top, seam_two, two), -1, 1)

    def coarse_prev_y(one, two):
        seam_one, seam_two = swapped(one, two, False)
        bottom = lax.broadcasted_iota(jnp.int32, one.shape, 1) == 7
        return roll(jnp.where(bottom, seam_one, one), 1, 1), roll(jnp.where(bottom, seam_two, two), 1, 1)

    def coarse_next_z(f):
        return jnp.where(lanes3(f.shape[0]) % 64 == 63, 0.0, roll(f, -1, 2))

    def coarse_prev_z(f):
        return jnp.where(lanes3(f.shape[0]) % 64 == 0, 0.0, roll(f, 1, 2))

    f_one, f_two = g_one[...], g_two[...]
    r_one = r_two = None
    answer = None
    low = -7
    for turn, (c_old, c_res) in enumerate(steps):
        n = f_one.shape[0]
        sg_one, sg_two = s_one[low + 7:low + 7 + n], s_two[low + 7:low + 7 + n]
        x_one = sg_one[:-1] * (f_one[1:] - f_one[:-1])
        x_two = sg_two[:-1] * (f_two[1:] - f_two[:-1])
        mid_one, mid_two = f_one[1:-1], f_two[1:-1]
        in_one, in_two = sg_one[1:-1], sg_two[1:-1]
        up_one, up_two = coarse_next_y(mid_one, mid_two)
        y_one, y_two = in_one * (up_one - mid_one), in_two * (up_two - mid_two)
        back_one, back_two = coarse_prev_y(y_one, y_two)
        results = []
        for f, x_flux, y_flux, y_back, s in (
            (mid_one, x_one, y_one, back_one, in_one), (mid_two, x_two, y_two, back_two, in_two)):
            z_flux = s * (coarse_next_z(f) - f)
            results.append((x_flux[1:] - x_flux[:-1]) + (y_flux - y_back) + (z_flux - coarse_prev_z(z_flux)))
        low += 1
        if turn == 0:
            r_one, r_two = mid_one - results[0] * inv, mid_two - results[1] * inv
            mid_one, mid_two = mid_one * inv, mid_two * inv
            answer = [mid_one[6:11], mid_two[6:11]]
        else:
            r_one, r_two = r_one[1:-1] - results[0], r_two[1:-1] - results[1]
        n -= 2
        f_one = c_old * mid_one + c_res * (cm_one[0, low + 7:low + 7 + n] * r_one)
        f_two = c_old * mid_two + c_res * (cm_one[1, low + 7:low + 7 + n] * r_two)
        answer = [answer[0] + f_one[-low:5 - low], answer[1] + f_two[-low:5 - low]]

    coarse_k = lax.broadcasted_iota(jnp.int32, (128, 256), 0)
    fine_k = lax.broadcasted_iota(jnp.int32, (128, 256), 1)
    same = coarse_k // 64 == fine_k // 128
    apart = (fine_k % 128) - 2 * (coarse_k % 64)
    grow = jnp.where(same, jnp.where(apart == 0, 1.0, jnp.where(jnp.abs(apart) == 1, 0.5, 0.0)), 0.0)
    body = dot(answer[0].reshape(40, 128), grow)
    edge = dot(answer[1].reshape(40, 128), grow[:, 0:128])
    for x in range(5):
        fine[x, 0:8] = body[8 * x:8 * x + 8, 0:128]
        fine[x, 8:16] = body[8 * x:8 * x + 8, 128:256]
        fine[x, 16:24] = edge[8 * x:8 * x + 8]

    own, nxt = None, None
    half_rows = []
    for x in range(5):
        a, b = fine[x, 0:16], fine[x, 1:17]
        red[x, pl.ds(0, 16, stride=2)] = a
        red[x, pl.ds(1, 16, stride=2)] = 0.5 * (a + b)
        red[x, 32:40] = fine[x, 16:24]
    for x in range(9):
        value = red[x // 2] if x % 2 == 0 else 0.5 * (red[x // 2] + red[x // 2 + 1])
        node_sum[x, 0:40] = node_sum[x, 0:40] + value
    keep_next = [keep_hi, keep_right]
    for x in range(8):
        here = node_sum[x, 0:32]
        after = node_sum[x + 1, 0:32]
        if x == 7:
            after = after * keep_right
        shifted = roll(node_sum[x], -1, 0)[0:32]
        last = (row[0:32] == 31) & last_y
        shifted = jnp.where(last, 0.0, shifted)
        out[0, x] = acc[0, x, 0:32] + (after - here)
        out[1, x] = acc[1, x, 0:32] + (shifted - here)
        out[2, x] = acc[2, x, 0:32] + (jnp.where(lane_end[0:32], 0.0, roll(here, -1, 1)) - here)


def solution(mesh):
    nx, ny = mesh.shape["gx"], mesh.shape["gy"]
    f32 = jnp.float32
    dma = pltpu.SemaphoreType.DMA

    def shards(right_side, classes, table):
        return pl.pallas_call(
            functools.partial(kernel, nx, ny),
            out_shape=jax.ShapeDtypeStruct(right_side.shape, f32),
            in_specs=[pl.BlockSpec(memory_space=pltpu.HBM)] * 3,
            out_specs=pl.BlockSpec(memory_space=pltpu.VMEM),
            scratch_shapes=[
                pltpu.VMEM((3, 14, ROWS, 128), f32),
                pltpu.VMEM((8, 32, 128), jnp.int32),
                pltpu.VMEM((16, ROWS, 128), f32),
                pltpu.VMEM((3, 14, ROWS, 128), f32),
                pltpu.VMEM((3, 14, ROWS, 128), f32),
                pltpu.VMEM((3, 8, ROWS, 128), f32),
                pltpu.VMEM((8, 2, 8, 128), f32),
                pltpu.VMEM((9, 2, 8, 128), f32),
                pltpu.VMEM((15, 2, 8, 128), f32),
                pltpu.VMEM((16, 2, 8, 128), f32),
                pltpu.VMEM((18, ROWS, 128), f32),
                pltpu.VMEM((9, ROWS, 128), f32),
                pltpu.VMEM((5, 40, 128), f32),
                pltpu.VMEM((19, 8, 128), f32),
                pltpu.VMEM((2, 5, 8, 128), f32),
                pltpu.VMEM((3, 2, 2, 8, 128), f32),
                pltpu.VMEM((2, 2, 8, 128), f32),
                pltpu.VMEM((23, 8, 128), f32),
                pltpu.VMEM((2, 5, 8, 128), f32),
                pltpu.VMEM((3, 2, 3, 8, 128), f32),
                pltpu.VMEM((2, 2, 8, 128), f32),
                pltpu.SMEM((16,), f32),
                pltpu.VMEM((2, 19, 8, 128), f32),
                pltpu.VMEM((19, 8, 128), f32),
                pltpu.VMEM((19, 8, 128), f32),
                pltpu.VMEM((19, 8, 128), f32),
                pltpu.VMEM((19, 8, 128), f32),
                pltpu.VMEM((5, 24, 128), f32),
                dma((3,)), dma((11,)), dma((11,)), dma((2,)), dma((2,)), dma((8,)), dma((8,)),
                dma((14,)), dma((14,)), dma((14,)), dma((14,)),
            ],
            compiler_params=pltpu.CompilerParams(
                collective_id=0, has_side_effects=True, vmem_limit_bytes=40 * 2**20),
            name="cycle",
        )(*(pltpu.with_memory_space_constraint(a, pltpu.HBM) for a in (right_side, classes, table)))

    return jax.shard_map(
        shards,
        mesh=mesh,
        in_specs=(P(None, "gx", "gy", None), P("gx", "gy", None), P()),
        out_specs=P(None, "gx", "gy", None),
        check_vma=False,
    )
```

```python
import functools

import jax
import jax.numpy as jnp
from jax import lax
from jax.experimental import pallas as pl
from jax.experimental.pallas import tpu as pltpu
from jax.sharding import PartitionSpec as P

MESH = pl.DeviceIdType.MESH
ROWS = 48


def coefficients(top, ratio, count):
    low = top / ratio
    center = 0.5 * (top + low)
    radius = 0.5 * (top - low)
    sharp = center / radius
    rho = 1.0 / sharp
    steps = []
    for _ in range(1, count):
        rho_next = 1.0 / (2.0 * sharp - rho)
        steps.append((rho_next * rho, 2.0 * rho_next / radius))
        rho = rho_next
    return 1.0 / center, steps


def roll(value, shift, axis):
    return pltpu.roll(value, shift % value.shape[axis], axis)


def kernel(nx, ny, rhs, classes, table, out, base, kinds, sig, upd, upd_next, drop, res, acc,
           pack_dn, pack_up, got_dn, got_up, nod, node_sum, red, cs_main, cs_pack, cs_got, cs_far,
           cf_main, cf_pack, cf_got, cf_far, values_in, cm_one, g_one, g_two, s_one, s_two, s_back, fine,
           sem_in, send, recv, far_send, far_recv, x2_send, x2_recv, cs_send, cs_recv, x3_send, x3_recv):
    gx, gy = lax.axis_index("gx"), lax.axis_index("gy")
    first_x, last_x, first_y, last_y = gx == 0, gx == nx - 1, gy == 0, gy == ny - 1

    def at(dx, dy):
        return (lax.rem(gx + dx + nx, nx), lax.rem(gy + dy + ny, ny))

    near = [(1, 1), (1, -1), (-1, 1), (-1, -1), (1, 0), (-1, 0), (0, 1), (0, -1)]

    def remote(source, target, sems, index, where):
        return pltpu.make_async_remote_copy(
            src_ref=source, dst_ref=target, send_sem=sems[0].at[index], recv_sem=sems[1].at[index],
            device_id=at(*where), device_id_type=MESH)

    barrier = pltpu.get_barrier_semaphore()
    for where in near:
        pl.semaphore_signal(barrier, inc=1, device_id=at(*where), device_id_type=MESH)
    loads = [
        pltpu.make_async_copy(table, values_in, sem_in.at[2]),
        pltpu.make_async_copy(classes, kinds, sem_in.at[1]),
        pltpu.make_async_copy(rhs, base.at[:, 3:11, 0:32], sem_in.at[0]),
    ]
    for copy in loads:
        copy.start()

    pl.semaphore_wait(barrier, len(near))
    x1 = (send, recv)
    first = [
        remote(rhs.at[1:3, 0:3], base.at[1:3, 11:14, 0:32], x1, 1, (-1, 0)),
        remote(rhs.at[1:3, 5:8], base.at[1:3, 0:3, 0:32], x1, 0, (1, 0)),
        remote(rhs.at[0:1, 0:2], base.at[0:1, 11:13, 0:32], x1, 10, (-1, 0)),
        remote(rhs.at[0:1, 5:8], base.at[0:1, 0:3, 0:32], x1, 11, (1, 0)),
    ]
    for copy in first:
        copy.start()
    for copy in loads:
        copy.wait()

    values = [values_in[k] for k in range(16)]
    for x in range(8):
        code = kinds[x]
        level = values
        for bit in range(4):
            flag = (code & (1 << bit)) != 0
            level = [jnp.where(flag, level[2 * i + 1], level[2 * i]) for i in range(len(level) // 2)]
        sig[x + 4, 0:32] = level[0]

    sub = lax.broadcasted_iota(jnp.int32, (8, 128), 0)
    lower = sub < 4
    for x in range(8):
        ux, uy, uz = (base[c, x + 3, 0:8] for c in range(3))
        sg = sig[x + 4, 0:8]
        pack_dn[x, 0] = jnp.where(lower, ux, roll(uy, 4, 0))
        pack_dn[x, 1] = jnp.where(lower, uz, roll(sg, 4, 0))
        ux, uy, uz = (base[c, x + 3, 24:32] for c in range(3))
        sg = sig[x + 4, 24:32]
        pack_up[x, 0] = jnp.where(lower, roll(uy, 4, 0), ux)
        pack_up[x, 1] = jnp.where(lower, roll(sg, 4, 0), uz)
    for x in range(8):
        pack_up[8, 0, x:x + 1] = sig[x + 4, 27:28]
    pack_up[8, 1] = jnp.zeros((8, 128), jnp.float32)

    second = [
        remote(pack_dn.at[0:3], got_dn.at[12:15], x1, 2, (-1, -1)),
        remote(pack_up.at[0:3], got_up.at[13:16], x1, 3, (-1, 1)),
        remote(pack_dn.at[5:8], got_dn.at[9:12], x1, 4, (1, -1)),
        remote(pack_up.at[4:8], got_up.at[9:13], x1, 5, (1, 1)),
        remote(pack_dn, got_dn.at[0:8], x1, 6, (0, -1)),
        remote(pack_up, got_up.at[0:9], x1, 7, (0, 1)),
        remote(sig.at[10:12, 0:32], sig.at[2:4, 0:32], x1, 8, (1, 0)),
        remote(sig.at[4:6, 0:32], sig.at[12:14, 0:32], x1, 9, (-1, 0)),
    ]
    for copy in second[4:6] + second[0:4] + second[6:8]:
        copy.start()
    far = (far_send, far_recv)
    later = [
        remote(sig.at[8:10, 0:32], sig.at[0:2, 0:32], far, 0, (1, 0)),
        remote(sig.at[6:7, 0:32], sig.at[14:15, 0:32], far, 1, (-1, 0)),
    ]

    lane = lax.broadcasted_iota(jnp.int32, (ROWS, 128), 1)
    row = lax.broadcasted_iota(jnp.int32, (ROWS, 128), 0)
    lane_end, lane_start = lane == 127, lane == 0
    f32 = lambda flag: flag.astype(jnp.float32)
    keep_hi, keep_lo = 1.0 - f32(last_y), 1.0 - f32(first_y)
    row_mask = jnp.where(row < 32, 1.0, jnp.where(row < 40, keep_hi, keep_lo))
    row_zero = (row[0:8] == 0) & first_y

    def next_z(f):
        return jnp.where(lane_end, 0.0, roll(f, -1, 1))

    def prev_z(f):
        return jnp.where(lane_start, 0.0, roll(f, 1, 1))

    def next_y(f):
        return roll(f, -1, 0)

    def prev_y(f):
        return roll(f, 1, 0)

    def prev_y_inside(f):
        moved = roll(f, 1, 0)
        return jnp.concatenate([jnp.where(row_zero, 0.0, moved[0:8]), moved[8:]], axis=0)

    fine_z = lax.broadcasted_iota(jnp.int32, (256, 128), 0)
    packed_z = lax.broadcasted_iota(jnp.int32, (256, 128), 1)
    half = fine_z // 128 == packed_z // 64
    apart = (fine_z % 128) - 2 * (packed_z % 64)
    mean_z = jnp.where(half & ((apart == 0) | (apart == 1)), 0.125, 0.0)
    rest_z = jnp.where(half, jnp.where(apart == 0, 1.0, jnp.where(jnp.abs(apart) == 1, 0.5, 0.0)), 0.0)

    def dot(value, weights):
        weights = weights.astype(jnp.bfloat16)
        total = None
        for _ in range(3):
            part = value.astype(jnp.bfloat16)
            value = value - part.astype(jnp.float32)
            product = jnp.dot(part, weights, preferred_element_type=jnp.float32)
            total = product if total is None else total + product
        return total

    for x in range(4):
        red[x, 8:40] = sig[2 * x + 4, 0:32] + sig[2 * x + 5, 0:32]
    pairs = [red[x, pl.ds(8, 16, stride=2)] + red[x, pl.ds(9, 16, stride=2)] for x in range(4)]
    wide = jnp.concatenate(
        [jnp.concatenate([p[0:8] for p in pairs], axis=0), jnp.concatenate([p[8:16] for p in pairs], axis=0)], axis=1)
    coarse = 2.0 * dot(wide, mean_z)
    for x in range(4):
        cs_main[7 + x] = coarse[8 * x:8 * x + 8]

    plane_x = lax.broadcasted_iota(jnp.int32, (19, 8, 128), 0) - 7 + 4 * gx
    plane_ok = (plane_x >= 0) & (plane_x < 4 * nx)
    left3 = lax.broadcasted_iota(jnp.int32, (19, 8, 128), 2) < 64
    cm_one[0] = jnp.where(plane_ok, 1.0, 0.0)
    cm_one[1] = jnp.where(plane_ok, jnp.where(left3, keep_hi, keep_lo), 0.0)

    left = lax.broadcasted_iota(jnp.int32, (8, 128), 1) < 64

    def flip(tile):
        return roll(tile, 64, 1)

    def halves(a, b):
        if b is None:
            return a, flip(a)
        return jnp.where(left, a, flip(b)), jnp.where(left, flip(a), b)

    def unhalve(dn, up):
        return jnp.where(left, dn, flip(up)), jnp.where(left, flip(dn), up)

    def spread(main, pack, got, far_got, sems, own, count):
        tiles = [main[own + i] for i in range(count)] + [None]
        pairs = [halves(tiles[0], tiles[1]), halves(tiles[2], tiles[3])]
        odd = [halves(tiles[1], tiles[2]), halves(tiles[3], tiles[4])]
        if count == 5:
            pairs.append(halves(tiles[4], None))
        number = len(pairs)
        for i, (dn, up) in enumerate(pairs):
            pack[0, i] = dn
            pack[1, i] = up
        for i, (one, two) in enumerate((odd, pairs[:2])):
            pack[0, 3 + i] = jnp.where(lower, one[0], roll(two[0], 4, 0))
            pack[1, 3 + i] = jnp.where(lower, roll(one[1], 4, 0), two[1])
        block = main.at[own:own + count]
        size, end = count - 1, own + 2 * count
        distant = [
            remote(main.at[own + 1:own + count], main.at[0:size], sems, 0, (2, 0)),
            remote(main.at[own:own + 4], main.at[end:end + 4], sems, 1, (-2, 0)),
        ]
        for i, dx in enumerate((2, -2)):
            for j, dy in enumerate((-1, 1)):
                distant.append(remote(pack.at[j, 3 + i], far_got.at[i, j], sems, 2 + 2 * i + j, (dx, dy)))
        close = []
        for i, dx in enumerate((1, -1, 0)):
            for j, dy in enumerate((-1, 1)):
                close.append(remote(pack.at[j, 0:number], got.at[i, j, 0:number], sems, 6 + 2 * i + j, (dx, dy)))
        close.append(remote(block, main.at[own - count:own], sems, 12, (1, 0)))
        close.append(remote(block, main.at[own + count:own + 2 * count], sems, 13, (-1, 0)))
        return distant, close

    def received(got, far_got, number):
        planes = []
        for spot in (0, 2, 1):
            block = []
            for i in range(number):
                block += list(unhalve(got[spot, 0, i], got[spot, 1, i]))
            planes.append(block[:5] if number == 3 else block)
        sides = []
        for i in range(2):
            dn, up = far_got[i, 0], far_got[i, 1]
            sides.append(list(unhalve(dn, roll(up, 4, 0))) + list(unhalve(roll(dn, 4, 0), up)))
        return sides[0], planes[0], planes[1], planes[2], sides[1]

    cs_distant, cs_close = spread(cs_main, cs_pack, cs_got, cs_far, (cs_send, cs_recv), 7, 4)

    def spot_dn(x):
        return x if 0 <= x < 8 else (12 + x if x < 0 else 4 + x)

    def spot_up(x):
        return x if 0 <= x < 8 else (13 + x if x < 0 else 5 + x)

    zero_tile = jnp.zeros((8, 128), jnp.float32)

    def unpack(planes):
        for x in planes:
            if x > -4:
                a, b = got_dn[spot_dn(x), 0], got_dn[spot_dn(x), 1]
                base[0, x + 3, 32:40] = a * keep_hi
                base[1, x + 3, 32:40] = roll(a, 4, 0) * keep_hi
                base[2, x + 3, 32:40] = b * keep_hi
                sig[x + 4, 32:40] = roll(b, 4, 0) * keep_hi
            else:
                sig[x + 4, 32:40] = zero_tile
            a, b = got_up[spot_up(x), 0], got_up[spot_up(x), 1]
            if x > -4:
                base[0, x + 3, 40:48] = a * keep_lo
                base[1, x + 3, 40:48] = roll(a, 4, 0) * keep_lo
                base[2, x + 3, 40:48] = b * keep_lo
            sg = roll(b, 4, 0)
            if 0 <= x < 8:
                sg = jnp.where(sub == 3, got_up[8, 0, x:x + 1], sg)
            sig[x + 4, 40:48] = sg * keep_lo

    keep_left, keep_right = 1.0 - f32(first_x), 1.0 - f32(last_x)

    def side(x):
        return keep_left if x < 0 else (keep_right if x > 7 else None)

    inv, edge_steps = coefficients(20.0, 30.0, 4)

    def edge_turn(turn, lo, hi):
        c_old, c_res = edge_steps[turn]
        source, target = ((base, upd), (upd, upd_next), (upd_next, None))[turn]
        shift = 3 if turn == 0 else 2
        scaled = row_mask * c_res
        before = None
        here = [source[c, lo - 1 + shift] for c in range(3)]
        for x in range(lo - 1, hi + 1):
            after = [None if (c == 0 and x == hi) else source[c, x + 1 + shift] for c in range(3)]
            ux, uy, uz = here
            cy = (next_z(ux) - ux) - (after[2] - uz)
            cz = (after[1] - uy) - (next_y(ux) - ux)
            if x == -1:
                cy, cz = cy * keep_left, cz * keep_left
            if x >= lo:
                cx = (next_y(uz) - uz) - (next_z(uy) - uy)
                sg = sig[x + 4]
                applied = [
                    (prev_y_inside(cz) - cz) - (prev_z(cy) - cy) + sg * ux,
                    (prev_z(cx) - cx) - (before[1] - cz) + sg * uy,
                    (before[0] - cy) - (prev_y_inside(cx) - cx) + sg * uz,
                ]
                weight = scaled if side(x) is None else scaled * side(x)
                rest = []
                for c in range(3):
                    if turn == 0:
                        u = here[c] * inv
                        r = here[c] - applied[c] * inv
                    else:
                        u = here[c]
                        r = res[c, x + 2] - applied[c]
                    new = c_old * u + weight * r
                    if turn < 2:
                        target[c, x + 2] = new
                        res[c, x + 2] = r
                        if 0 <= x < 8:
                            acc[c, x] = u + new if turn == 0 else acc[c, x] + new
                    else:
                        answer = acc[c, x] + new
                        acc[c, x] = answer
                        rest.append(base[c, x + 3] - sg * answer)
                if turn == 2:
                    rx, ry, rz = rest
                    total = (ry - prev_y(ry)) + (rz - prev_z(rz)) + rx
                    if x not in (0, lo) or x == 5:
                        total = total - drop[x - 1]
                    nod[x + 5, 0:32] = total[0:32]
                    drop[x] = rx
            before = (cy, cz)
            here = after

    for copy in (second[4], second[5]):
        copy.wait()
    unpack(range(8))
    edge_turn(0, 1, 6)
    edge_turn(1, 2, 5)
    edge_turn(2, 3, 4)

    for copy in (first[0], first[2], second[0], second[1], second[7]):
        copy.wait()
    unpack(range(8, 11))

    @pl.when(last_x)
    def _():
        base[:, 11:14] = jnp.zeros((3, 3, ROWS, 128), jnp.float32)
        sig[12:14] = jnp.zeros((2, ROWS, 128), jnp.float32)

    edge_turn(0, 7, 9)
    edge_turn(1, 6, 8)
    edge_turn(2, 5, 7)
    nod[13, 0:32] = drop[7, 0:32]

    x2 = (x2_send, x2_recv)
    swap = [
        remote(nod.at[9:14, 0:32], nod.at[0:5, 0:32], x2, 0, (1, 0)),
        remote(nod.at[5:9, 0:32], nod.at[14:18, 0:32], x2, 1, (-1, 0)),
        remote(nod.at[9:14, 24:32], nod.at[0:5, 40:48], x2, 2, (1, 1)),
        remote(nod.at[9:14, 0:8], nod.at[0:5, 32:40], x2, 3, (1, -1)),
        remote(nod.at[5:9, 24:32], nod.at[14:18, 40:48], x2, 4, (-1, 1)),
        remote(nod.at[5:9, 0:8], nod.at[14:18, 32:40], x2, 5, (-1, -1)),
        remote(nod.at[5:14, 24:32], nod.at[5:14, 40:48], x2, 6, (0, 1)),
        remote(nod.at[5:14, 0:8], nod.at[5:14, 32:40], x2, 7, (0, -1)),
    ]
    for copy in (swap[2], swap[3], swap[0]):
        copy.start()

    for copy in (first[1], first[3], second[2], second[3], second[6]):
        copy.wait()
    for copy in later + cs_close:
        copy.start()
    unpack(range(-4, 0))

    @pl.when(first_x)
    def _():
        base[:, 0:3] = jnp.zeros((3, 3, ROWS, 128), jnp.float32)
        sig[2:4] = jnp.zeros((2, ROWS, 128), jnp.float32)

    edge_turn(0, -2, 0)
    edge_turn(1, -1, 1)
    edge_turn(2, 0, 2)
    nod[8, 0:32] = nod[8, 0:32] - drop[2, 0:32]
    for copy in (swap[4], swap[5], swap[1], swap[6], swap[7]):
        copy.start()
    for copy in cs_distant:
        copy.start()

    for copy in later + swap:
        copy.wait()

    @pl.when(first_x)
    def _():
        nod[0:5] = jnp.zeros((5, ROWS, 128), jnp.float32)
        sig[0:2] = jnp.zeros((2, ROWS, 128), jnp.float32)

    @pl.when(last_x)
    def _():
        sig[14:15] = jnp.zeros((1, ROWS, 128), jnp.float32)

    nod[5] = nod[5] - nod[4]
    nod[14] = nod[14] - nod[13]

    @pl.when(last_x)
    def _():
        nod[14:18] = jnp.zeros((4, ROWS, 128), jnp.float32)

    @pl.when(first_y)
    def _():
        nod[:, 40:48] = jnp.zeros((18, 8, 128), jnp.float32)

    @pl.when(last_y)
    def _():
        nod[:, 32:40] = jnp.zeros((18, 8, 128), jnp.float32)

    def place(x):
        return x + 4 if x < 0 else (x + 5 if x < 8 else x + 6)

    inv, steps = coefficients(48.0, 30.0, 4)
    steps = steps + [None]
    nupd, nres = upd.at[0], res.at[0]
    planes = []
    for turn, step in enumerate(steps):
        lo, hi = -3 + turn, 10 - turn
        get = (lambda x: nod[place(x)]) if turn == 0 else (lambda x: nupd[x + 3])
        here = get(lo - 1)
        before = None
        for x in range(lo - 1, hi + 1):
            after = get(x + 1)
            sg = sig[x + 4]
            flux_x = sg * (after - here)
            if x >= lo:
                flux_y = sg * (next_y(here) - here)
                flux_z = sg * (next_z(here) - here)
                applied = (flux_x - before) + (flux_y - prev_y(flux_y)) + (flux_z - prev_z(flux_z))
                if turn == 0:
                    u = here * inv
                    r = here - applied * inv
                else:
                    u = here
                    r = nres[x + 3] - applied
                if step is not None:
                    weight = row_mask * step[1]
                    weight = weight if side(x) is None else weight * side(x)
                    new = step[0] * u + weight * r
                    nupd[x + 3] = new
                    nres[x + 3] = r
                    if 0 <= x < 9:
                        node_sum[x] = u + new if turn == 0 else node_sum[x] + new
                else:
                    planes.append(r)
                    if x % 2 == 1:
                        total = planes[x - 1] + 0.5 * planes[x]
                        if x > 1:
                            total = total + 0.5 * planes[x - 2]
                        red[x // 2, 8:40] = total[0:32]
                        red[x // 2, 0:8] = total[40:48] * keep_lo
                    if x == 7:
                        red[4, 8:40] = 0.5 * r[0:32]
                        red[4, 0:8] = 0.5 * r[40:48] * keep_lo
            before = flux_x
            here = after

    thin = [red[x, pl.ds(8, 16, stride=2)] + 0.5 * (red[x, pl.ds(9, 16, stride=2)] + red[x, pl.ds(7, 16, stride=2)])
            for x in range(5)]
    wide = jnp.concatenate(
        [jnp.concatenate([p[0:8] for p in thin], axis=0), jnp.concatenate([p[8:16] for p in thin], axis=0)], axis=1)
    coarse = dot(wide, rest_z)
    for x in range(5):
        cf_main[9 + x] = coarse[8 * x:8 * x + 8]
    cf_distant, cf_close = spread(cf_main, cf_pack, cf_got, cf_far, (x3_send, x3_recv), 9, 5)
    for copy in cf_distant + cf_close:
        copy.start()
    for copy in cs_distant + cs_close:
        copy.wait()

    far_low, low_block, own_block, high_block, far_high = received(cs_got, cs_far, 2)
    halo = far_low[:3] + low_block + own_block + high_block + far_high
    for x in range(19):
        s_one[x] = cs_main[x] * cm_one[0, x]
        s_two[x] = halo[x] * cm_one[1, x]

    def lanes3(n):
        return lax.broadcasted_iota(jnp.int32, (n, 8, 128), 2)

    def coarse_both_y(one, two, ahead=True):
        turn_one, turn_two = roll(one, 64, 2), roll(two, 64, 2)
        pick = lanes3(one.shape[0]) < 64
        mixed, other = jnp.where(pick, turn_one, turn_two), jnp.where(pick, turn_two, turn_one)
        rows = lax.broadcasted_iota(jnp.int32, one.shape, 1)
        behind = (roll(jnp.where(rows == 7, other, one), 1, 1), roll(jnp.where(rows == 7, mixed, two), 1, 1))
        if not ahead:
            return None, behind
        return (roll(jnp.where(rows == 0, mixed, one), -1, 1), roll(jnp.where(rows == 0, other, two), -1, 1)), behind

    def coarse_next_z(f):
        return jnp.where(lanes3(f.shape[0]) % 64 == 63, 0.0, roll(f, -1, 2))

    def coarse_prev_z(f):
        return jnp.where(lanes3(f.shape[0]) % 64 == 0, 0.0, roll(f, 1, 2))

    _, (back_one, back_two) = coarse_both_y(s_one[...], s_two[...], False)
    s_back[0, 0], s_back[0, 1] = back_one, back_two
    s_back[1, 0], s_back[1, 1] = coarse_prev_z(s_one[...]), coarse_prev_z(s_two[...])

    for copy in cf_distant + cf_close:
        copy.wait()

    far_low, low_block, own_block, high_block, far_high = received(cf_got, cf_far, 3)
    halo = far_low + low_block + own_block + high_block + far_high
    where_plane = [0, 1, 2, 4, 5, 6, 7, 9, 10, 11, 12, 14, 15, 16, 17, 19, 20, 21, 22]
    extra = {-4: (3, gx > 1), 0: (8, gx > 0), 4: (13, None), 8: (18, None)}
    for x in range(-7, 12):
        one, two = cf_main[where_plane[x + 7]], halo[where_plane[x + 7]]
        if x in extra:
            spot, valid = extra[x]
            add_one, add_two = cf_main[spot], halo[spot]
            if valid is not None:
                add_one, add_two = add_one * f32(valid), add_two * f32(valid)
            one, two = one + add_one, two + add_two
        g_one[x + 7] = one * cm_one[0, x + 7]
        g_two[x + 7] = two * cm_one[1, x + 7]

    inv, steps = coefficients(96.0, 100.0, 8)
    f_one, f_two = g_one[...], g_two[...]
    r_one = r_two = None
    answer = None
    low = -7
    for turn, (c_old, c_res) in enumerate(steps):
        n = f_one.shape[0]
        sg_one, sg_two = s_one[low + 7:low + 7 + n], s_two[low + 7:low + 7 + n]
        x_one = sg_one[:-1] * (f_one[1:] - f_one[:-1])
        x_two = sg_two[:-1] * (f_two[1:] - f_two[:-1])
        mid_one, mid_two = f_one[1:-1], f_two[1:-1]
        inner = slice(low + 8, low + 6 + n)
        ahead_y, behind_y = coarse_both_y(mid_one, mid_two)
        results = []
        for k, (f, x_flux, s) in enumerate(((mid_one, x_one, sg_one[1:-1]), (mid_two, x_two, sg_two[1:-1]))):
            ahead = s * ((ahead_y[k] - f) + (coarse_next_z(f) - f))
            behind = s_back[0, k, inner] * (behind_y[k] - f) + s_back[1, k, inner] * (roll(f, 1, 2) - f)
            results.append((x_flux[1:] - x_flux[:-1]) + (ahead + behind))
        low += 1
        if turn == 0:
            r_one, r_two = mid_one - results[0] * inv, mid_two - results[1] * inv
            mid_one, mid_two = mid_one * inv, mid_two * inv
            answer = [mid_one[6:11], mid_two[6:11]]
        else:
            r_one, r_two = r_one[1:-1] - results[0], r_two[1:-1] - results[1]
        n -= 2
        f_one = c_old * mid_one + c_res * (cm_one[0, low + 7:low + 7 + n] * r_one)
        f_two = c_old * mid_two + c_res * (cm_one[1, low + 7:low + 7 + n] * r_two)
        answer = [answer[0] + f_one[-low:5 - low], answer[1] + f_two[-low:5 - low]]

    coarse_k = lax.broadcasted_iota(jnp.int32, (128, 256), 0)
    fine_k = lax.broadcasted_iota(jnp.int32, (128, 256), 1)
    same = coarse_k // 64 == fine_k // 128
    apart = (fine_k % 128) - 2 * (coarse_k % 64)
    grow = jnp.where(same, jnp.where(apart == 0, 1.0, jnp.where(jnp.abs(apart) == 1, 0.5, 0.0)), 0.0)
    body = dot(answer[0].reshape(40, 128), grow)
    edge = dot(answer[1].reshape(40, 128), grow[:, 0:128])
    for x in range(5):
        fine[x, 0:8] = body[8 * x:8 * x + 8, 0:128]
        fine[x, 8:16] = body[8 * x:8 * x + 8, 128:256]
        fine[x, 16:24] = edge[8 * x:8 * x + 8]

    own, nxt = None, None
    half_rows = []
    for x in range(5):
        a, b = fine[x, 0:16], fine[x, 1:17]
        red[x, pl.ds(0, 16, stride=2)] = a
        red[x, pl.ds(1, 16, stride=2)] = 0.5 * (a + b)
        red[x, 32:40] = fine[x, 16:24]
    for x in range(9):
        value = red[x // 2] if x % 2 == 0 else 0.5 * (red[x // 2] + red[x // 2 + 1])
        node_sum[x, 0:40] = node_sum[x, 0:40] + value
    keep_next = [keep_hi, keep_right]
    for x in range(8):
        here = node_sum[x, 0:32]
        after = node_sum[x + 1, 0:32]
        if x == 7:
            after = after * keep_right
        shifted = roll(node_sum[x], -1, 0)[0:32]
        last = (row[0:32] == 31) & last_y
        shifted = jnp.where(last, 0.0, shifted)
        out[0, x] = acc[0, x, 0:32] + (after - here)
        out[1, x] = acc[1, x, 0:32] + (shifted - here)
        out[2, x] = acc[2, x, 0:32] + (jnp.where(lane_end[0:32], 0.0, roll(here, -1, 1)) - here)


def solution(mesh):
    nx, ny = mesh.shape["gx"], mesh.shape["gy"]
    f32 = jnp.float32
    dma = pltpu.SemaphoreType.DMA

    def shards(right_side, classes, table):
        return pl.pallas_call(
            functools.partial(kernel, nx, ny),
            out_shape=jax.ShapeDtypeStruct(right_side.shape, f32),
            in_specs=[pl.BlockSpec(memory_space=pltpu.HBM)] * 3,
            out_specs=pl.BlockSpec(memory_space=pltpu.VMEM),
            scratch_shapes=[
                pltpu.VMEM((3, 14, ROWS, 128), f32),
                pltpu.VMEM((8, 32, 128), jnp.int32),
                pltpu.VMEM((16, ROWS, 128), f32),
                pltpu.VMEM((3, 14, ROWS, 128), f32),
                pltpu.VMEM((3, 14, ROWS, 128), f32),
                pltpu.VMEM((8, ROWS, 128), f32),
                pltpu.VMEM((3, 14, ROWS, 128), f32),
                pltpu.VMEM((3, 8, ROWS, 128), f32),
                pltpu.VMEM((8, 2, 8, 128), f32),
                pltpu.VMEM((9, 2, 8, 128), f32),
                pltpu.VMEM((15, 2, 8, 128), f32),
                pltpu.VMEM((16, 2, 8, 128), f32),
                pltpu.VMEM((18, ROWS, 128), f32),
                pltpu.VMEM((9, ROWS, 128), f32),
                pltpu.VMEM((5, 40, 128), f32),
                pltpu.VMEM((19, 8, 128), f32),
                pltpu.VMEM((2, 5, 8, 128), f32),
                pltpu.VMEM((3, 2, 2, 8, 128), f32),
                pltpu.VMEM((2, 2, 8, 128), f32),
                pltpu.VMEM((23, 8, 128), f32),
                pltpu.VMEM((2, 5, 8, 128), f32),
                pltpu.VMEM((3, 2, 3, 8, 128), f32),
                pltpu.VMEM((2, 2, 8, 128), f32),
                pltpu.SMEM((16,), f32),
                pltpu.VMEM((2, 19, 8, 128), f32),
                pltpu.VMEM((19, 8, 128), f32),
                pltpu.VMEM((19, 8, 128), f32),
                pltpu.VMEM((19, 8, 128), f32),
                pltpu.VMEM((19, 8, 128), f32),
                pltpu.VMEM((2, 2, 19, 8, 128), f32),
                pltpu.VMEM((5, 24, 128), f32),
                dma((3,)), dma((12,)), dma((12,)), dma((2,)), dma((2,)), dma((8,)), dma((8,)),
                dma((14,)), dma((14,)), dma((14,)), dma((14,)),
            ],
            compiler_params=pltpu.CompilerParams(
                collective_id=0, has_side_effects=True, vmem_limit_bytes=40 * 2**20),
            name="cycle",
        )(*(pltpu.with_memory_space_constraint(a, pltpu.HBM) for a in (right_side, classes, table)))

    return jax.shard_map(
        shards,
        mesh=mesh,
        in_specs=(P(None, "gx", "gy", None), P("gx", "gy", None), P()),
        out_specs=P(None, "gx", "gy", None),
        check_vma=False,
    )
```

```python
import functools

import jax
import jax.numpy as jnp
from jax import lax
from jax.experimental import pallas as pl
from jax.experimental.pallas import tpu as pltpu
from jax.sharding import PartitionSpec as P

MESH = pl.DeviceIdType.MESH
ROWS = 48


def coefficients(top, ratio, count):
    low = top / ratio
    center = 0.5 * (top + low)
    radius = 0.5 * (top - low)
    sharp = center / radius
    rho = 1.0 / sharp
    steps = []
    for _ in range(1, count):
        rho_next = 1.0 / (2.0 * sharp - rho)
        steps.append((rho_next * rho, 2.0 * rho_next / radius))
        rho = rho_next
    return 1.0 / center, steps


def roll(value, shift, axis):
    return pltpu.roll(value, shift % value.shape[axis], axis)


def kernel(nx, ny, rhs, classes, table, out, base, kinds, sig, upd, upd_next, drop, res, acc,
           pack_dn, pack_up, got_dn, got_up, turn_pack, turn_got, nod, node_sum, red, cs_main, cs_pack, cs_got, cs_far,
           cf_main, cf_pack, cf_got, cf_far, values_in, cm_one, g_one, g_two, s_one, s_two, s_back, fine,
           sem_in, send, recv, far_send, far_recv, x2_send, x2_recv, cs_send, cs_recv, x3_send, x3_recv):
    gx, gy = lax.axis_index("gx"), lax.axis_index("gy")
    first_x, last_x, first_y, last_y = gx == 0, gx == nx - 1, gy == 0, gy == ny - 1

    def at(dx, dy):
        return (lax.rem(gx + dx + nx, nx), lax.rem(gy + dy + ny, ny))

    near = [(1, 1), (1, -1), (-1, 1), (-1, -1), (1, 0), (-1, 0), (0, 1), (0, -1)]

    def remote(source, target, sems, index, where):
        return pltpu.make_async_remote_copy(
            src_ref=source, dst_ref=target, send_sem=sems[0].at[index], recv_sem=sems[1].at[index],
            device_id=at(*where), device_id_type=MESH)

    barrier = pltpu.get_barrier_semaphore()
    for where in near:
        pl.semaphore_signal(barrier, inc=1, device_id=at(*where), device_id_type=MESH)
    loads = [
        pltpu.make_async_copy(table, values_in, sem_in.at[2]),
        pltpu.make_async_copy(classes, kinds, sem_in.at[1]),
        pltpu.make_async_copy(rhs, base.at[:, 3:11, 0:32], sem_in.at[0]),
    ]
    for copy in loads:
        copy.start()

    pl.semaphore_wait(barrier, len(near))
    x1 = (send, recv)
    first = [
        remote(rhs.at[1:3, 0:3], base.at[1:3, 11:14, 0:32], x1, 1, (-1, 0)),
        remote(rhs.at[1:3, 5:8], base.at[1:3, 0:3, 0:32], x1, 0, (1, 0)),
        remote(rhs.at[0:1, 0:2], base.at[0:1, 11:13, 0:32], x1, 10, (-1, 0)),
        remote(rhs.at[0:1, 5:8], base.at[0:1, 0:3, 0:32], x1, 11, (1, 0)),
    ]
    for copy in first:
        copy.start()
    for copy in loads:
        copy.wait()

    values = [values_in[k] for k in range(16)]
    for x in range(8):
        code = kinds[x]
        level = values
        for bit in range(4):
            flag = (code & (1 << bit)) != 0
            level = [jnp.where(flag, level[2 * i + 1], level[2 * i]) for i in range(len(level) // 2)]
        sig[x + 4, 0:32] = level[0]

    sub = lax.broadcasted_iota(jnp.int32, (8, 128), 0)
    lower = sub < 4
    for x in range(8):
        ux, uy, uz = (base[c, x + 3, 0:8] for c in range(3))
        sg = sig[x + 4, 0:8]
        pack_dn[x, 0] = jnp.where(lower, ux, roll(uy, 4, 0))
        pack_dn[x, 1] = jnp.where(lower, uz, roll(sg, 4, 0))
        ux, uy, uz = (base[c, x + 3, 24:32] for c in range(3))
        sg = sig[x + 4, 24:32]
        pack_up[x, 0] = jnp.where(lower, roll(uy, 4, 0), ux)
        pack_up[x, 1] = jnp.where(lower, roll(sg, 4, 0), uz)
    for x in range(8):
        pack_up[8, 0, x:x + 1] = sig[x + 4, 27:28]
    pack_up[8, 1] = jnp.zeros((8, 128), jnp.float32)

    second = [
        remote(pack_dn.at[0:2], got_dn.at[12:14], x1, 2, (-1, -1)),
        remote(pack_up.at[0:3], got_up.at[13:16], x1, 3, (-1, 1)),
        remote(pack_dn.at[5:8], got_dn.at[9:12], x1, 4, (1, -1)),
        remote(pack_up.at[4:8], got_up.at[9:13], x1, 5, (1, 1)),
        remote(pack_dn, got_dn.at[0:8], x1, 6, (0, -1)),
        remote(pack_up, got_up.at[0:9], x1, 7, (0, 1)),
        remote(sig.at[10:12, 0:32], sig.at[2:4, 0:32], x1, 8, (1, 0)),
        remote(sig.at[4:6, 0:32], sig.at[12:14, 0:32], x1, 9, (-1, 0)),
    ]
    for copy in second[4:6] + second[0:4] + second[6:8]:
        copy.start()
    far = (far_send, far_recv)
    later = [
        remote(sig.at[8:10, 0:32], sig.at[0:2, 0:32], far, 0, (1, 0)),
        remote(sig.at[6:7, 0:32], sig.at[14:15, 0:32], far, 1, (-1, 0)),
    ]

    lane = lax.broadcasted_iota(jnp.int32, (ROWS, 128), 1)
    row = lax.broadcasted_iota(jnp.int32, (ROWS, 128), 0)
    lane_end, lane_start = lane == 127, lane == 0
    f32 = lambda flag: flag.astype(jnp.float32)
    keep_hi, keep_lo = 1.0 - f32(last_y), 1.0 - f32(first_y)
    row_mask = jnp.where(row < 32, 1.0, jnp.where(row < 40, keep_hi, keep_lo))
    row_zero = (row[0:8] == 0) & first_y

    def next_z(f):
        return jnp.where(lane_end, 0.0, roll(f, -1, 1))

    def prev_z(f):
        return jnp.where(lane_start, 0.0, roll(f, 1, 1))

    def next_y(f):
        return roll(f, -1, 0)

    def prev_y(f):
        return roll(f, 1, 0)

    def prev_y_inside(f):
        moved = roll(f, 1, 0)
        return jnp.concatenate([jnp.where(row_zero, 0.0, moved[0:8]), moved[8:]], axis=0)

    fine_z = lax.broadcasted_iota(jnp.int32, (256, 128), 0)
    packed_z = lax.broadcasted_iota(jnp.int32, (256, 128), 1)
    half = fine_z // 128 == packed_z // 64
    apart = (fine_z % 128) - 2 * (packed_z % 64)
    mean_z = jnp.where(half & ((apart == 0) | (apart == 1)), 0.125, 0.0)
    rest_z = jnp.where(half, jnp.where(apart == 0, 1.0, jnp.where(jnp.abs(apart) == 1, 0.5, 0.0)), 0.0)

    def dot(value, weights):
        weights = weights.astype(jnp.bfloat16)
        total = None
        for _ in range(3):
            part = value.astype(jnp.bfloat16)
            value = value - part.astype(jnp.float32)
            product = jnp.dot(part, weights, preferred_element_type=jnp.float32)
            total = product if total is None else total + product
        return total

    for x in range(4):
        red[x, 8:40] = sig[2 * x + 4, 0:32] + sig[2 * x + 5, 0:32]
    pairs = [red[x, pl.ds(8, 16, stride=2)] + red[x, pl.ds(9, 16, stride=2)] for x in range(4)]
    wide = jnp.concatenate(
        [jnp.concatenate([p[0:8] for p in pairs], axis=0), jnp.concatenate([p[8:16] for p in pairs], axis=0)], axis=1)
    coarse = 2.0 * dot(wide, mean_z)
    for x in range(4):
        cs_main[7 + x] = coarse[8 * x:8 * x + 8]

    plane_x = lax.broadcasted_iota(jnp.int32, (19, 8, 128), 0) - 7 + 4 * gx
    plane_ok = (plane_x >= 0) & (plane_x < 4 * nx)
    left3 = lax.broadcasted_iota(jnp.int32, (19, 8, 128), 2) < 64
    cm_one[0] = jnp.where(plane_ok, 1.0, 0.0)
    cm_one[1] = jnp.where(plane_ok, jnp.where(left3, keep_hi, keep_lo), 0.0)

    left = lax.broadcasted_iota(jnp.int32, (8, 128), 1) < 64

    def flip(tile):
        return roll(tile, 64, 1)

    def halves(a, b):
        if b is None:
            return a, flip(a)
        return jnp.where(left, a, flip(b)), jnp.where(left, flip(a), b)

    def unhalve(dn, up):
        return jnp.where(left, dn, flip(up)), jnp.where(left, flip(dn), up)

    def spread(main, pack, got, far_got, sems, own, count):
        tiles = [main[own + i] for i in range(count)] + [None]
        pairs = [halves(tiles[0], tiles[1]), halves(tiles[2], tiles[3])]
        odd = [halves(tiles[1], tiles[2]), halves(tiles[3], tiles[4])]
        if count == 5:
            pairs.append(halves(tiles[4], None))
        number = len(pairs)
        for i, (dn, up) in enumerate(pairs):
            pack[0, i] = dn
            pack[1, i] = up
        for i, (one, two) in enumerate((odd, pairs[:2])):
            pack[0, 3 + i] = jnp.where(lower, one[0], roll(two[0], 4, 0))
            pack[1, 3 + i] = jnp.where(lower, roll(one[1], 4, 0), two[1])
        block = main.at[own:own + count]
        size, end = count - 1, own + 2 * count
        reach = 4 if count == 5 else 3
        distant = [
            remote(main.at[own + 1:own + count], main.at[0:size], sems, 0, (2, 0)),
            remote(main.at[own:own + reach], main.at[end:end + reach], sems, 1, (-2, 0)),
        ]
        for i, dx in enumerate((2, -2)):
            for j, dy in enumerate((-1, 1)):
                distant.append(remote(pack.at[j, 3 + i], far_got.at[i, j], sems, 2 + 2 * i + j, (dx, dy)))
        close = []
        for i, dx in enumerate((1, -1, 0)):
            for j, dy in enumerate((-1, 1)):
                close.append(remote(pack.at[j, 0:number], got.at[i, j, 0:number], sems, 6 + 2 * i + j, (dx, dy)))
        close.append(remote(block, main.at[own - count:own], sems, 12, (1, 0)))
        close.append(remote(block, main.at[own + count:own + 2 * count], sems, 13, (-1, 0)))
        return distant, close

    def received(got, far_got, number):
        planes = []
        for spot in (0, 2, 1):
            block = []
            for i in range(number):
                block += list(unhalve(got[spot, 0, i], got[spot, 1, i]))
            planes.append(block[:5] if number == 3 else block)
        sides = []
        for i in range(2):
            dn, up = far_got[i, 0], far_got[i, 1]
            sides.append(list(unhalve(dn, roll(up, 4, 0))) + list(unhalve(roll(dn, 4, 0), up)))
        return sides[0], planes[0], planes[1], planes[2], sides[1]

    cs_distant, cs_close = spread(cs_main, cs_pack, cs_got, cs_far, (cs_send, cs_recv), 7, 4)

    def spot_dn(x):
        return x if 0 <= x < 8 else (12 + x if x < 0 else 4 + x)

    def spot_up(x):
        return x if 0 <= x < 8 else (13 + x if x < 0 else 5 + x)

    zero_tile = jnp.zeros((8, 128), jnp.float32)

    def unpack(planes):
        for x in planes:
            if x == 10:
                for c in range(3):
                    base[c, x + 3, 32:40] = zero_tile
                sig[x + 4, 32:40] = zero_tile
            elif x > -4:
                a, b = got_dn[spot_dn(x), 0], got_dn[spot_dn(x), 1]
                base[0, x + 3, 32:40] = a * keep_hi
                base[1, x + 3, 32:40] = roll(a, 4, 0) * keep_hi
                base[2, x + 3, 32:40] = b * keep_hi
                sig[x + 4, 32:40] = roll(b, 4, 0) * keep_hi
            else:
                sig[x + 4, 32:40] = zero_tile
            a, b = got_up[spot_up(x), 0], got_up[spot_up(x), 1]
            if x > -4:
                base[0, x + 3, 40:48] = a * keep_lo
                base[1, x + 3, 40:48] = roll(a, 4, 0) * keep_lo
                base[2, x + 3, 40:48] = b * keep_lo
            sg = roll(b, 4, 0)
            if 0 <= x < 8:
                sg = jnp.where(sub == 3, got_up[8, 0, x:x + 1], sg)
            sig[x + 4, 40:48] = sg * keep_lo

    keep_left, keep_right = 1.0 - f32(first_x), 1.0 - f32(last_x)

    def side(x):
        return keep_left if x < 0 else (keep_right if x > 7 else None)

    inv, edge_steps = coefficients(20.0, 30.0, 4)

    def edge_turn(turn, lo, hi):
        c_old, c_res = edge_steps[turn]
        source, target = ((base, upd), (upd, upd_next), (upd_next, None))[turn]
        shift = 3 if turn == 0 else 2
        scaled = row_mask * c_res
        before = None
        here = [source[c, lo - 1 + shift] for c in range(3)]
        for x in range(lo - 1, hi + 1):
            after = [None if (c == 0 and x == hi) else source[c, x + 1 + shift] for c in range(3)]
            ux, uy, uz = here
            cy = (next_z(ux) - ux) - (after[2] - uz)
            cz = (after[1] - uy) - (next_y(ux) - ux)
            if x == -1:
                cy, cz = cy * keep_left, cz * keep_left
            if x >= lo:
                cx = (next_y(uz) - uz) - (next_z(uy) - uy)
                sg = sig[x + 4]
                applied = [
                    (prev_y_inside(cz) - cz) - (prev_z(cy) - cy) + sg * ux,
                    (prev_z(cx) - cx) - (before[1] - cz) + sg * uy,
                    (before[0] - cy) - (prev_y_inside(cx) - cx) + sg * uz,
                ]
                weight = scaled if side(x) is None else scaled * side(x)
                rest = []
                for c in range(3):
                    if turn == 0:
                        u = here[c] * inv
                        r = here[c] - applied[c] * inv
                    else:
                        u = here[c]
                        r = res[c, x + 2] - applied[c]
                    new = c_old * u + weight * r
                    if turn < 2:
                        target[c, x + 2] = new
                        res[c, x + 2] = r
                        if 0 <= x < 8:
                            acc[c, x] = u + new if turn == 0 else acc[c, x] + new
                    else:
                        answer = acc[c, x] + new
                        acc[c, x] = answer
                        rest.append(base[c, x + 3] - sg * answer)
                if turn == 2:
                    rx, ry, rz = rest
                    total = (ry - prev_y(ry)) + (rz - prev_z(rz)) + rx
                    if x not in (0, lo) or x == 5:
                        total = total - drop[x - 1]
                    nod[x + 5, 0:32] = total[0:32]
                    drop[x] = rx
            before = (cy, cz)
            here = after

    for copy in (second[4], second[5]):
        copy.wait()
    unpack(range(8))
    edge_turn(0, 1, 6)
    edge_turn(1, 2, 5)
    edge_turn(2, 3, 4)

    for copy in (first[0], first[2], second[0], second[1], second[7]):
        copy.wait()
    unpack(range(8, 11))

    @pl.when(last_x)
    def _():
        base[:, 11:14] = jnp.zeros((3, 3, ROWS, 128), jnp.float32)
        sig[12:14] = jnp.zeros((2, ROWS, 128), jnp.float32)

    edge_turn(0, 7, 9)
    edge_turn(1, 6, 8)
    edge_turn(2, 5, 7)
    nod[13, 0:32] = drop[7, 0:32]

    x2 = (x2_send, x2_recv)
    swap = [
        remote(nod.at[9:14, 0:32], nod.at[0:5, 0:32], x2, 0, (1, 0)),
        remote(nod.at[5:9, 0:32], nod.at[14:18, 0:32], x2, 1, (-1, 0)),
        remote(turn_pack.at[0:2], turn_got.at[0:2], x2, 2, (1, 1)),
        remote(turn_pack.at[2:4], turn_got.at[2:4], x2, 3, (1, -1)),
        remote(turn_pack.at[4:6], turn_got.at[4:6], x2, 4, (-1, 1)),
        remote(turn_pack.at[6], turn_got.at[6], x2, 5, (-1, -1)),
        remote(nod.at[5:14, 24:32], nod.at[5:14, 40:48], x2, 6, (0, 1)),
        remote(nod.at[5:14, 0:8], nod.at[5:14, 32:40], x2, 7, (0, -1)),
    ]
    up = [nod[9 + i, 24:32] for i in range(5)]
    turn_pack[0] = jnp.where(sub >= 3, up[4], jnp.where(sub == 0, roll(up[0], 1, 0), roll(up[1], 3, 0)))
    turn_pack[1] = jnp.where(lower, roll(up[2], 4, 0), up[3])
    dn = [nod[9 + i, 0:8] for i in range(5)]
    turn_pack[2] = jnp.where(lower, dn[4], roll(dn[3], 4, 0))
    turn_pack[3] = jnp.where(lower, dn[2], roll(dn[1], 4, 0))
    for copy in (swap[2], swap[3], swap[0]):
        copy.start()

    for copy in (first[1], first[3], second[2], second[3], second[6]):
        copy.wait()
    for copy in later + cs_close:
        copy.start()
    unpack(range(-4, 0))

    @pl.when(first_x)
    def _():
        base[:, 0:3] = jnp.zeros((3, 3, ROWS, 128), jnp.float32)
        sig[2:4] = jnp.zeros((2, ROWS, 128), jnp.float32)

    edge_turn(0, -2, 0)
    edge_turn(1, -1, 1)
    edge_turn(2, 0, 2)
    nod[8, 0:32] = nod[8, 0:32] - drop[2, 0:32]
    up = [nod[5 + i, 24:32] for i in range(4)]
    turn_pack[4] = jnp.where(lower, roll(up[1], 4, 0), up[0])
    turn_pack[5] = jnp.where(lower, roll(up[3], 4, 0), up[2])
    dn = [nod[5 + i, 0:8] for i in range(3)]
    turn_pack[6] = jnp.where(lower, dn[0], jnp.where(sub < 6, roll(dn[1], 4, 0), roll(dn[2], 6, 0)))
    for copy in (swap[4], swap[5], swap[1], swap[6], swap[7]):
        copy.start()
    for copy in cs_distant:
        copy.start()

    for copy in later + swap:
        copy.wait()
    one, two = turn_got[0], turn_got[1]
    for spot, tile in enumerate((roll(one, 7, 0), roll(one, 5, 0), roll(two, 4, 0), two, one)):
        nod[spot, 40:48] = tile
    one, two = turn_got[2], turn_got[3]
    for spot, tile in enumerate((zero_tile, roll(two, 4, 0), two, roll(one, 4, 0), one)):
        nod[spot, 32:40] = tile
    one, two = turn_got[4], turn_got[5]
    for spot, tile in enumerate((one, roll(one, 4, 0), two, roll(two, 4, 0))):
        nod[14 + spot, 40:48] = tile
    one = turn_got[6]
    for spot, tile in enumerate((one, roll(one, 4, 0), roll(one, 2, 0), zero_tile)):
        nod[14 + spot, 32:40] = tile

    @pl.when(first_x)
    def _():
        nod[0:5] = jnp.zeros((5, ROWS, 128), jnp.float32)
        sig[0:2] = jnp.zeros((2, ROWS, 128), jnp.float32)

    @pl.when(last_x)
    def _():
        sig[14:15] = jnp.zeros((1, ROWS, 128), jnp.float32)

    nod[5] = nod[5] - nod[4]
    nod[14] = nod[14] - nod[13]

    @pl.when(last_x)
    def _():
        nod[14:18] = jnp.zeros((4, ROWS, 128), jnp.float32)

    @pl.when(first_y)
    def _():
        nod[:, 40:48] = jnp.zeros((18, 8, 128), jnp.float32)

    @pl.when(last_y)
    def _():
        nod[:, 32:40] = jnp.zeros((18, 8, 128), jnp.float32)

    def place(x):
        return x + 4 if x < 0 else (x + 5 if x < 8 else x + 6)

    inv, steps = coefficients(48.0, 30.0, 4)
    steps = steps + [None]
    nupd, nres = upd.at[0], res.at[0]
    planes = []
    for turn, step in enumerate(steps):
        lo, hi = -3 + turn, 10 - turn
        get = (lambda x: nod[place(x)]) if turn == 0 else (lambda x: nupd[x + 3])
        here = get(lo - 1)
        before = None
        for x in range(lo - 1, hi + 1):
            after = get(x + 1)
            sg = sig[x + 4]
            flux_x = sg * (after - here)
            if x >= lo:
                flux_y = sg * (next_y(here) - here)
                flux_z = sg * (next_z(here) - here)
                applied = (flux_x - before) + (flux_y - prev_y(flux_y)) + (flux_z - prev_z(flux_z))
                if turn == 0:
                    u = here * inv
                    r = here - applied * inv
                else:
                    u = here
                    r = nres[x + 3] - applied
                if step is not None:
                    weight = row_mask * step[1]
                    weight = weight if side(x) is None else weight * side(x)
                    new = step[0] * u + weight * r
                    nupd[x + 3] = new
                    nres[x + 3] = r
                    if 0 <= x < 9:
                        node_sum[x] = u + new if turn == 0 else node_sum[x] + new
                else:
                    planes.append(r)
                    if x % 2 == 1:
                        total = planes[x - 1] + 0.5 * planes[x]
                        if x > 1:
                            total = total + 0.5 * planes[x - 2]
                        red[x // 2, 8:40] = total[0:32]
                        red[x // 2, 0:8] = total[40:48] * keep_lo
                    if x == 7:
                        red[4, 8:40] = 0.5 * r[0:32]
                        red[4, 0:8] = 0.5 * r[40:48] * keep_lo
            before = flux_x
            here = after

    thin = [red[x, pl.ds(8, 16, stride=2)] + 0.5 * (red[x, pl.ds(9, 16, stride=2)] + red[x, pl.ds(7, 16, stride=2)])
            for x in range(5)]
    wide = jnp.concatenate(
        [jnp.concatenate([p[0:8] for p in thin], axis=0), jnp.concatenate([p[8:16] for p in thin], axis=0)], axis=1)
    coarse = dot(wide, rest_z)
    for x in range(5):
        cf_main[9 + x] = coarse[8 * x:8 * x + 8]
    cf_distant, cf_close = spread(cf_main, cf_pack, cf_got, cf_far, (x3_send, x3_recv), 9, 5)
    for copy in cf_distant + cf_close:
        copy.start()
    for copy in cs_distant + cs_close:
        copy.wait()

    far_low, low_block, own_block, high_block, far_high = received(cs_got, cs_far, 2)
    halo = far_low[:3] + low_block + own_block + high_block + far_high
    for x in range(18):
        s_one[x] = cs_main[x] * cm_one[0, x]
        s_two[x] = halo[x] * cm_one[1, x]
    s_one[18], s_two[18] = zero_tile, zero_tile

    def lanes3(n):
        return lax.broadcasted_iota(jnp.int32, (n, 8, 128), 2)

    def coarse_both_y(one, two, ahead=True):
        turn_one, turn_two = roll(one, 64, 2), roll(two, 64, 2)
        pick = lanes3(one.shape[0]) < 64
        mixed, other = jnp.where(pick, turn_one, turn_two), jnp.where(pick, turn_two, turn_one)
        rows = lax.broadcasted_iota(jnp.int32, one.shape, 1)
        behind = (roll(jnp.where(rows == 7, other, one), 1, 1), roll(jnp.where(rows == 7, mixed, two), 1, 1))
        if not ahead:
            return None, behind
        return (roll(jnp.where(rows == 0, mixed, one), -1, 1), roll(jnp.where(rows == 0, other, two), -1, 1)), behind

    def coarse_next_z(f):
        return jnp.where(lanes3(f.shape[0]) % 64 == 63, 0.0, roll(f, -1, 2))

    def coarse_prev_z(f):
        return jnp.where(lanes3(f.shape[0]) % 64 == 0, 0.0, roll(f, 1, 2))

    _, (back_one, back_two) = coarse_both_y(s_one[...], s_two[...], False)
    s_back[0, 0], s_back[0, 1] = back_one, back_two
    s_back[1, 0], s_back[1, 1] = coarse_prev_z(s_one[...]), coarse_prev_z(s_two[...])

    for copy in cf_distant + cf_close:
        copy.wait()

    far_low, low_block, own_block, high_block, far_high = received(cf_got, cf_far, 3)
    halo = far_low + low_block + own_block + high_block + far_high
    where_plane = [0, 1, 2, 4, 5, 6, 7, 9, 10, 11, 12, 14, 15, 16, 17, 19, 20, 21, 22]
    extra = {-4: (3, gx > 1), 0: (8, gx > 0), 4: (13, None), 8: (18, None)}
    for x in range(-7, 12):
        one, two = cf_main[where_plane[x + 7]], halo[where_plane[x + 7]]
        if x in extra:
            spot, valid = extra[x]
            add_one, add_two = cf_main[spot], halo[spot]
            if valid is not None:
                add_one, add_two = add_one * f32(valid), add_two * f32(valid)
            one, two = one + add_one, two + add_two
        g_one[x + 7] = one * cm_one[0, x + 7]
        g_two[x + 7] = two * cm_one[1, x + 7]

    inv, steps = coefficients(96.0, 100.0, 8)
    f_one, f_two = g_one[...], g_two[...]
    r_one = r_two = None
    answer = None
    low = -7
    for turn, (c_old, c_res) in enumerate(steps):
        n = f_one.shape[0]
        sg_one, sg_two = s_one[low + 7:low + 7 + n], s_two[low + 7:low + 7 + n]
        x_one = sg_one[:-1] * (f_one[1:] - f_one[:-1])
        x_two = sg_two[:-1] * (f_two[1:] - f_two[:-1])
        mid_one, mid_two = f_one[1:-1], f_two[1:-1]
        inner = slice(low + 8, low + 6 + n)
        ahead_y, behind_y = coarse_both_y(mid_one, mid_two)
        results = []
        for k, (f, x_flux, s) in enumerate(((mid_one, x_one, sg_one[1:-1]), (mid_two, x_two, sg_two[1:-1]))):
            ahead = s * ((ahead_y[k] - f) + (coarse_next_z(f) - f))
            behind = s_back[0, k, inner] * (behind_y[k] - f) + s_back[1, k, inner] * (roll(f, 1, 2) - f)
            results.append((x_flux[1:] - x_flux[:-1]) + (ahead + behind))
        low += 1
        if turn == 0:
            r_one, r_two = mid_one - results[0] * inv, mid_two - results[1] * inv
            mid_one, mid_two = mid_one * inv, mid_two * inv
            answer = [mid_one[6:11], mid_two[6:11]]
        else:
            r_one, r_two = r_one[1:-1] - results[0], r_two[1:-1] - results[1]
        n -= 2
        f_one = c_old * mid_one + c_res * (cm_one[0, low + 7:low + 7 + n] * r_one)
        f_two = c_old * mid_two + c_res * (cm_one[1, low + 7:low + 7 + n] * r_two)
        answer = [answer[0] + f_one[-low:5 - low], answer[1] + f_two[-low:5 - low]]

    coarse_k = lax.broadcasted_iota(jnp.int32, (128, 256), 0)
    fine_k = lax.broadcasted_iota(jnp.int32, (128, 256), 1)
    same = coarse_k // 64 == fine_k // 128
    apart = (fine_k % 128) - 2 * (coarse_k % 64)
    grow = jnp.where(same, jnp.where(apart == 0, 1.0, jnp.where(jnp.abs(apart) == 1, 0.5, 0.0)), 0.0)
    body = dot(answer[0].reshape(40, 128), grow)
    edge = dot(answer[1].reshape(40, 128), grow[:, 0:128])
    for x in range(5):
        fine[x, 0:8] = body[8 * x:8 * x + 8, 0:128]
        fine[x, 8:16] = body[8 * x:8 * x + 8, 128:256]
        fine[x, 16:24] = edge[8 * x:8 * x + 8]

    own, nxt = None, None
    half_rows = []
    for x in range(5):
        a, b = fine[x, 0:16], fine[x, 1:17]
        red[x, pl.ds(0, 16, stride=2)] = a
        red[x, pl.ds(1, 16, stride=2)] = 0.5 * (a + b)
        red[x, 32:40] = fine[x, 16:24]
    for x in range(9):
        value = red[x // 2] if x % 2 == 0 else 0.5 * (red[x // 2] + red[x // 2 + 1])
        node_sum[x, 0:40] = node_sum[x, 0:40] + value
    keep_next = [keep_hi, keep_right]
    for x in range(8):
        here = node_sum[x, 0:32]
        after = node_sum[x + 1, 0:32]
        if x == 7:
            after = after * keep_right
        shifted = roll(node_sum[x], -1, 0)[0:32]
        last = (row[0:32] == 31) & last_y
        shifted = jnp.where(last, 0.0, shifted)
        out[0, x] = acc[0, x, 0:32] + (after - here)
        out[1, x] = acc[1, x, 0:32] + (shifted - here)
        out[2, x] = acc[2, x, 0:32] + (jnp.where(lane_end[0:32], 0.0, roll(here, -1, 1)) - here)


def solution(mesh):
    nx, ny = mesh.shape["gx"], mesh.shape["gy"]
    f32 = jnp.float32
    dma = pltpu.SemaphoreType.DMA

    def shards(right_side, classes, table):
        return pl.pallas_call(
            functools.partial(kernel, nx, ny),
            out_shape=jax.ShapeDtypeStruct(right_side.shape, f32),
            in_specs=[pl.BlockSpec(memory_space=pltpu.HBM)] * 3,
            out_specs=pl.BlockSpec(memory_space=pltpu.VMEM),
            scratch_shapes=[
                pltpu.VMEM((3, 14, ROWS, 128), f32),
                pltpu.VMEM((8, 32, 128), jnp.int32),
                pltpu.VMEM((16, ROWS, 128), f32),
                pltpu.VMEM((3, 14, ROWS, 128), f32),
                pltpu.VMEM((3, 14, ROWS, 128), f32),
                pltpu.VMEM((8, ROWS, 128), f32),
                pltpu.VMEM((3, 14, ROWS, 128), f32),
                pltpu.VMEM((3, 8, ROWS, 128), f32),
                pltpu.VMEM((8, 2, 8, 128), f32),
                pltpu.VMEM((9, 2, 8, 128), f32),
                pltpu.VMEM((15, 2, 8, 128), f32),
                pltpu.VMEM((16, 2, 8, 128), f32),
                pltpu.VMEM((7, 8, 128), f32),
                pltpu.VMEM((7, 8, 128), f32),
                pltpu.VMEM((18, ROWS, 128), f32),
                pltpu.VMEM((9, ROWS, 128), f32),
                pltpu.VMEM((5, 40, 128), f32),
                pltpu.VMEM((19, 8, 128), f32),
                pltpu.VMEM((2, 5, 8, 128), f32),
                pltpu.VMEM((3, 2, 2, 8, 128), f32),
                pltpu.VMEM((2, 2, 8, 128), f32),
                pltpu.VMEM((23, 8, 128), f32),
                pltpu.VMEM((2, 5, 8, 128), f32),
                pltpu.VMEM((3, 2, 3, 8, 128), f32),
                pltpu.VMEM((2, 2, 8, 128), f32),
                pltpu.SMEM((16,), f32),
                pltpu.VMEM((2, 19, 8, 128), f32),
                pltpu.VMEM((19, 8, 128), f32),
                pltpu.VMEM((19, 8, 128), f32),
                pltpu.VMEM((19, 8, 128), f32),
                pltpu.VMEM((19, 8, 128), f32),
                pltpu.VMEM((2, 2, 19, 8, 128), f32),
                pltpu.VMEM((5, 24, 128), f32),
                dma((3,)), dma((12,)), dma((12,)), dma((2,)), dma((2,)), dma((8,)), dma((8,)),
                dma((14,)), dma((14,)), dma((14,)), dma((14,)),
            ],
            compiler_params=pltpu.CompilerParams(
                collective_id=0, has_side_effects=True, vmem_limit_bytes=40 * 2**20),
            name="cycle",
        )(*(pltpu.with_memory_space_constraint(a, pltpu.HBM) for a in (right_side, classes, table)))

    return jax.shard_map(
        shards,
        mesh=mesh,
        in_specs=(P(None, "gx", "gy", None), P("gx", "gy", None), P()),
        out_specs=P(None, "gx", "gy", None),
        check_vma=False,
    )
```

```python
import functools

import jax
import jax.numpy as jnp
from jax import lax
from jax.experimental import pallas as pl
from jax.experimental.pallas import tpu as pltpu
from jax.sharding import PartitionSpec as P

MESH = pl.DeviceIdType.MESH
ROWS = 48


def coefficients(top, ratio, count):
    low = top / ratio
    center = 0.5 * (top + low)
    radius = 0.5 * (top - low)
    sharp = center / radius
    rho = 1.0 / sharp
    steps = []
    for _ in range(1, count):
        rho_next = 1.0 / (2.0 * sharp - rho)
        steps.append((rho_next * rho, 2.0 * rho_next / radius))
        rho = rho_next
    return 1.0 / center, steps


def roll(value, shift, axis):
    return pltpu.roll(value, shift % value.shape[axis], axis)


def kernel(nx, ny, rhs, classes, table, out, base, kinds, sig, upd, upd_next, drop, res, acc,
           pack_dn, pack_up, got_dn, got_up, turn_pack, turn_got, nod, node_sum, red, cs_main, cs_pack, cs_got, cs_far,
           cf_main, cf_pack, cf_got, cf_far, values_in, cm_one, g_one, g_two, s_one, s_two, s_back, fine,
           sem_in, send, recv, far_send, far_recv, x2_send, x2_recv, cs_send, cs_recv, x3_send, x3_recv):
    gx, gy = lax.axis_index("gx"), lax.axis_index("gy")
    first_x, last_x, first_y, last_y = gx == 0, gx == nx - 1, gy == 0, gy == ny - 1

    def at(dx, dy):
        return (lax.rem(gx + dx + nx, nx), lax.rem(gy + dy + ny, ny))

    near = [(1, 1), (1, -1), (-1, 1), (-1, -1), (1, 0), (-1, 0), (0, 1), (0, -1)]

    def remote(source, target, sems, index, where):
        return pltpu.make_async_remote_copy(
            src_ref=source, dst_ref=target, send_sem=sems[0].at[index], recv_sem=sems[1].at[index],
            device_id=at(*where), device_id_type=MESH)

    barrier = pltpu.get_barrier_semaphore()
    for where in near:
        pl.semaphore_signal(barrier, inc=1, device_id=at(*where), device_id_type=MESH)
    loads = [
        pltpu.make_async_copy(table, values_in, sem_in.at[2]),
        pltpu.make_async_copy(classes, kinds, sem_in.at[1]),
        pltpu.make_async_copy(rhs, base.at[:, 3:11, 0:32], sem_in.at[0]),
    ]
    for copy in loads:
        copy.start()

    pl.semaphore_wait(barrier, len(near))
    x1 = (send, recv)
    first = [
        remote(rhs.at[1:3, 0:3], base.at[1:3, 11:14, 0:32], x1, 1, (-1, 0)),
        remote(rhs.at[1:3, 5:8], base.at[1:3, 0:3, 0:32], x1, 0, (1, 0)),
        remote(rhs.at[0:1, 0:2], base.at[0:1, 11:13, 0:32], x1, 10, (-1, 0)),
        remote(rhs.at[0:1, 5:8], base.at[0:1, 0:3, 0:32], x1, 11, (1, 0)),
    ]
    for copy in first:
        copy.start()
    for copy in loads:
        copy.wait()

    values = [values_in[k] for k in range(16)]
    for x in range(8):
        code = kinds[x]
        level = values
        for bit in range(4):
            flag = (code & (1 << bit)) != 0
            level = [jnp.where(flag, level[2 * i + 1], level[2 * i]) for i in range(len(level) // 2)]
        sig[x + 4, 0:32] = level[0]

    sub = lax.broadcasted_iota(jnp.int32, (8, 128), 0)
    lower = sub < 4
    for x in range(8):
        ux, uy, uz = (base[c, x + 3, 0:8] for c in range(3))
        sg = sig[x + 4, 0:8]
        pack_dn[x, 0] = jnp.where(lower, ux, roll(uy, 4, 0))
        pack_dn[x, 1] = jnp.where(lower, uz, roll(sg, 4, 0))
        ux, uy, uz = (base[c, x + 3, 24:32] for c in range(3))
        sg = sig[x + 4, 24:32]
        pack_up[x, 0] = jnp.where(lower, roll(uy, 4, 0), ux)
        pack_up[x, 1] = jnp.where(lower, roll(sg, 4, 0), uz)
    for x in range(8):
        pack_up[8, 0, x:x + 1] = sig[x + 4, 27:28]
    pack_up[8, 1] = jnp.zeros((8, 128), jnp.float32)

    second = [
        remote(pack_dn.at[0:2], got_dn.at[12:14], x1, 2, (-1, -1)),
        remote(pack_up.at[0:3], got_up.at[13:16], x1, 3, (-1, 1)),
        remote(pack_dn.at[5:8], got_dn.at[9:12], x1, 4, (1, -1)),
        remote(pack_up.at[4:8], got_up.at[9:13], x1, 5, (1, 1)),
        remote(pack_dn, got_dn.at[0:8], x1, 6, (0, -1)),
        remote(pack_up, got_up.at[0:9], x1, 7, (0, 1)),
        remote(sig.at[10:12, 0:32], sig.at[2:4, 0:32], x1, 8, (1, 0)),
        remote(sig.at[4:6, 0:32], sig.at[12:14, 0:32], x1, 9, (-1, 0)),
    ]
    for copy in second[0:4] + second[6:8] + second[4:6]:
        copy.start()
    far = (far_send, far_recv)
    later = [
        remote(sig.at[8:10, 0:32], sig.at[0:2, 0:32], far, 0, (1, 0)),
        remote(sig.at[6:7, 0:32], sig.at[14:15, 0:32], far, 1, (-1, 0)),
    ]

    lane = lax.broadcasted_iota(jnp.int32, (ROWS, 128), 1)
    row = lax.broadcasted_iota(jnp.int32, (ROWS, 128), 0)
    lane_end, lane_start = lane == 127, lane == 0
    f32 = lambda flag: flag.astype(jnp.float32)
    keep_hi, keep_lo = 1.0 - f32(last_y), 1.0 - f32(first_y)
    row_mask = jnp.where(row < 32, 1.0, jnp.where(row < 40, keep_hi, keep_lo))
    row_zero = (row[0:8] == 0) & first_y

    def next_z(f):
        return jnp.where(lane_end, 0.0, roll(f, -1, 1))

    def prev_z(f):
        return jnp.where(lane_start, 0.0, roll(f, 1, 1))

    def next_y(f):
        return roll(f, -1, 0)

    def prev_y(f):
        return roll(f, 1, 0)

    def prev_y_inside(f):
        moved = roll(f, 1, 0)
        return jnp.concatenate([jnp.where(row_zero, 0.0, moved[0:8]), moved[8:]], axis=0)

    fine_z = lax.broadcasted_iota(jnp.int32, (256, 128), 0)
    packed_z = lax.broadcasted_iota(jnp.int32, (256, 128), 1)
    half = fine_z // 128 == packed_z // 64
    apart = (fine_z % 128) - 2 * (packed_z % 64)
    mean_z = jnp.where(half & ((apart == 0) | (apart == 1)), 0.125, 0.0)
    rest_z = jnp.where(half, jnp.where(apart == 0, 1.0, jnp.where(jnp.abs(apart) == 1, 0.5, 0.0)), 0.0)

    def dot(value, weights):
        weights = weights.astype(jnp.bfloat16)
        total = None
        for _ in range(3):
            part = value.astype(jnp.bfloat16)
            value = value - part.astype(jnp.float32)
            product = jnp.dot(part, weights, preferred_element_type=jnp.float32)
            total = product if total is None else total + product
        return total

    for x in range(4):
        red[x, 8:40] = sig[2 * x + 4, 0:32] + sig[2 * x + 5, 0:32]
    pairs = [red[x, pl.ds(8, 16, stride=2)] + red[x, pl.ds(9, 16, stride=2)] for x in range(4)]
    wide = jnp.concatenate(
        [jnp.concatenate([p[0:8] for p in pairs], axis=0), jnp.concatenate([p[8:16] for p in pairs], axis=0)], axis=1)
    coarse = 2.0 * dot(wide, mean_z)
    for x in range(4):
        cs_main[7 + x] = coarse[8 * x:8 * x + 8]

    plane_x = lax.broadcasted_iota(jnp.int32, (19, 8, 128), 0) - 7 + 4 * gx
    plane_ok = (plane_x >= 0) & (plane_x < 4 * nx)
    left3 = lax.broadcasted_iota(jnp.int32, (19, 8, 128), 2) < 64
    cm_one[0] = jnp.where(plane_ok, 1.0, 0.0)
    cm_one[1] = jnp.where(plane_ok, jnp.where(left3, keep_hi, keep_lo), 0.0)

    left = lax.broadcasted_iota(jnp.int32, (8, 128), 1) < 64

    def flip(tile):
        return roll(tile, 64, 1)

    def halves(a, b):
        if b is None:
            return a, flip(a)
        return jnp.where(left, a, flip(b)), jnp.where(left, flip(a), b)

    def unhalve(dn, up):
        return jnp.where(left, dn, flip(up)), jnp.where(left, flip(dn), up)

    def spread(main, pack, got, far_got, sems, own, count):
        tiles = [main[own + i] for i in range(count)] + [None]
        pairs = [halves(tiles[0], tiles[1]), halves(tiles[2], tiles[3])]
        odd = [halves(tiles[1], tiles[2]), halves(tiles[3], tiles[4])]
        if count == 5:
            pairs.append(halves(tiles[4], None))
        number = len(pairs)
        for i, (dn, up) in enumerate(pairs):
            pack[0, i] = dn
            pack[1, i] = up
        for i, (one, two) in enumerate((odd, pairs[:2])):
            pack[0, 3 + i] = jnp.where(lower, one[0], roll(two[0], 4, 0))
            pack[1, 3 + i] = jnp.where(lower, roll(one[1], 4, 0), two[1])
        block = main.at[own:own + count]
        size, end = count - 1, own + 2 * count
        reach = 4 if count == 5 else 3
        distant = [
            remote(main.at[own + 1:own + count], main.at[0:size], sems, 0, (2, 0)),
            remote(main.at[own:own + reach], main.at[end:end + reach], sems, 1, (-2, 0)),
        ]
        for i, dx in enumerate((2, -2)):
            for j, dy in enumerate((-1, 1)):
                distant.append(remote(pack.at[j, 3 + i], far_got.at[i, j], sems, 2 + 2 * i + j, (dx, dy)))
        close = []
        for i, dx in enumerate((1, -1, 0)):
            for j, dy in enumerate((-1, 1)):
                close.append(remote(pack.at[j, 0:number], got.at[i, j, 0:number], sems, 6 + 2 * i + j, (dx, dy)))
        close.append(remote(block, main.at[own - count:own], sems, 12, (1, 0)))
        close.append(remote(block, main.at[own + count:own + 2 * count], sems, 13, (-1, 0)))
        return distant, close

    def received(got, far_got, number):
        planes = []
        for spot in (0, 2, 1):
            block = []
            for i in range(number):
                block += list(unhalve(got[spot, 0, i], got[spot, 1, i]))
            planes.append(block[:5] if number == 3 else block)
        sides = []
        for i in range(2):
            dn, up = far_got[i, 0], far_got[i, 1]
            sides.append(list(unhalve(dn, roll(up, 4, 0))) + list(unhalve(roll(dn, 4, 0), up)))
        return sides[0], planes[0], planes[1], planes[2], sides[1]

    cs_distant, cs_close = spread(cs_main, cs_pack, cs_got, cs_far, (cs_send, cs_recv), 7, 4)

    def spot_dn(x):
        return x if 0 <= x < 8 else (12 + x if x < 0 else 4 + x)

    def spot_up(x):
        return x if 0 <= x < 8 else (13 + x if x < 0 else 5 + x)

    zero_tile = jnp.zeros((8, 128), jnp.float32)

    def unpack(planes):
        for x in planes:
            if x == 10:
                for c in range(3):
                    base[c, x + 3, 32:40] = zero_tile
                sig[x + 4, 32:40] = zero_tile
            elif x > -4:
                a, b = got_dn[spot_dn(x), 0], got_dn[spot_dn(x), 1]
                base[0, x + 3, 32:40] = a * keep_hi
                base[1, x + 3, 32:40] = roll(a, 4, 0) * keep_hi
                base[2, x + 3, 32:40] = b * keep_hi
                sig[x + 4, 32:40] = roll(b, 4, 0) * keep_hi
            else:
                sig[x + 4, 32:40] = zero_tile
            a, b = got_up[spot_up(x), 0], got_up[spot_up(x), 1]
            if x > -4:
                base[0, x + 3, 40:48] = a * keep_lo
                base[1, x + 3, 40:48] = roll(a, 4, 0) * keep_lo
                base[2, x + 3, 40:48] = b * keep_lo
            sg = roll(b, 4, 0)
            if 0 <= x < 8:
                sg = jnp.where(sub == 3, got_up[8, 0, x:x + 1], sg)
            sig[x + 4, 40:48] = sg * keep_lo

    keep_left, keep_right = 1.0 - f32(first_x), 1.0 - f32(last_x)

    def side(x):
        return keep_left if x < 0 else (keep_right if x > 7 else None)

    inv, edge_steps = coefficients(20.0, 30.0, 4)

    def edge_turn(turn, lo, hi):
        c_old, c_res = edge_steps[turn]
        source, target = ((base, upd), (upd, upd_next), (upd_next, None))[turn]
        shift = 3 if turn == 0 else 2
        scaled = row_mask * c_res
        before = None
        here = [source[c, lo - 1 + shift] for c in range(3)]
        for x in range(lo - 1, hi + 1):
            after = [None if (c == 0 and x == hi) else source[c, x + 1 + shift] for c in range(3)]
            ux, uy, uz = here
            cy = (next_z(ux) - ux) - (after[2] - uz)
            cz = (after[1] - uy) - (next_y(ux) - ux)
            if x == -1:
                cy, cz = cy * keep_left, cz * keep_left
            if x >= lo:
                cx = (next_y(uz) - uz) - (next_z(uy) - uy)
                sg = sig[x + 4]
                applied = [
                    (prev_y_inside(cz) - cz) - (prev_z(cy) - cy) + sg * ux,
                    (prev_z(cx) - cx) - (before[1] - cz) + sg * uy,
                    (before[0] - cy) - (prev_y_inside(cx) - cx) + sg * uz,
                ]
                weight = scaled if side(x) is None else scaled * side(x)
                rest = []
                for c in range(3):
                    if turn == 0:
                        u = here[c] * inv
                        r = here[c] - applied[c] * inv
                    else:
                        u = here[c]
                        r = res[c, x + 2] - applied[c]
                    new = c_old * u + weight * r
                    if turn < 2:
                        target[c, x + 2] = new
                        res[c, x + 2] = r
                        if 0 <= x < 8:
                            acc[c, x] = u + new if turn == 0 else acc[c, x] + new
                    else:
                        answer = acc[c, x] + new
                        acc[c, x] = answer
                        rest.append(base[c, x + 3] - sg * answer)
                if turn == 2:
                    rx, ry, rz = rest
                    total = (ry - prev_y(ry)) + (rz - prev_z(rz)) + rx
                    if x not in (0, lo) or x == 5:
                        total = total - drop[x - 1]
                    nod[x + 5, 0:32] = total[0:32]
                    drop[x] = rx
            before = (cy, cz)
            here = after

    for copy in (second[4], second[5]):
        copy.wait()
    unpack(range(8))
    edge_turn(0, 1, 6)
    edge_turn(1, 2, 5)
    edge_turn(2, 3, 4)

    for copy in (first[0], first[2], second[0], second[1], second[7]):
        copy.wait()
    unpack(range(8, 11))
    for copy in later:
        copy.start()

    @pl.when(last_x)
    def _():
        base[:, 11:14] = jnp.zeros((3, 3, ROWS, 128), jnp.float32)
        sig[12:14] = jnp.zeros((2, ROWS, 128), jnp.float32)

    edge_turn(0, 7, 9)
    edge_turn(1, 6, 8)
    edge_turn(2, 5, 7)
    nod[13, 0:32] = drop[7, 0:32]

    x2 = (x2_send, x2_recv)
    swap = [
        remote(nod.at[9:14, 0:32], nod.at[0:5, 0:32], x2, 0, (1, 0)),
        remote(nod.at[5:9, 0:32], nod.at[14:18, 0:32], x2, 1, (-1, 0)),
        remote(turn_pack.at[0:2], turn_got.at[0:2], x2, 2, (1, 1)),
        remote(turn_pack.at[2:4], turn_got.at[2:4], x2, 3, (1, -1)),
        remote(turn_pack.at[4:6], turn_got.at[4:6], x2, 4, (-1, 1)),
        remote(turn_pack.at[6], turn_got.at[6], x2, 5, (-1, -1)),
        remote(nod.at[5:14, 24:32], nod.at[5:14, 40:48], x2, 6, (0, 1)),
        remote(nod.at[5:14, 0:8], nod.at[5:14, 32:40], x2, 7, (0, -1)),
    ]
    up = [nod[9 + i, 24:32] for i in range(5)]
    turn_pack[0] = jnp.where(sub >= 3, up[4], jnp.where(sub == 0, roll(up[0], 1, 0), roll(up[1], 3, 0)))
    turn_pack[1] = jnp.where(lower, roll(up[2], 4, 0), up[3])
    dn = [nod[9 + i, 0:8] for i in range(5)]
    turn_pack[2] = jnp.where(lower, dn[4], roll(dn[3], 4, 0))
    turn_pack[3] = jnp.where(lower, dn[2], roll(dn[1], 4, 0))
    for copy in (swap[2], swap[3], swap[0]):
        copy.start()

    for copy in (first[1], first[3], second[2], second[3], second[6]):
        copy.wait()
    unpack(range(-4, 0))

    @pl.when(first_x)
    def _():
        base[:, 0:3] = jnp.zeros((3, 3, ROWS, 128), jnp.float32)
        sig[2:4] = jnp.zeros((2, ROWS, 128), jnp.float32)

    edge_turn(0, -2, 0)
    edge_turn(1, -1, 1)
    edge_turn(2, 0, 2)
    nod[8, 0:32] = nod[8, 0:32] - drop[2, 0:32]
    up = [nod[5 + i, 24:32] for i in range(4)]
    turn_pack[4] = jnp.where(lower, roll(up[1], 4, 0), up[0])
    turn_pack[5] = jnp.where(lower, roll(up[3], 4, 0), up[2])
    dn = [nod[5 + i, 0:8] for i in range(3)]
    turn_pack[6] = jnp.where(lower, dn[0], jnp.where(sub < 6, roll(dn[1], 4, 0), roll(dn[2], 6, 0)))
    for copy in (swap[4], swap[5], swap[1], swap[6], swap[7]):
        copy.start()
    for copy in cs_close + cs_distant:
        copy.start()

    for copy in later + swap:
        copy.wait()
    one, two = turn_got[0], turn_got[1]
    for spot, tile in enumerate((roll(one, 7, 0), roll(one, 5, 0), roll(two, 4, 0), two, one)):
        nod[spot, 40:48] = tile
    one, two = turn_got[2], turn_got[3]
    for spot, tile in enumerate((zero_tile, roll(two, 4, 0), two, roll(one, 4, 0), one)):
        nod[spot, 32:40] = tile
    one, two = turn_got[4], turn_got[5]
    for spot, tile in enumerate((one, roll(one, 4, 0), two, roll(two, 4, 0))):
        nod[14 + spot, 40:48] = tile
    one = turn_got[6]
    for spot, tile in enumerate((one, roll(one, 4, 0), roll(one, 2, 0), zero_tile)):
        nod[14 + spot, 32:40] = tile

    @pl.when(first_x)
    def _():
        nod[0:5] = jnp.zeros((5, ROWS, 128), jnp.float32)
        sig[0:2] = jnp.zeros((2, ROWS, 128), jnp.float32)

    @pl.when(last_x)
    def _():
        sig[14:15] = jnp.zeros((1, ROWS, 128), jnp.float32)

    nod[5] = nod[5] - nod[4]
    nod[14] = nod[14] - nod[13]

    @pl.when(last_x)
    def _():
        nod[14:18] = jnp.zeros((4, ROWS, 128), jnp.float32)

    @pl.when(first_y)
    def _():
        nod[:, 40:48] = jnp.zeros((18, 8, 128), jnp.float32)

    @pl.when(last_y)
    def _():
        nod[:, 32:40] = jnp.zeros((18, 8, 128), jnp.float32)

    def place(x):
        return x + 4 if x < 0 else (x + 5 if x < 8 else x + 6)

    inv, steps = coefficients(48.0, 30.0, 4)
    steps = steps + [None]
    nupd, nres = upd.at[0], res.at[0]
    planes = []
    for turn, step in enumerate(steps):
        lo, hi = -3 + turn, 10 - turn
        get = (lambda x: nod[place(x)]) if turn == 0 else (lambda x: nupd[x + 3])
        here = get(lo - 1)
        before = None
        for x in range(lo - 1, hi + 1):
            after = get(x + 1)
            sg = sig[x + 4]
            flux_x = sg * (after - here)
            if x >= lo:
                flux_y = sg * (next_y(here) - here)
                flux_z = sg * (next_z(here) - here)
                applied = (flux_x - before) + (flux_y - prev_y(flux_y)) + (flux_z - prev_z(flux_z))
                if turn == 0:
                    u = here * inv
                    r = here - applied * inv
                else:
                    u = here
                    r = nres[x + 3] - applied
                if step is not None:
                    weight = row_mask * step[1]
                    weight = weight if side(x) is None else weight * side(x)
                    new = step[0] * u + weight * r
                    nupd[x + 3] = new
                    nres[x + 3] = r
                    if 0 <= x < 9:
                        node_sum[x] = u + new if turn == 0 else node_sum[x] + new
                else:
                    planes.append(r)
                    if x % 2 == 1:
                        total = planes[x - 1] + 0.5 * planes[x]
                        if x > 1:
                            total = total + 0.5 * planes[x - 2]
                        red[x // 2, 8:40] = total[0:32]
                        red[x // 2, 0:8] = total[40:48] * keep_lo
                    if x == 7:
                        red[4, 8:40] = 0.5 * r[0:32]
                        red[4, 0:8] = 0.5 * r[40:48] * keep_lo
            before = flux_x
            here = after

    thin = [red[x, pl.ds(8, 16, stride=2)] + 0.5 * (red[x, pl.ds(9, 16, stride=2)] + red[x, pl.ds(7, 16, stride=2)])
            for x in range(5)]
    wide = jnp.concatenate(
        [jnp.concatenate([p[0:8] for p in thin], axis=0), jnp.concatenate([p[8:16] for p in thin], axis=0)], axis=1)
    coarse = dot(wide, rest_z)
    for x in range(5):
        cf_main[9 + x] = coarse[8 * x:8 * x + 8]
    cf_distant, cf_close = spread(cf_main, cf_pack, cf_got, cf_far, (x3_send, x3_recv), 9, 5)
    for copy in cf_distant + cf_close:
        copy.start()
    for copy in cs_distant + cs_close:
        copy.wait()

    far_low, low_block, own_block, high_block, far_high = received(cs_got, cs_far, 2)
    halo = far_low[:3] + low_block + own_block + high_block + far_high
    for x in range(18):
        s_one[x] = cs_main[x] * cm_one[0, x]
        s_two[x] = halo[x] * cm_one[1, x]
    s_one[18], s_two[18] = zero_tile, zero_tile

    def lanes3(n):
        return lax.broadcasted_iota(jnp.int32, (n, 8, 128), 2)

    def coarse_both_y(one, two, ahead=True):
        turn_one, turn_two = roll(one, 64, 2), roll(two, 64, 2)
        pick = lanes3(one.shape[0]) < 64
        mixed, other = jnp.where(pick, turn_one, turn_two), jnp.where(pick, turn_two, turn_one)
        rows = lax.broadcasted_iota(jnp.int32, one.shape, 1)
        behind = (roll(jnp.where(rows == 7, other, one), 1, 1), roll(jnp.where(rows == 7, mixed, two), 1, 1))
        if not ahead:
            return None, behind
        return (roll(jnp.where(rows == 0, mixed, one), -1, 1), roll(jnp.where(rows == 0, other, two), -1, 1)), behind

    def coarse_next_z(f):
        return jnp.where(lanes3(f.shape[0]) % 64 == 63, 0.0, roll(f, -1, 2))

    def coarse_prev_z(f):
        return jnp.where(lanes3(f.shape[0]) % 64 == 0, 0.0, roll(f, 1, 2))

    _, (back_one, back_two) = coarse_both_y(s_one[...], s_two[...], False)
    s_back[0, 0], s_back[0, 1] = back_one, back_two
    s_back[1, 0], s_back[1, 1] = coarse_prev_z(s_one[...]), coarse_prev_z(s_two[...])

    for copy in cf_distant + cf_close:
        copy.wait()

    far_low, low_block, own_block, high_block, far_high = received(cf_got, cf_far, 3)
    halo = far_low + low_block + own_block + high_block + far_high
    where_plane = [0, 1, 2, 4, 5, 6, 7, 9, 10, 11, 12, 14, 15, 16, 17, 19, 20, 21, 22]
    extra = {-4: (3, gx > 1), 0: (8, gx > 0), 4: (13, None), 8: (18, None)}
    for x in range(-7, 12):
        one, two = cf_main[where_plane[x + 7]], halo[where_plane[x + 7]]
        if x in extra:
            spot, valid = extra[x]
            add_one, add_two = cf_main[spot], halo[spot]
            if valid is not None:
                add_one, add_two = add_one * f32(valid), add_two * f32(valid)
            one, two = one + add_one, two + add_two
        g_one[x + 7] = one * cm_one[0, x + 7]
        g_two[x + 7] = two * cm_one[1, x + 7]

    inv, steps = coefficients(96.0, 100.0, 8)
    f_one, f_two = g_one[...], g_two[...]
    r_one = r_two = None
    answer = None
    low = -7
    for turn, (c_old, c_res) in enumerate(steps):
        n = f_one.shape[0]
        sg_one, sg_two = s_one[low + 7:low + 7 + n], s_two[low + 7:low + 7 + n]
        x_one = sg_one[:-1] * (f_one[1:] - f_one[:-1])
        x_two = sg_two[:-1] * (f_two[1:] - f_two[:-1])
        mid_one, mid_two = f_one[1:-1], f_two[1:-1]
        inner = slice(low + 8, low + 6 + n)
        ahead_y, behind_y = coarse_both_y(mid_one, mid_two)
        results = []
        for k, (f, x_flux, s) in enumerate(((mid_one, x_one, sg_one[1:-1]), (mid_two, x_two, sg_two[1:-1]))):
            ahead = s * ((ahead_y[k] - f) + (coarse_next_z(f) - f))
            behind = s_back[0, k, inner] * (behind_y[k] - f) + s_back[1, k, inner] * (roll(f, 1, 2) - f)
            results.append((x_flux[1:] - x_flux[:-1]) + (ahead + behind))
        low += 1
        if turn == 0:
            r_one, r_two = mid_one - results[0] * inv, mid_two - results[1] * inv
            mid_one, mid_two = mid_one * inv, mid_two * inv
            answer = [mid_one[6:11], mid_two[6:11]]
        else:
            r_one, r_two = r_one[1:-1] - results[0], r_two[1:-1] - results[1]
        n -= 2
        f_one = c_old * mid_one + c_res * (cm_one[0, low + 7:low + 7 + n] * r_one)
        f_two = c_old * mid_two + c_res * (cm_one[1, low + 7:low + 7 + n] * r_two)
        answer = [answer[0] + f_one[-low:5 - low], answer[1] + f_two[-low:5 - low]]

    coarse_k = lax.broadcasted_iota(jnp.int32, (128, 256), 0)
    fine_k = lax.broadcasted_iota(jnp.int32, (128, 256), 1)
    same = coarse_k // 64 == fine_k // 128
    apart = (fine_k % 128) - 2 * (coarse_k % 64)
    grow = jnp.where(same, jnp.where(apart == 0, 1.0, jnp.where(jnp.abs(apart) == 1, 0.5, 0.0)), 0.0)
    body = dot(answer[0].reshape(40, 128), grow)
    edge = dot(answer[1].reshape(40, 128), grow[:, 0:128])
    for x in range(5):
        fine[x, 0:8] = body[8 * x:8 * x + 8, 0:128]
        fine[x, 8:16] = body[8 * x:8 * x + 8, 128:256]
        fine[x, 16:24] = edge[8 * x:8 * x + 8]

    own, nxt = None, None
    half_rows = []
    for x in range(5):
        a, b = fine[x, 0:16], fine[x, 1:17]
        red[x, pl.ds(0, 16, stride=2)] = a
        red[x, pl.ds(1, 16, stride=2)] = 0.5 * (a + b)
        red[x, 32:40] = fine[x, 16:24]
    for x in range(9):
        value = red[x // 2] if x % 2 == 0 else 0.5 * (red[x // 2] + red[x // 2 + 1])
        node_sum[x, 0:40] = node_sum[x, 0:40] + value
    keep_next = [keep_hi, keep_right]
    for x in range(8):
        here = node_sum[x, 0:32]
        after = node_sum[x + 1, 0:32]
        if x == 7:
            after = after * keep_right
        shifted = roll(node_sum[x], -1, 0)[0:32]
        last = (row[0:32] == 31) & last_y
        shifted = jnp.where(last, 0.0, shifted)
        out[0, x] = acc[0, x, 0:32] + (after - here)
        out[1, x] = acc[1, x, 0:32] + (shifted - here)
        out[2, x] = acc[2, x, 0:32] + (jnp.where(lane_end[0:32], 0.0, roll(here, -1, 1)) - here)


def solution(mesh):
    nx, ny = mesh.shape["gx"], mesh.shape["gy"]
    f32 = jnp.float32
    dma = pltpu.SemaphoreType.DMA

    def shards(right_side, classes, table):
        return pl.pallas_call(
            functools.partial(kernel, nx, ny),
            out_shape=jax.ShapeDtypeStruct(right_side.shape, f32),
            in_specs=[pl.BlockSpec(memory_space=pltpu.HBM)] * 3,
            out_specs=pl.BlockSpec(memory_space=pltpu.VMEM),
            scratch_shapes=[
                pltpu.VMEM((3, 14, ROWS, 128), f32),
                pltpu.VMEM((8, 32, 128), jnp.int32),
                pltpu.VMEM((16, ROWS, 128), f32),
                pltpu.VMEM((3, 14, ROWS, 128), f32),
                pltpu.VMEM((3, 14, ROWS, 128), f32),
                pltpu.VMEM((8, ROWS, 128), f32),
                pltpu.VMEM((3, 14, ROWS, 128), f32),
                pltpu.VMEM((3, 8, ROWS, 128), f32),
                pltpu.VMEM((8, 2, 8, 128), f32),
                pltpu.VMEM((9, 2, 8, 128), f32),
                pltpu.VMEM((15, 2, 8, 128), f32),
                pltpu.VMEM((16, 2, 8, 128), f32),
                pltpu.VMEM((7, 8, 128), f32),
                pltpu.VMEM((7, 8, 128), f32),
                pltpu.VMEM((18, ROWS, 128), f32),
                pltpu.VMEM((9, ROWS, 128), f32),
                pltpu.VMEM((5, 40, 128), f32),
                pltpu.VMEM((19, 8, 128), f32),
                pltpu.VMEM((2, 5, 8, 128), f32),
                pltpu.VMEM((3, 2, 2, 8, 128), f32),
                pltpu.VMEM((2, 2, 8, 128), f32),
                pltpu.VMEM((23, 8, 128), f32),
                pltpu.VMEM((2, 5, 8, 128), f32),
                pltpu.VMEM((3, 2, 3, 8, 128), f32),
                pltpu.VMEM((2, 2, 8, 128), f32),
                pltpu.SMEM((16,), f32),
                pltpu.VMEM((2, 19, 8, 128), f32),
                pltpu.VMEM((19, 8, 128), f32),
                pltpu.VMEM((19, 8, 128), f32),
                pltpu.VMEM((19, 8, 128), f32),
                pltpu.VMEM((19, 8, 128), f32),
                pltpu.VMEM((2, 2, 19, 8, 128), f32),
                pltpu.VMEM((5, 24, 128), f32),
                dma((3,)), dma((12,)), dma((12,)), dma((2,)), dma((2,)), dma((8,)), dma((8,)),
                dma((14,)), dma((14,)), dma((14,)), dma((14,)),
            ],
            compiler_params=pltpu.CompilerParams(
                collective_id=0, has_side_effects=True, vmem_limit_bytes=40 * 2**20),
            name="cycle",
        )(*(pltpu.with_memory_space_constraint(a, pltpu.HBM) for a in (right_side, classes, table)))

    return jax.shard_map(
        shards,
        mesh=mesh,
        in_specs=(P(None, "gx", "gy", None), P("gx", "gy", None), P()),
        out_specs=P(None, "gx", "gy", None),
        check_vma=False,
    )
```

```python
import functools

import jax
import jax.numpy as jnp
from jax import lax
from jax.experimental import pallas as pl
from jax.experimental.pallas import tpu as pltpu
from jax.sharding import PartitionSpec as P

MESH = pl.DeviceIdType.MESH
ROWS = 48


def coefficients(top, ratio, count):
    low = top / ratio
    center = 0.5 * (top + low)
    radius = 0.5 * (top - low)
    sharp = center / radius
    rho = 1.0 / sharp
    steps = []
    for _ in range(1, count):
        rho_next = 1.0 / (2.0 * sharp - rho)
        steps.append((rho_next * rho, 2.0 * rho_next / radius))
        rho = rho_next
    return 1.0 / center, steps


def roll(value, shift, axis):
    return pltpu.roll(value, shift % value.shape[axis], axis)


def kernel(nx, ny, rhs, classes, table, out, base, kinds, sig, upd, upd_next, drop, res, acc,
           pack_dn, pack_up, got_dn, got_up, turn_pack, turn_got, nod, node_sum, red, cs_main, cs_pack, cs_got, cs_far,
           cf_main, cf_pack, cf_got, cf_far, values_in, cm_one, g_one, g_two, s_one, s_two, s_back, fine,
           sem_in, send, recv, far_send, far_recv, x2_send, x2_recv, cs_send, cs_recv, x3_send, x3_recv):
    gx, gy = lax.axis_index("gx"), lax.axis_index("gy")
    first_x, last_x, first_y, last_y = gx == 0, gx == nx - 1, gy == 0, gy == ny - 1

    def at(dx, dy):
        return (lax.rem(gx + dx + nx, nx), lax.rem(gy + dy + ny, ny))

    near = [(1, 1), (1, -1), (-1, 1), (-1, -1), (1, 0), (-1, 0), (0, 1), (0, -1)]

    def remote(source, target, sems, index, where):
        return pltpu.make_async_remote_copy(
            src_ref=source, dst_ref=target, send_sem=sems[0].at[index], recv_sem=sems[1].at[index],
            device_id=at(*where), device_id_type=MESH)

    barrier = pltpu.get_barrier_semaphore()
    for where in near:
        pl.semaphore_signal(barrier, inc=1, device_id=at(*where), device_id_type=MESH)
    loads = [
        pltpu.make_async_copy(table, values_in, sem_in.at[2]),
        pltpu.make_async_copy(classes, kinds, sem_in.at[1]),
        pltpu.make_async_copy(rhs, base.at[:, 3:11, 0:32], sem_in.at[0]),
    ]
    for copy in loads:
        copy.start()

    pl.semaphore_wait(barrier, len(near))
    x1 = (send, recv)
    first = [
        remote(rhs.at[1:3, 0:3], base.at[1:3, 11:14, 0:32], x1, 1, (-1, 0)),
        remote(rhs.at[1:3, 5:8], base.at[1:3, 0:3, 0:32], x1, 0, (1, 0)),
        remote(rhs.at[0:1, 0:2], base.at[0:1, 11:13, 0:32], x1, 10, (-1, 0)),
        remote(rhs.at[0:1, 5:8], base.at[0:1, 0:3, 0:32], x1, 11, (1, 0)),
    ]
    for copy in first:
        copy.start()
    for copy in loads:
        copy.wait()

    values = [values_in[k] for k in range(16)]
    for x in range(8):
        code = kinds[x]
        level = values
        for bit in range(4):
            flag = (code & (1 << bit)) != 0
            level = [jnp.where(flag, level[2 * i + 1], level[2 * i]) for i in range(len(level) // 2)]
        sig[x + 4, 0:32] = level[0]

    sub = lax.broadcasted_iota(jnp.int32, (8, 128), 0)
    lower = sub < 4
    for x in range(8):
        ux, uy, uz = (base[c, x + 3, 0:8] for c in range(3))
        sg = sig[x + 4, 0:8]
        pack_dn[x, 0] = jnp.where(lower, ux, roll(uy, 4, 0))
        pack_dn[x, 1] = jnp.where(lower, uz, roll(sg, 4, 0))
        ux, uy, uz = (base[c, x + 3, 24:32] for c in range(3))
        sg = sig[x + 4, 24:32]
        pack_up[x, 0] = jnp.where(lower, roll(uy, 4, 0), ux)
        pack_up[x, 1] = jnp.where(lower, roll(sg, 4, 0), uz)
    for x in range(8):
        pack_up[8, 0, x:x + 1] = sig[x + 4, 27:28]
    pack_up[8, 1] = jnp.zeros((8, 128), jnp.float32)

    second = [
        remote(pack_dn.at[0:2], got_dn.at[12:14], x1, 2, (-1, -1)),
        remote(pack_up.at[0:3], got_up.at[13:16], x1, 3, (-1, 1)),
        remote(pack_dn.at[5:8], got_dn.at[9:12], x1, 4, (1, -1)),
        remote(pack_up.at[4:8], got_up.at[9:13], x1, 5, (1, 1)),
        remote(pack_dn, got_dn.at[0:8], x1, 6, (0, -1)),
        remote(pack_up, got_up.at[0:9], x1, 7, (0, 1)),
        remote(sig.at[10:12, 0:32], sig.at[2:4, 0:32], x1, 8, (1, 0)),
        remote(sig.at[4:6, 0:32], sig.at[12:14, 0:32], x1, 9, (-1, 0)),
    ]
    for copy in second[0:4] + second[6:8] + second[4:6]:
        copy.start()
    far = (far_send, far_recv)
    later = [
        remote(sig.at[8:10, 0:32], sig.at[0:2, 0:32], far, 0, (1, 0)),
        remote(sig.at[6:7, 0:32], sig.at[14:15, 0:32], far, 1, (-1, 0)),
    ]

    lane = lax.broadcasted_iota(jnp.int32, (ROWS, 128), 1)
    row = lax.broadcasted_iota(jnp.int32, (ROWS, 128), 0)
    lane_end, lane_start = lane == 127, lane == 0
    f32 = lambda flag: flag.astype(jnp.float32)
    keep_hi, keep_lo = 1.0 - f32(last_y), 1.0 - f32(first_y)
    row_mask = jnp.where(row < 32, 1.0, jnp.where(row < 40, keep_hi, keep_lo))
    row_zero = (row[0:8] == 0) & first_y

    def next_z(f):
        return jnp.where(lane_end, 0.0, roll(f, -1, 1))

    def prev_z(f):
        return jnp.where(lane_start, 0.0, roll(f, 1, 1))

    def next_y(f):
        return roll(f, -1, 0)

    def prev_y(f):
        return roll(f, 1, 0)

    def prev_y_inside(f):
        moved = roll(f, 1, 0)
        return jnp.concatenate([jnp.where(row_zero, 0.0, moved[0:8]), moved[8:]], axis=0)

    fine_z = lax.broadcasted_iota(jnp.int32, (256, 128), 0)
    packed_z = lax.broadcasted_iota(jnp.int32, (256, 128), 1)
    half = fine_z // 128 == packed_z // 64
    apart = (fine_z % 128) - 2 * (packed_z % 64)
    mean_z = jnp.where(half & ((apart == 0) | (apart == 1)), 0.125, 0.0)
    rest_z = jnp.where(half, jnp.where(apart == 0, 1.0, jnp.where(jnp.abs(apart) == 1, 0.5, 0.0)), 0.0)

    def dot(value, weights):
        weights = weights.astype(jnp.bfloat16)
        total = None
        for _ in range(3):
            part = value.astype(jnp.bfloat16)
            value = value - part.astype(jnp.float32)
            product = jnp.dot(part, weights, preferred_element_type=jnp.float32)
            total = product if total is None else total + product
        return total

    for x in range(4):
        red[x, 8:40] = sig[2 * x + 4, 0:32] + sig[2 * x + 5, 0:32]
    pairs = [red[x, pl.ds(8, 16, stride=2)] + red[x, pl.ds(9, 16, stride=2)] for x in range(4)]
    wide = jnp.concatenate(
        [jnp.concatenate([p[0:8] for p in pairs], axis=0), jnp.concatenate([p[8:16] for p in pairs], axis=0)], axis=1)
    coarse = 2.0 * dot(wide, mean_z)
    for x in range(4):
        cs_main[7 + x] = coarse[8 * x:8 * x + 8]

    plane_x = lax.broadcasted_iota(jnp.int32, (19, 8, 128), 0) - 7 + 4 * gx
    plane_ok = (plane_x >= 0) & (plane_x < 4 * nx)
    left3 = lax.broadcasted_iota(jnp.int32, (19, 8, 128), 2) < 64
    cm_one[0] = jnp.where(plane_ok, 1.0, 0.0)
    cm_one[1] = jnp.where(plane_ok, jnp.where(left3, keep_hi, keep_lo), 0.0)

    left = lax.broadcasted_iota(jnp.int32, (8, 128), 1) < 64

    def flip(tile):
        return roll(tile, 64, 1)

    def halves(a, b):
        if b is None:
            return a, flip(a)
        return jnp.where(left, a, flip(b)), jnp.where(left, flip(a), b)

    def unhalve(dn, up):
        return jnp.where(left, dn, flip(up)), jnp.where(left, flip(dn), up)

    def spread(main, pack, got, far_got, sems, own, count):
        tiles = [main[own + i] for i in range(count)] + [None]
        pairs = [halves(tiles[0], tiles[1]), halves(tiles[2], tiles[3])]
        odd = [halves(tiles[1], tiles[2]), halves(tiles[3], tiles[4])]
        if count == 5:
            pairs.append(halves(tiles[4], None))
        number = len(pairs)
        for i, (dn, up) in enumerate(pairs):
            pack[0, i] = dn
            pack[1, i] = up
        for i, (one, two) in enumerate((odd, pairs[:2])):
            pack[0, 3 + i] = jnp.where(lower, one[0], roll(two[0], 4, 0))
            pack[1, 3 + i] = jnp.where(lower, roll(one[1], 4, 0), two[1])
        block = main.at[own:own + count]
        size, end = count - 1, own + 2 * count
        reach = 4 if count == 5 else 3
        distant = [
            remote(main.at[own + 1:own + count], main.at[0:size], sems, 0, (2, 0)),
            remote(main.at[own:own + reach], main.at[end:end + reach], sems, 1, (-2, 0)),
        ]
        for i, dx in enumerate((2, -2)):
            for j, dy in enumerate((-1, 1)):
                distant.append(remote(pack.at[j, 3 + i], far_got.at[i, j], sems, 2 + 2 * i + j, (dx, dy)))
        close = []
        for i, dx in enumerate((1, -1, 0)):
            for j, dy in enumerate((-1, 1)):
                close.append(remote(pack.at[j, 0:number], got.at[i, j, 0:number], sems, 6 + 2 * i + j, (dx, dy)))
        close.append(remote(block, main.at[own - count:own], sems, 12, (1, 0)))
        close.append(remote(block, main.at[own + count:own + 2 * count], sems, 13, (-1, 0)))
        return distant, close

    def received(got, far_got, number):
        planes = []
        for spot in (0, 2, 1):
            block = []
            for i in range(number):
                block += list(unhalve(got[spot, 0, i], got[spot, 1, i]))
            planes.append(block[:5] if number == 3 else block)
        sides = []
        for i in range(2):
            dn, up = far_got[i, 0], far_got[i, 1]
            sides.append(list(unhalve(dn, roll(up, 4, 0))) + list(unhalve(roll(dn, 4, 0), up)))
        return sides[0], planes[0], planes[1], planes[2], sides[1]

    cs_distant, cs_close = spread(cs_main, cs_pack, cs_got, cs_far, (cs_send, cs_recv), 7, 4)

    def spot_dn(x):
        return x if 0 <= x < 8 else (12 + x if x < 0 else 4 + x)

    def spot_up(x):
        return x if 0 <= x < 8 else (13 + x if x < 0 else 5 + x)

    zero_tile = jnp.zeros((8, 128), jnp.float32)

    def unpack(planes):
        for x in planes:
            if x == 10:
                for c in range(3):
                    base[c, x + 3, 32:40] = zero_tile
                sig[x + 4, 32:40] = zero_tile
            elif x > -4:
                a, b = got_dn[spot_dn(x), 0], got_dn[spot_dn(x), 1]
                base[0, x + 3, 32:40] = a * keep_hi
                base[1, x + 3, 32:40] = roll(a, 4, 0) * keep_hi
                base[2, x + 3, 32:40] = b * keep_hi
                sig[x + 4, 32:40] = roll(b, 4, 0) * keep_hi
            else:
                sig[x + 4, 32:40] = zero_tile
            a, b = got_up[spot_up(x), 0], got_up[spot_up(x), 1]
            if x > -4:
                base[0, x + 3, 40:48] = a * keep_lo
                base[1, x + 3, 40:48] = roll(a, 4, 0) * keep_lo
                base[2, x + 3, 40:48] = b * keep_lo
            sg = roll(b, 4, 0)
            if 0 <= x < 8:
                sg = jnp.where(sub == 3, got_up[8, 0, x:x + 1], sg)
            sig[x + 4, 40:48] = sg * keep_lo

    keep_left, keep_right = 1.0 - f32(first_x), 1.0 - f32(last_x)

    def side(x):
        return keep_left if x < 0 else (keep_right if x > 7 else None)

    inv, edge_steps = coefficients(20.0, 30.0, 4)

    def edge_turn(turn, lo, hi):
        c_old, c_res = edge_steps[turn]
        source, target = ((base, upd), (upd, upd_next), (upd_next, None))[turn]
        shift = 3 if turn == 0 else 2
        scaled = row_mask * c_res
        before = None
        here = [source[c, lo - 1 + shift] for c in range(3)]
        for x in range(lo - 1, hi + 1):
            after = [None if (c == 0 and x == hi) else source[c, x + 1 + shift] for c in range(3)]
            ux, uy, uz = here
            cy = (next_z(ux) - ux) - (after[2] - uz)
            cz = (after[1] - uy) - (next_y(ux) - ux)
            if x == -1:
                cy, cz = cy * keep_left, cz * keep_left
            if x >= lo:
                cx = (next_y(uz) - uz) - (next_z(uy) - uy)
                sg = sig[x + 4]
                applied = [
                    (prev_y_inside(cz) - cz) - (prev_z(cy) - cy) + sg * ux,
                    (prev_z(cx) - cx) - (before[1] - cz) + sg * uy,
                    (before[0] - cy) - (prev_y_inside(cx) - cx) + sg * uz,
                ]
                weight = scaled if side(x) is None else scaled * side(x)
                rest = []
                for c in range(3):
                    if turn == 0:
                        u = here[c] * inv
                        r = here[c] - applied[c] * inv
                    else:
                        u = here[c]
                        r = res[c, x + 2] - applied[c]
                    new = c_old * u + weight * r
                    if turn < 2:
                        target[c, x + 2] = new
                        res[c, x + 2] = r
                        if 0 <= x < 8:
                            acc[c, x] = u + new if turn == 0 else acc[c, x] + new
                    else:
                        answer = acc[c, x] + new
                        acc[c, x] = answer
                        rest.append(base[c, x + 3] - sg * answer)
                if turn == 2:
                    rx, ry, rz = rest
                    total = (ry - prev_y(ry)) + (rz - prev_z(rz)) + rx
                    if x not in (0, lo) or x == 5:
                        total = total - drop[x - 1]
                    nod[x + 5, 0:32] = total[0:32]
                    drop[x] = rx
            before = (cy, cz)
            here = after

    for copy in (second[4], second[5]):
        copy.wait()
    unpack(range(8))
    edge_turn(0, 1, 6)
    edge_turn(1, 2, 5)
    edge_turn(2, 3, 4)

    for copy in (first[0], first[2], second[0], second[1], second[7]):
        copy.wait()
    unpack(range(8, 11))
    for copy in later:
        copy.start()

    @pl.when(last_x)
    def _():
        base[:, 11:14] = jnp.zeros((3, 3, ROWS, 128), jnp.float32)
        sig[12:14] = jnp.zeros((2, ROWS, 128), jnp.float32)

    edge_turn(0, 7, 9)
    edge_turn(1, 6, 8)
    edge_turn(2, 5, 7)
    nod[13, 0:32] = drop[7, 0:32]

    x2 = (x2_send, x2_recv)
    swap = [
        remote(nod.at[9:14, 0:32], nod.at[0:5, 0:32], x2, 0, (1, 0)),
        remote(nod.at[5:9, 0:32], nod.at[14:18, 0:32], x2, 1, (-1, 0)),
        remote(turn_pack.at[0:2], turn_got.at[0:2], x2, 2, (1, 1)),
        remote(turn_pack.at[2:4], turn_got.at[2:4], x2, 3, (1, -1)),
        remote(turn_pack.at[4:6], turn_got.at[4:6], x2, 4, (-1, 1)),
        remote(turn_pack.at[6], turn_got.at[6], x2, 5, (-1, -1)),
        remote(nod.at[5:14, 24:32], nod.at[5:14, 40:48], x2, 6, (0, 1)),
        remote(nod.at[5:14, 0:8], nod.at[5:14, 32:40], x2, 7, (0, -1)),
    ]
    up = [nod[9 + i, 24:32] for i in range(5)]
    turn_pack[0] = jnp.where(sub >= 3, up[4], jnp.where(sub == 0, roll(up[0], 1, 0), roll(up[1], 3, 0)))
    turn_pack[1] = jnp.where(lower, roll(up[2], 4, 0), up[3])
    dn = [nod[9 + i, 0:8] for i in range(5)]
    turn_pack[2] = jnp.where(lower, dn[4], roll(dn[3], 4, 0))
    turn_pack[3] = jnp.where(lower, dn[2], roll(dn[1], 4, 0))
    for copy in (swap[2], swap[3], swap[0]):
        copy.start()

    for copy in (first[1], first[3], second[2], second[3], second[6]):
        copy.wait()
    unpack(range(-4, 0))

    @pl.when(first_x)
    def _():
        base[:, 0:3] = jnp.zeros((3, 3, ROWS, 128), jnp.float32)
        sig[2:4] = jnp.zeros((2, ROWS, 128), jnp.float32)

    edge_turn(0, -2, 0)
    edge_turn(1, -1, 1)
    edge_turn(2, 0, 2)
    nod[8, 0:32] = nod[8, 0:32] - drop[2, 0:32]
    up = [nod[5 + i, 24:32] for i in range(4)]
    turn_pack[4] = jnp.where(lower, roll(up[1], 4, 0), up[0])
    turn_pack[5] = jnp.where(lower, roll(up[3], 4, 0), up[2])
    dn = [nod[5 + i, 0:8] for i in range(3)]
    turn_pack[6] = jnp.where(lower, dn[0], jnp.where(sub < 6, roll(dn[1], 4, 0), roll(dn[2], 6, 0)))
    for copy in (swap[4], swap[5], swap[6], swap[7], swap[1]):
        copy.start()
    for copy in cs_close + cs_distant:
        copy.start()

    for copy in later + swap:
        copy.wait()
    one, two = turn_got[0], turn_got[1]
    for spot, tile in enumerate((roll(one, 7, 0), roll(one, 5, 0), roll(two, 4, 0), two, one)):
        nod[spot, 40:48] = tile
    one, two = turn_got[2], turn_got[3]
    for spot, tile in enumerate((zero_tile, roll(two, 4, 0), two, roll(one, 4, 0), one)):
        nod[spot, 32:40] = tile
    one, two = turn_got[4], turn_got[5]
    for spot, tile in enumerate((one, roll(one, 4, 0), two, roll(two, 4, 0))):
        nod[14 + spot, 40:48] = tile
    one = turn_got[6]
    for spot, tile in enumerate((one, roll(one, 4, 0), roll(one, 2, 0), zero_tile)):
        nod[14 + spot, 32:40] = tile

    @pl.when(first_x)
    def _():
        nod[0:5] = jnp.zeros((5, ROWS, 128), jnp.float32)
        sig[0:2] = jnp.zeros((2, ROWS, 128), jnp.float32)

    @pl.when(last_x)
    def _():
        sig[14:15] = jnp.zeros((1, ROWS, 128), jnp.float32)

    nod[5] = nod[5] - nod[4]
    nod[14] = nod[14] - nod[13]

    @pl.when(last_x)
    def _():
        nod[14:18] = jnp.zeros((4, ROWS, 128), jnp.float32)

    @pl.when(first_y)
    def _():
        nod[:, 40:48] = jnp.zeros((18, 8, 128), jnp.float32)

    @pl.when(last_y)
    def _():
        nod[:, 32:40] = jnp.zeros((18, 8, 128), jnp.float32)

    def place(x):
        return x + 4 if x < 0 else (x + 5 if x < 8 else x + 6)

    inv, steps = coefficients(48.0, 30.0, 4)
    steps = steps + [None]
    nupd, nres = upd.at[0], res.at[0]
    planes = []
    for turn, step in enumerate(steps):
        lo, hi = -3 + turn, 10 - turn
        get = (lambda x: nod[place(x)]) if turn == 0 else (lambda x: nupd[x + 3])
        here = get(lo - 1)
        before = None
        for x in range(lo - 1, hi + 1):
            after = get(x + 1)
            sg = sig[x + 4]
            flux_x = sg * (after - here)
            if x >= lo:
                flux_y = sg * (next_y(here) - here)
                flux_z = sg * (next_z(here) - here)
                applied = (flux_x - before) + (flux_y - prev_y(flux_y)) + (flux_z - prev_z(flux_z))
                if turn == 0:
                    u = here * inv
                    r = here - applied * inv
                else:
                    u = here
                    r = nres[x + 3] - applied
                if step is not None:
                    weight = row_mask * step[1]
                    weight = weight if side(x) is None else weight * side(x)
                    new = step[0] * u + weight * r
                    nupd[x + 3] = new
                    nres[x + 3] = r
                    if 0 <= x < 9:
                        node_sum[x] = u + new if turn == 0 else node_sum[x] + new
                else:
                    planes.append(r)
                    if x % 2 == 1:
                        total = planes[x - 1] + 0.5 * planes[x]
                        if x > 1:
                            total = total + 0.5 * planes[x - 2]
                        red[x // 2, 8:40] = total[0:32]
                        red[x // 2, 0:8] = total[40:48] * keep_lo
                    if x == 7:
                        red[4, 8:40] = 0.5 * r[0:32]
                        red[4, 0:8] = 0.5 * r[40:48] * keep_lo
            before = flux_x
            here = after

    thin = [red[x, pl.ds(8, 16, stride=2)] + 0.5 * (red[x, pl.ds(9, 16, stride=2)] + red[x, pl.ds(7, 16, stride=2)])
            for x in range(5)]
    wide = jnp.concatenate(
        [jnp.concatenate([p[0:8] for p in thin], axis=0), jnp.concatenate([p[8:16] for p in thin], axis=0)], axis=1)
    coarse = dot(wide, rest_z)
    for x in range(5):
        cf_main[9 + x] = coarse[8 * x:8 * x + 8]
    cf_distant, cf_close = spread(cf_main, cf_pack, cf_got, cf_far, (x3_send, x3_recv), 9, 5)
    for copy in cf_distant[2:] + cf_close[:4] + cf_distant[:2] + cf_close[6:] + cf_close[4:6]:
        copy.start()
    for copy in cs_distant + cs_close:
        copy.wait()

    far_low, low_block, own_block, high_block, far_high = received(cs_got, cs_far, 2)
    halo = far_low[:3] + low_block + own_block + high_block + far_high
    for x in range(18):
        s_one[x] = cs_main[x] * cm_one[0, x]
        s_two[x] = halo[x] * cm_one[1, x]
    s_one[18], s_two[18] = zero_tile, zero_tile

    def lanes3(n):
        return lax.broadcasted_iota(jnp.int32, (n, 8, 128), 2)

    def coarse_both_y(one, two, ahead=True):
        turn_one, turn_two = roll(one, 64, 2), roll(two, 64, 2)
        pick = lanes3(one.shape[0]) < 64
        mixed, other = jnp.where(pick, turn_one, turn_two), jnp.where(pick, turn_two, turn_one)
        rows = lax.broadcasted_iota(jnp.int32, one.shape, 1)
        behind = (roll(jnp.where(rows == 7, other, one), 1, 1), roll(jnp.where(rows == 7, mixed, two), 1, 1))
        if not ahead:
            return None, behind
        return (roll(jnp.where(rows == 0, mixed, one), -1, 1), roll(jnp.where(rows == 0, other, two), -1, 1)), behind

    def coarse_next_z(f):
        return jnp.where(lanes3(f.shape[0]) % 64 == 63, 0.0, roll(f, -1, 2))

    def coarse_prev_z(f):
        return jnp.where(lanes3(f.shape[0]) % 64 == 0, 0.0, roll(f, 1, 2))

    _, (back_one, back_two) = coarse_both_y(s_one[...], s_two[...], False)
    s_back[0, 0], s_back[0, 1] = back_one, back_two
    s_back[1, 0], s_back[1, 1] = coarse_prev_z(s_one[...]), coarse_prev_z(s_two[...])

    for copy in cf_distant + cf_close:
        copy.wait()

    far_low, low_block, own_block, high_block, far_high = received(cf_got, cf_far, 3)
    halo = far_low + low_block + own_block + high_block + far_high
    where_plane = [0, 1, 2, 4, 5, 6, 7, 9, 10, 11, 12, 14, 15, 16, 17, 19, 20, 21, 22]
    extra = {-4: (3, gx > 1), 0: (8, gx > 0), 4: (13, None), 8: (18, None)}
    for x in range(-7, 12):
        one, two = cf_main[where_plane[x + 7]], halo[where_plane[x + 7]]
        if x in extra:
            spot, valid = extra[x]
            add_one, add_two = cf_main[spot], halo[spot]
            if valid is not None:
                add_one, add_two = add_one * f32(valid), add_two * f32(valid)
            one, two = one + add_one, two + add_two
        g_one[x + 7] = one * cm_one[0, x + 7]
        g_two[x + 7] = two * cm_one[1, x + 7]

    inv, steps = coefficients(96.0, 100.0, 8)
    f_one, f_two = g_one[...], g_two[...]
    r_one = r_two = None
    answer = None
    low = -7
    for turn, (c_old, c_res) in enumerate(steps):
        n = f_one.shape[0]
        sg_one, sg_two = s_one[low + 7:low + 7 + n], s_two[low + 7:low + 7 + n]
        x_one = sg_one[:-1] * (f_one[1:] - f_one[:-1])
        x_two = sg_two[:-1] * (f_two[1:] - f_two[:-1])
        mid_one, mid_two = f_one[1:-1], f_two[1:-1]
        inner = slice(low + 8, low + 6 + n)
        ahead_y, behind_y = coarse_both_y(mid_one, mid_two)
        results = []
        for k, (f, x_flux, s) in enumerate(((mid_one, x_one, sg_one[1:-1]), (mid_two, x_two, sg_two[1:-1]))):
            ahead = s * ((ahead_y[k] - f) + (coarse_next_z(f) - f))
            behind = s_back[0, k, inner] * (behind_y[k] - f) + s_back[1, k, inner] * (roll(f, 1, 2) - f)
            results.append((x_flux[1:] - x_flux[:-1]) + (ahead + behind))
        low += 1
        if turn == 0:
            r_one, r_two = mid_one - results[0] * inv, mid_two - results[1] * inv
            mid_one, mid_two = mid_one * inv, mid_two * inv
            answer = [mid_one[6:11], mid_two[6:11]]
        else:
            r_one, r_two = r_one[1:-1] - results[0], r_two[1:-1] - results[1]
        n -= 2
        f_one = c_old * mid_one + c_res * (cm_one[0, low + 7:low + 7 + n] * r_one)
        f_two = c_old * mid_two + c_res * (cm_one[1, low + 7:low + 7 + n] * r_two)
        answer = [answer[0] + f_one[-low:5 - low], answer[1] + f_two[-low:5 - low]]

    coarse_k = lax.broadcasted_iota(jnp.int32, (128, 256), 0)
    fine_k = lax.broadcasted_iota(jnp.int32, (128, 256), 1)
    same = coarse_k // 64 == fine_k // 128
    apart = (fine_k % 128) - 2 * (coarse_k % 64)
    grow = jnp.where(same, jnp.where(apart == 0, 1.0, jnp.where(jnp.abs(apart) == 1, 0.5, 0.0)), 0.0)
    body = dot(answer[0].reshape(40, 128), grow)
    edge = dot(answer[1].reshape(40, 128), grow[:, 0:128])
    for x in range(5):
        fine[x, 0:8] = body[8 * x:8 * x + 8, 0:128]
        fine[x, 8:16] = body[8 * x:8 * x + 8, 128:256]
        fine[x, 16:24] = edge[8 * x:8 * x + 8]

    own, nxt = None, None
    half_rows = []
    for x in range(5):
        a, b = fine[x, 0:16], fine[x, 1:17]
        red[x, pl.ds(0, 16, stride=2)] = a
        red[x, pl.ds(1, 16, stride=2)] = 0.5 * (a + b)
        red[x, 32:40] = fine[x, 16:24]
    for x in range(9):
        value = red[x // 2] if x % 2 == 0 else 0.5 * (red[x // 2] + red[x // 2 + 1])
        node_sum[x, 0:40] = node_sum[x, 0:40] + value
    keep_next = [keep_hi, keep_right]
    for x in range(8):
        here = node_sum[x, 0:32]
        after = node_sum[x + 1, 0:32]
        if x == 7:
            after = after * keep_right
        shifted = roll(node_sum[x], -1, 0)[0:32]
        last = (row[0:32] == 31) & last_y
        shifted = jnp.where(last, 0.0, shifted)
        out[0, x] = acc[0, x, 0:32] + (after - here)
        out[1, x] = acc[1, x, 0:32] + (shifted - here)
        out[2, x] = acc[2, x, 0:32] + (jnp.where(lane_end[0:32], 0.0, roll(here, -1, 1)) - here)


def solution(mesh):
    nx, ny = mesh.shape["gx"], mesh.shape["gy"]
    f32 = jnp.float32
    dma = pltpu.SemaphoreType.DMA

    def shards(right_side, classes, table):
        return pl.pallas_call(
            functools.partial(kernel, nx, ny),
            out_shape=jax.ShapeDtypeStruct(right_side.shape, f32),
            in_specs=[pl.BlockSpec(memory_space=pltpu.HBM)] * 3,
            out_specs=pl.BlockSpec(memory_space=pltpu.VMEM),
            scratch_shapes=[
                pltpu.VMEM((3, 14, ROWS, 128), f32),
                pltpu.VMEM((8, 32, 128), jnp.int32),
                pltpu.VMEM((16, ROWS, 128), f32),
                pltpu.VMEM((3, 14, ROWS, 128), f32),
                pltpu.VMEM((3, 14, ROWS, 128), f32),
                pltpu.VMEM((8, ROWS, 128), f32),
                pltpu.VMEM((3, 14, ROWS, 128), f32),
                pltpu.VMEM((3, 8, ROWS, 128), f32),
                pltpu.VMEM((8, 2, 8, 128), f32),
                pltpu.VMEM((9, 2, 8, 128), f32),
                pltpu.VMEM((15, 2, 8, 128), f32),
                pltpu.VMEM((16, 2, 8, 128), f32),
                pltpu.VMEM((7, 8, 128), f32),
                pltpu.VMEM((7, 8, 128), f32),
                pltpu.VMEM((18, ROWS, 128), f32),
                pltpu.VMEM((9, ROWS, 128), f32),
                pltpu.VMEM((5, 40, 128), f32),
                pltpu.VMEM((19, 8, 128), f32),
                pltpu.VMEM((2, 5, 8, 128), f32),
                pltpu.VMEM((3, 2, 2, 8, 128), f32),
                pltpu.VMEM((2, 2, 8, 128), f32),
                pltpu.VMEM((23, 8, 128), f32),
                pltpu.VMEM((2, 5, 8, 128), f32),
                pltpu.VMEM((3, 2, 3, 8, 128), f32),
                pltpu.VMEM((2, 2, 8, 128), f32),
                pltpu.SMEM((16,), f32),
                pltpu.VMEM((2, 19, 8, 128), f32),
                pltpu.VMEM((19, 8, 128), f32),
                pltpu.VMEM((19, 8, 128), f32),
                pltpu.VMEM((19, 8, 128), f32),
                pltpu.VMEM((19, 8, 128), f32),
                pltpu.VMEM((2, 2, 19, 8, 128), f32),
                pltpu.VMEM((5, 24, 128), f32),
                dma((3,)), dma((12,)), dma((12,)), dma((2,)), dma((2,)), dma((8,)), dma((8,)),
                dma((14,)), dma((14,)), dma((14,)), dma((14,)),
            ],
            compiler_params=pltpu.CompilerParams(
                collective_id=0, has_side_effects=True, vmem_limit_bytes=40 * 2**20),
            name="cycle",
        )(*(pltpu.with_memory_space_constraint(a, pltpu.HBM) for a in (right_side, classes, table)))

    return jax.shard_map(
        shards,
        mesh=mesh,
        in_specs=(P(None, "gx", "gy", None), P("gx", "gy", None), P()),
        out_specs=P(None, "gx", "gy", None),
        check_vma=False,
    )
```

```python
import functools

import jax
import jax.numpy as jnp
from jax import lax
from jax.experimental import pallas as pl
from jax.experimental.pallas import tpu as pltpu
from jax.sharding import PartitionSpec as P

MESH = pl.DeviceIdType.MESH
ROWS = 48


def coefficients(top, ratio, count):
    low = top / ratio
    center = 0.5 * (top + low)
    radius = 0.5 * (top - low)
    sharp = center / radius
    rho = 1.0 / sharp
    steps = []
    for _ in range(1, count):
        rho_next = 1.0 / (2.0 * sharp - rho)
        steps.append((rho_next * rho, 2.0 * rho_next / radius))
        rho = rho_next
    return 1.0 / center, steps


def roll(value, shift, axis):
    return pltpu.roll(value, shift % value.shape[axis], axis)


def kernel(nx, ny, rhs, classes, table, out, base, kinds, sig, upd, upd_next, drop, res, acc,
           pack_dn, pack_up, got_dn, got_up, turn_pack, turn_got, nod, node_sum, red, cs_main, cs_pack, cs_got, cs_far,
           cf_main, cf_pack, cf_got, cf_far, values_in, cm_one, g_one, g_two, s_one, s_two, s_back, fine,
           sem_in, send, recv, far_send, far_recv, x2_send, x2_recv, cs_send, cs_recv, x3_send, x3_recv):
    gx, gy = lax.axis_index("gx"), lax.axis_index("gy")
    first_x, last_x, first_y, last_y = gx == 0, gx == nx - 1, gy == 0, gy == ny - 1

    def at(dx, dy):
        return (lax.rem(gx + dx + nx, nx), lax.rem(gy + dy + ny, ny))

    near = [(1, 1), (1, -1), (-1, 1), (-1, -1), (1, 0), (-1, 0), (0, 1), (0, -1)]

    def remote(source, target, sems, index, where):
        return pltpu.make_async_remote_copy(
            src_ref=source, dst_ref=target, send_sem=sems[0].at[index], recv_sem=sems[1].at[index],
            device_id=at(*where), device_id_type=MESH)

    barrier = pltpu.get_barrier_semaphore()
    for where in near:
        pl.semaphore_signal(barrier, inc=1, device_id=at(*where), device_id_type=MESH)
    loads = [
        pltpu.make_async_copy(table, values_in, sem_in.at[2]),
        pltpu.make_async_copy(classes, kinds, sem_in.at[1]),
        pltpu.make_async_copy(rhs, base.at[:, 3:11, 0:32], sem_in.at[0]),
    ]
    for copy in loads:
        copy.start()

    pl.semaphore_wait(barrier, len(near))
    x1 = (send, recv)
    first = [
        remote(rhs.at[1:3, 0:3], base.at[1:3, 11:14, 0:32], x1, 1, (-1, 0)),
        remote(rhs.at[1:3, 5:8], base.at[1:3, 0:3, 0:32], x1, 0, (1, 0)),
        remote(rhs.at[0:1, 0:2], base.at[0:1, 11:13, 0:32], x1, 10, (-1, 0)),
        remote(rhs.at[0:1, 5:8], base.at[0:1, 0:3, 0:32], x1, 11, (1, 0)),
    ]
    for copy in first:
        copy.start()
    for copy in loads:
        copy.wait()

    values = [values_in[k] for k in range(16)]
    for x in range(8):
        code = kinds[x]
        level = values
        for bit in range(4):
            flag = (code & (1 << bit)) != 0
            level = [jnp.where(flag, level[2 * i + 1], level[2 * i]) for i in range(len(level) // 2)]
        sig[x + 4, 0:32] = level[0]

    sub = lax.broadcasted_iota(jnp.int32, (8, 128), 0)
    lower = sub < 4
    for x in range(8):
        ux, uy, uz = (base[c, x + 3, 0:8] for c in range(3))
        sg = sig[x + 4, 0:8]
        pack_dn[x, 0] = jnp.where(lower, ux, roll(uy, 4, 0))
        pack_dn[x, 1] = jnp.where(lower, uz, roll(sg, 4, 0))
        ux, uy, uz = (base[c, x + 3, 24:32] for c in range(3))
        sg = sig[x + 4, 24:32]
        pack_up[x, 0] = jnp.where(lower, roll(uy, 4, 0), ux)
        pack_up[x, 1] = jnp.where(lower, roll(sg, 4, 0), uz)
    for x in range(8):
        pack_up[8, 0, x:x + 1] = sig[x + 4, 27:28]
    pack_up[8, 1] = jnp.zeros((8, 128), jnp.float32)

    second = [
        remote(pack_dn.at[0:2], got_dn.at[12:14], x1, 2, (-1, -1)),
        remote(pack_up.at[0:3], got_up.at[13:16], x1, 3, (-1, 1)),
        remote(pack_dn.at[5:8], got_dn.at[9:12], x1, 4, (1, -1)),
        remote(pack_up.at[4:8], got_up.at[9:13], x1, 5, (1, 1)),
        remote(pack_dn, got_dn.at[0:8], x1, 6, (0, -1)),
        remote(pack_up, got_up.at[0:9], x1, 7, (0, 1)),
        remote(sig.at[10:12, 0:32], sig.at[2:4, 0:32], x1, 8, (1, 0)),
        remote(sig.at[4:6, 0:32], sig.at[12:14, 0:32], x1, 9, (-1, 0)),
    ]
    for copy in second[0:4] + second[6:8] + second[4:6]:
        copy.start()
    far = (far_send, far_recv)
    later = [
        remote(sig.at[8:10, 0:32], sig.at[0:2, 0:32], far, 0, (1, 0)),
        remote(sig.at[6:7, 0:32], sig.at[14:15, 0:32], far, 1, (-1, 0)),
    ]

    lane = lax.broadcasted_iota(jnp.int32, (ROWS, 128), 1)
    row = lax.broadcasted_iota(jnp.int32, (ROWS, 128), 0)
    lane_end, lane_start = lane == 127, lane == 0
    f32 = lambda flag: flag.astype(jnp.float32)
    keep_hi, keep_lo = 1.0 - f32(last_y), 1.0 - f32(first_y)
    row_mask = jnp.where(row < 32, 1.0, jnp.where(row < 40, keep_hi, keep_lo))
    row_zero = (row[0:8] == 0) & first_y

    def next_z(f):
        return jnp.where(lane_end, 0.0, roll(f, -1, 1))

    def prev_z(f):
        return jnp.where(lane_start, 0.0, roll(f, 1, 1))

    def next_y(f):
        return roll(f, -1, 0)

    def prev_y(f):
        return roll(f, 1, 0)

    def prev_y_inside(f):
        moved = roll(f, 1, 0)
        return jnp.concatenate([jnp.where(row_zero, 0.0, moved[0:8]), moved[8:]], axis=0)

    fine_z = lax.broadcasted_iota(jnp.int32, (256, 128), 0)
    packed_z = lax.broadcasted_iota(jnp.int32, (256, 128), 1)
    half = fine_z // 128 == packed_z // 64
    apart = (fine_z % 128) - 2 * (packed_z % 64)
    mean_z = jnp.where(half & ((apart == 0) | (apart == 1)), 0.125, 0.0)
    rest_z = jnp.where(half, jnp.where(apart == 0, 1.0, jnp.where(jnp.abs(apart) == 1, 0.5, 0.0)), 0.0)

    def dot(value, weights):
        weights = weights.astype(jnp.bfloat16)
        total = None
        for _ in range(3):
            part = value.astype(jnp.bfloat16)
            value = value - part.astype(jnp.float32)
            product = jnp.dot(part, weights, preferred_element_type=jnp.float32)
            total = product if total is None else total + product
        return total

    for x in range(4):
        red[x, 8:40] = sig[2 * x + 4, 0:32] + sig[2 * x + 5, 0:32]
    pairs = [red[x, pl.ds(8, 16, stride=2)] + red[x, pl.ds(9, 16, stride=2)] for x in range(4)]
    wide = jnp.concatenate(
        [jnp.concatenate([p[0:8] for p in pairs], axis=0), jnp.concatenate([p[8:16] for p in pairs], axis=0)], axis=1)
    coarse = 2.0 * dot(wide, mean_z)
    for x in range(4):
        cs_main[7 + x] = coarse[8 * x:8 * x + 8]

    plane_x = lax.broadcasted_iota(jnp.int32, (19, 8, 128), 0) - 7 + 4 * gx
    plane_ok = (plane_x >= 0) & (plane_x < 4 * nx)
    left3 = lax.broadcasted_iota(jnp.int32, (19, 8, 128), 2) < 64
    cm_one[0] = jnp.where(plane_ok, 1.0, 0.0)
    cm_one[1] = jnp.where(plane_ok, jnp.where(left3, keep_hi, keep_lo), 0.0)

    left = lax.broadcasted_iota(jnp.int32, (8, 128), 1) < 64

    def flip(tile):
        return roll(tile, 64, 1)

    def halves(a, b):
        if b is None:
            return a, flip(a)
        return jnp.where(left, a, flip(b)), jnp.where(left, flip(a), b)

    def unhalve(dn, up):
        return jnp.where(left, dn, flip(up)), jnp.where(left, flip(dn), up)

    def spread(main, pack, got, far_got, sems, own, count):
        tiles = [main[own + i] for i in range(count)] + [None]
        pairs = [halves(tiles[0], tiles[1]), halves(tiles[2], tiles[3])]
        odd = [halves(tiles[1], tiles[2]), halves(tiles[3], tiles[4])]
        if count == 5:
            pairs.append(halves(tiles[4], None))
        number = len(pairs)
        for i, (dn, up) in enumerate(pairs):
            pack[0, i] = dn
            pack[1, i] = up
        for i, (one, two) in enumerate((odd, pairs[:2])):
            pack[0, 3 + i] = jnp.where(lower, one[0], roll(two[0], 4, 0))
            pack[1, 3 + i] = jnp.where(lower, roll(one[1], 4, 0), two[1])
        block = main.at[own:own + count]
        size, end = count - 1, own + 2 * count
        reach = 4 if count == 5 else 3
        distant = [
            remote(main.at[own + 1:own + count], main.at[0:size], sems, 0, (2, 0)),
            remote(main.at[own:own + reach], main.at[end:end + reach], sems, 1, (-2, 0)),
        ]
        for i, dx in enumerate((2, -2)):
            for j, dy in enumerate((-1, 1)):
                distant.append(remote(pack.at[j, 3 + i], far_got.at[i, j], sems, 2 + 2 * i + j, (dx, dy)))
        close = []
        for i, dx in enumerate((1, -1, 0)):
            for j, dy in enumerate((-1, 1)):
                close.append(remote(pack.at[j, 0:number], got.at[i, j, 0:number], sems, 6 + 2 * i + j, (dx, dy)))
        close.append(remote(block, main.at[own - count:own], sems, 12, (1, 0)))
        close.append(remote(block, main.at[own + count:own + 2 * count], sems, 13, (-1, 0)))
        return distant, close

    def received(got, far_got, number):
        planes = []
        for spot in (0, 2, 1):
            block = []
            for i in range(number):
                block += list(unhalve(got[spot, 0, i], got[spot, 1, i]))
            planes.append(block[:5] if number == 3 else block)
        sides = []
        for i in range(2):
            dn, up = far_got[i, 0], far_got[i, 1]
            sides.append(list(unhalve(dn, roll(up, 4, 0))) + list(unhalve(roll(dn, 4, 0), up)))
        return sides[0], planes[0], planes[1], planes[2], sides[1]

    cs_distant, cs_close = spread(cs_main, cs_pack, cs_got, cs_far, (cs_send, cs_recv), 7, 4)

    def spot_dn(x):
        return x if 0 <= x < 8 else (12 + x if x < 0 else 4 + x)

    def spot_up(x):
        return x if 0 <= x < 8 else (13 + x if x < 0 else 5 + x)

    zero_tile = jnp.zeros((8, 128), jnp.float32)

    def unpack(planes):
        for x in planes:
            if x == 10:
                for c in range(3):
                    base[c, x + 3, 32:40] = zero_tile
                sig[x + 4, 32:40] = zero_tile
            elif x > -4:
                a, b = got_dn[spot_dn(x), 0], got_dn[spot_dn(x), 1]
                base[0, x + 3, 32:40] = a * keep_hi
                base[1, x + 3, 32:40] = roll(a, 4, 0) * keep_hi
                base[2, x + 3, 32:40] = b * keep_hi
                sig[x + 4, 32:40] = roll(b, 4, 0) * keep_hi
            else:
                sig[x + 4, 32:40] = zero_tile
            a, b = got_up[spot_up(x), 0], got_up[spot_up(x), 1]
            if x > -4:
                base[0, x + 3, 40:48] = a * keep_lo
                base[1, x + 3, 40:48] = roll(a, 4, 0) * keep_lo
                base[2, x + 3, 40:48] = b * keep_lo
            sg = roll(b, 4, 0)
            if 0 <= x < 8:
                sg = jnp.where(sub == 3, got_up[8, 0, x:x + 1], sg)
            sig[x + 4, 40:48] = sg * keep_lo

    keep_left, keep_right = 1.0 - f32(first_x), 1.0 - f32(last_x)

    def side(x):
        return keep_left if x < 0 else (keep_right if x > 7 else None)

    inv, edge_steps = coefficients(20.0, 30.0, 4)

    def edge_turn(turn, lo, hi):
        c_old, c_res = edge_steps[turn]
        source, target = ((base, upd), (upd, upd_next), (upd_next, None))[turn]
        shift = 3 if turn == 0 else 2
        scaled = row_mask * c_res
        before = None
        here = [source[c, lo - 1 + shift] for c in range(3)]
        for x in range(lo - 1, hi + 1):
            after = [None if (c == 0 and x == hi) else source[c, x + 1 + shift] for c in range(3)]
            ux, uy, uz = here
            cy = (next_z(ux) - ux) - (after[2] - uz)
            cz = (after[1] - uy) - (next_y(ux) - ux)
            if x == -1:
                cy, cz = cy * keep_left, cz * keep_left
            if x >= lo:
                cx = (next_y(uz) - uz) - (next_z(uy) - uy)
                sg = sig[x + 4]
                applied = [
                    (prev_y_inside(cz) - cz) - (prev_z(cy) - cy) + sg * ux,
                    (prev_z(cx) - cx) - (before[1] - cz) + sg * uy,
                    (before[0] - cy) - (prev_y_inside(cx) - cx) + sg * uz,
                ]
                weight = scaled if side(x) is None else scaled * side(x)
                rest = []
                for c in range(3):
                    if turn == 0:
                        u = here[c] * inv
                        r = here[c] - applied[c] * inv
                    else:
                        u = here[c]
                        r = res[c, x + 2] - applied[c]
                    new = c_old * u + weight * r
                    if turn < 2:
                        target[c, x + 2] = new
                        res[c, x + 2] = r
                        if 0 <= x < 8:
                            acc[c, x] = u + new if turn == 0 else acc[c, x] + new
                    else:
                        answer = acc[c, x] + new
                        acc[c, x] = answer
                        rest.append(base[c, x + 3] - sg * answer)
                if turn == 2:
                    rx, ry, rz = rest
                    total = (ry - prev_y(ry)) + (rz - prev_z(rz)) + rx
                    if x not in (0, lo) or x == 5:
                        total = total - drop[x - 1]
                    nod[x + 5, 0:32] = total[0:32]
                    drop[x] = rx
            before = (cy, cz)
            here = after

    for copy in (second[4], second[5]):
        copy.wait()
    unpack(range(8))
    edge_turn(0, 1, 6)
    edge_turn(1, 2, 5)
    edge_turn(2, 3, 4)

    for copy in (first[0], first[2], second[0], second[1], second[7]):
        copy.wait()
    unpack(range(8, 11))
    for copy in later:
        copy.start()

    @pl.when(last_x)
    def _():
        base[:, 11:14] = jnp.zeros((3, 3, ROWS, 128), jnp.float32)
        sig[12:14] = jnp.zeros((2, ROWS, 128), jnp.float32)

    edge_turn(0, 7, 9)
    edge_turn(1, 6, 8)
    edge_turn(2, 5, 7)
    nod[13, 0:32] = drop[7, 0:32]

    x2 = (x2_send, x2_recv)
    swap = [
        remote(nod.at[9:14, 0:32], nod.at[0:5, 0:32], x2, 0, (1, 0)),
        remote(nod.at[5:9, 0:32], nod.at[14:18, 0:32], x2, 1, (-1, 0)),
        remote(turn_pack.at[0:2], turn_got.at[0:2], x2, 2, (1, 1)),
        remote(turn_pack.at[2:4], turn_got.at[2:4], x2, 3, (1, -1)),
        remote(turn_pack.at[4:6], turn_got.at[4:6], x2, 4, (-1, 1)),
        remote(turn_pack.at[6], turn_got.at[6], x2, 5, (-1, -1)),
        remote(nod.at[5:14, 24:32], nod.at[5:14, 40:48], x2, 6, (0, 1)),
        remote(nod.at[5:14, 0:8], nod.at[5:14, 32:40], x2, 7, (0, -1)),
    ]
    up = [nod[9 + i, 24:32] for i in range(5)]
    turn_pack[0] = jnp.where(sub >= 3, up[4], jnp.where(sub == 0, roll(up[0], 1, 0), roll(up[1], 3, 0)))
    turn_pack[1] = jnp.where(lower, roll(up[2], 4, 0), up[3])
    dn = [nod[9 + i, 0:8] for i in range(5)]
    turn_pack[2] = jnp.where(lower, dn[4], roll(dn[3], 4, 0))
    turn_pack[3] = jnp.where(lower, dn[2], roll(dn[1], 4, 0))
    for copy in (swap[2], swap[3], swap[0]):
        copy.start()

    for copy in (first[1], first[3], second[2], second[3], second[6]):
        copy.wait()
    unpack(range(-4, 0))

    @pl.when(first_x)
    def _():
        base[:, 0:3] = jnp.zeros((3, 3, ROWS, 128), jnp.float32)
        sig[2:4] = jnp.zeros((2, ROWS, 128), jnp.float32)

    edge_turn(0, -2, 0)
    edge_turn(1, -1, 1)
    edge_turn(2, 0, 2)
    nod[8, 0:32] = nod[8, 0:32] - drop[2, 0:32]
    up = [nod[5 + i, 24:32] for i in range(4)]
    turn_pack[4] = jnp.where(lower, roll(up[1], 4, 0), up[0])
    turn_pack[5] = jnp.where(lower, roll(up[3], 4, 0), up[2])
    dn = [nod[5 + i, 0:8] for i in range(3)]
    turn_pack[6] = jnp.where(lower, dn[0], jnp.where(sub < 6, roll(dn[1], 4, 0), roll(dn[2], 6, 0)))
    for copy in (swap[4], swap[5], swap[6], swap[7], swap[1]):
        copy.start()
    for copy in cs_close + cs_distant:
        copy.start()

    for copy in later + swap:
        copy.wait()
    one, two = turn_got[0], turn_got[1]
    for spot, tile in enumerate((roll(one, 7, 0), roll(one, 5, 0), roll(two, 4, 0), two, one)):
        nod[spot, 40:48] = tile
    one, two = turn_got[2], turn_got[3]
    for spot, tile in enumerate((zero_tile, roll(two, 4, 0), two, roll(one, 4, 0), one)):
        nod[spot, 32:40] = tile
    one, two = turn_got[4], turn_got[5]
    for spot, tile in enumerate((one, roll(one, 4, 0), two, roll(two, 4, 0))):
        nod[14 + spot, 40:48] = tile
    one = turn_got[6]
    for spot, tile in enumerate((one, roll(one, 4, 0), roll(one, 2, 0), zero_tile)):
        nod[14 + spot, 32:40] = tile

    @pl.when(first_x)
    def _():
        nod[0:5] = jnp.zeros((5, ROWS, 128), jnp.float32)
        sig[0:2] = jnp.zeros((2, ROWS, 128), jnp.float32)

    @pl.when(last_x)
    def _():
        sig[14:15] = jnp.zeros((1, ROWS, 128), jnp.float32)

    nod[5] = nod[5] - nod[4]
    nod[14] = nod[14] - nod[13]

    @pl.when(last_x)
    def _():
        nod[14:18] = jnp.zeros((4, ROWS, 128), jnp.float32)

    @pl.when(first_y)
    def _():
        nod[:, 40:48] = jnp.zeros((18, 8, 128), jnp.float32)

    @pl.when(last_y)
    def _():
        nod[:, 32:40] = jnp.zeros((18, 8, 128), jnp.float32)

    def place(x):
        return x + 4 if x < 0 else (x + 5 if x < 8 else x + 6)

    inv, steps = coefficients(48.0, 30.0, 4)
    steps = steps + [None]
    nupd, nres = upd.at[0], res.at[0]
    planes = []
    for turn, step in enumerate(steps):
        lo, hi = -3 + turn, 10 - turn
        get = (lambda x: nod[place(x)]) if turn == 0 else (lambda x: nupd[x + 3])
        here = get(lo - 1)
        before = None
        for x in range(lo - 1, hi + 1):
            after = get(x + 1)
            sg = sig[x + 4]
            flux_x = sg * (after - here)
            if x >= lo:
                flux_y = sg * (next_y(here) - here)
                flux_z = sg * (next_z(here) - here)
                applied = (flux_x - before) + (flux_y - prev_y(flux_y)) + (flux_z - prev_z(flux_z))
                if turn == 0:
                    u = here * inv
                    r = here - applied * inv
                else:
                    u = here
                    r = nres[x + 3] - applied
                if step is not None:
                    weight = row_mask * step[1]
                    weight = weight if side(x) is None else weight * side(x)
                    new = step[0] * u + weight * r
                    nupd[x + 3] = new
                    nres[x + 3] = r
                    if 0 <= x < 9:
                        node_sum[x] = u + new if turn == 0 else node_sum[x] + new
                else:
                    planes.append(r)
                    if x % 2 == 1:
                        total = planes[x - 1] + 0.5 * planes[x]
                        if x > 1:
                            total = total + 0.5 * planes[x - 2]
                        red[x // 2, 8:40] = total[0:32]
                        red[x // 2, 0:8] = total[40:48] * keep_lo
                    if x == 7:
                        red[4, 8:40] = 0.5 * r[0:32]
                        red[4, 0:8] = 0.5 * r[40:48] * keep_lo
            before = flux_x
            here = after

    thin = [red[x, pl.ds(8, 16, stride=2)] + 0.5 * (red[x, pl.ds(9, 16, stride=2)] + red[x, pl.ds(7, 16, stride=2)])
            for x in range(5)]
    wide = jnp.concatenate(
        [jnp.concatenate([p[0:8] for p in thin], axis=0), jnp.concatenate([p[8:16] for p in thin], axis=0)], axis=1)
    coarse = dot(wide, rest_z)
    for x in range(5):
        cf_main[9 + x] = coarse[8 * x:8 * x + 8]
    cf_distant, cf_close = spread(cf_main, cf_pack, cf_got, cf_far, (x3_send, x3_recv), 9, 5)
    for copy in cf_distant[2:] + cf_close[:4] + cf_distant[:2] + cf_close[6:] + cf_close[4:6]:
        copy.start()
    for copy in cs_distant + cs_close:
        copy.wait()

    far_low, low_block, own_block, high_block, far_high = received(cs_got, cs_far, 2)
    halo = far_low[:3] + low_block + own_block + high_block + far_high
    for x in range(18):
        s_one[x] = cs_main[x] * cm_one[0, x]
        s_two[x] = halo[x] * cm_one[1, x]
    s_one[18], s_two[18] = zero_tile, zero_tile

    def lanes3(n):
        return lax.broadcasted_iota(jnp.int32, (n, 8, 128), 2)

    def coarse_both_y(one, two, ahead=True):
        turn_one, turn_two = roll(one, 64, 2), roll(two, 64, 2)
        pick = lanes3(one.shape[0]) < 64
        mixed, other = jnp.where(pick, turn_one, turn_two), jnp.where(pick, turn_two, turn_one)
        rows = lax.broadcasted_iota(jnp.int32, one.shape, 1)
        behind = (roll(jnp.where(rows == 7, other, one), 1, 1), roll(jnp.where(rows == 7, mixed, two), 1, 1))
        if not ahead:
            return None, behind
        return (roll(jnp.where(rows == 0, mixed, one), -1, 1), roll(jnp.where(rows == 0, other, two), -1, 1)), behind

    def coarse_next_z(f):
        return jnp.where(lanes3(f.shape[0]) % 64 == 63, 0.0, roll(f, -1, 2))

    def coarse_prev_z(f):
        return jnp.where(lanes3(f.shape[0]) % 64 == 0, 0.0, roll(f, 1, 2))

    _, (back_one, back_two) = coarse_both_y(s_one[...], s_two[...], False)
    s_back[0, 0], s_back[0, 1] = back_one, back_two
    s_back[1, 0], s_back[1, 1] = coarse_prev_z(s_one[...]), coarse_prev_z(s_two[...])

    for copy in cf_distant + cf_close:
        copy.wait()

    far_low, low_block, own_block, high_block, far_high = received(cf_got, cf_far, 3)
    halo = far_low + low_block + own_block + high_block + far_high
    where_plane = [0, 1, 2, 4, 5, 6, 7, 9, 10, 11, 12, 14, 15, 16, 17, 19, 20, 21, 22]
    extra = {-4: (3, gx > 1), 0: (8, gx > 0), 4: (13, None), 8: (18, None)}
    for x in range(-7, 12):
        one, two = cf_main[where_plane[x + 7]], halo[where_plane[x + 7]]
        if x in extra:
            spot, valid = extra[x]
            add_one, add_two = cf_main[spot], halo[spot]
            if valid is not None:
                add_one, add_two = add_one * f32(valid), add_two * f32(valid)
            one, two = one + add_one, two + add_two
        g_one[x + 7] = one * cm_one[0, x + 7]
        g_two[x + 7] = two * cm_one[1, x + 7]

    inv, steps = coefficients(96.0, 100.0, 8)
    f_one, f_two = g_one[...], g_two[...]
    r_one = r_two = None
    answer = None
    low = -7
    for turn, (c_old, c_res) in enumerate(steps):
        n = f_one.shape[0]
        sg_one, sg_two = s_one[low + 7:low + 7 + n], s_two[low + 7:low + 7 + n]
        x_one = sg_one[:-1] * (f_one[1:] - f_one[:-1])
        x_two = sg_two[:-1] * (f_two[1:] - f_two[:-1])
        mid_one, mid_two = f_one[1:-1], f_two[1:-1]
        inner = slice(low + 8, low + 6 + n)
        ahead_y, behind_y = coarse_both_y(mid_one, mid_two)
        results = []
        for k, (f, x_flux, s) in enumerate(((mid_one, x_one, sg_one[1:-1]), (mid_two, x_two, sg_two[1:-1]))):
            ahead = s * ((ahead_y[k] - f) + (coarse_next_z(f) - f))
            behind = s_back[0, k, inner] * (behind_y[k] - f) + s_back[1, k, inner] * (roll(f, 1, 2) - f)
            results.append((x_flux[1:] - x_flux[:-1]) + (ahead + behind))
        low += 1
        if turn == 0:
            r_one, r_two = mid_one - results[0] * inv, mid_two - results[1] * inv
            mid_one, mid_two = mid_one * inv, mid_two * inv
            answer = [mid_one[6:11], mid_two[6:11]]
        else:
            r_one, r_two = r_one[1:-1] - results[0], r_two[1:-1] - results[1]
        n -= 2
        f_one = c_old * mid_one + c_res * (cm_one[0, low + 7:low + 7 + n] * r_one)
        f_two = c_old * mid_two + c_res * (cm_one[1, low + 7:low + 7 + n] * r_two)
        answer = [answer[0] + f_one[-low:5 - low], answer[1] + f_two[-low:5 - low]]

    coarse_k = lax.broadcasted_iota(jnp.int32, (128, 256), 0)
    fine_k = lax.broadcasted_iota(jnp.int32, (128, 256), 1)
    same = coarse_k // 64 == fine_k // 128
    apart = (fine_k % 128) - 2 * (coarse_k % 64)
    grow = jnp.where(same, jnp.where(apart == 0, 1.0, jnp.where(jnp.abs(apart) == 1, 0.5, 0.0)), 0.0)
    body = dot(answer[0].reshape(40, 128), grow)
    edge = dot(answer[1].reshape(40, 128), grow[:, 0:128])
    for x in range(5):
        fine[x, 0:8] = body[8 * x:8 * x + 8, 0:128]
        fine[x, 8:16] = body[8 * x:8 * x + 8, 128:256]
        fine[x, 16:24] = edge[8 * x:8 * x + 8]

    own, nxt = None, None
    half_rows = []
    for x in range(5):
        a, b = fine[x, 0:16], fine[x, 1:17]
        red[x, pl.ds(0, 16, stride=2)] = a
        red[x, pl.ds(1, 16, stride=2)] = 0.5 * (a + b)
        red[x, 32:40] = fine[x, 16:24]
    for x in range(9):
        value = red[x // 2] if x % 2 == 0 else 0.5 * (red[x // 2] + red[x // 2 + 1])
        node_sum[x, 0:40] = node_sum[x, 0:40] + value
    keep_next = [keep_hi, keep_right]
    for x in range(8):
        here = node_sum[x, 0:32]
        after = node_sum[x + 1, 0:32]
        if x == 7:
            after = after * keep_right
        shifted = roll(node_sum[x], -1, 0)[0:32]
        last = (row[0:32] == 31) & last_y
        shifted = jnp.where(last, 0.0, shifted)
        out[0, x] = acc[0, x, 0:32] + (after - here)
        out[1, x] = acc[1, x, 0:32] + (shifted - here)
        out[2, x] = acc[2, x, 0:32] + (jnp.where(lane_end[0:32], 0.0, roll(here, -1, 1)) - here)


def solution(mesh):
    nx, ny = mesh.shape["gx"], mesh.shape["gy"]
    f32 = jnp.float32
    dma = pltpu.SemaphoreType.DMA

    def shards(right_side, classes, table):
        return pl.pallas_call(
            functools.partial(kernel, nx, ny),
            out_shape=jax.ShapeDtypeStruct(right_side.shape, f32),
            in_specs=[pl.BlockSpec(memory_space=pltpu.HBM)] * 3,
            out_specs=pl.BlockSpec(memory_space=pltpu.VMEM),
            scratch_shapes=[
                pltpu.VMEM((3, 14, ROWS, 128), f32),
                pltpu.VMEM((8, 32, 128), jnp.int32),
                pltpu.VMEM((16, ROWS, 128), f32),
                pltpu.VMEM((3, 14, ROWS, 128), f32),
                pltpu.VMEM((3, 14, ROWS, 128), f32),
                pltpu.VMEM((8, ROWS, 128), f32),
                pltpu.VMEM((3, 14, ROWS, 128), f32),
                pltpu.VMEM((3, 8, ROWS, 128), f32),
                pltpu.VMEM((8, 2, 8, 128), f32),
                pltpu.VMEM((9, 2, 8, 128), f32),
                pltpu.VMEM((15, 2, 8, 128), f32),
                pltpu.VMEM((16, 2, 8, 128), f32),
                pltpu.VMEM((7, 8, 128), f32),
                pltpu.VMEM((7, 8, 128), f32),
                pltpu.VMEM((18, ROWS, 128), f32),
                pltpu.VMEM((9, ROWS, 128), f32),
                pltpu.VMEM((6, 40, 128), f32),
                pltpu.VMEM((19, 8, 128), f32),
                pltpu.VMEM((2, 5, 8, 128), f32),
                pltpu.VMEM((3, 2, 2, 8, 128), f32),
                pltpu.VMEM((2, 2, 8, 128), f32),
                pltpu.VMEM((23, 8, 128), f32),
                pltpu.VMEM((2, 5, 8, 128), f32),
                pltpu.VMEM((3, 2, 3, 8, 128), f32),
                pltpu.VMEM((2, 2, 8, 128), f32),
                pltpu.SMEM((16,), f32),
                pltpu.VMEM((2, 19, 8, 128), f32),
                pltpu.VMEM((19, 8, 128), f32),
                pltpu.VMEM((19, 8, 128), f32),
                pltpu.VMEM((19, 8, 128), f32),
                pltpu.VMEM((19, 8, 128), f32),
                pltpu.VMEM((2, 2, 19, 8, 128), f32),
                pltpu.VMEM((5, 24, 128), f32),
                dma((3,)), dma((12,)), dma((12,)), dma((2,)), dma((2,)), dma((8,)), dma((8,)),
                dma((14,)), dma((14,)), dma((14,)), dma((14,)),
            ],
            compiler_params=pltpu.CompilerParams(
                collective_id=0, has_side_effects=True, vmem_limit_bytes=40 * 2**20),
            name="cycle",
        )(*(pltpu.with_memory_space_constraint(a, pltpu.HBM) for a in (right_side, classes, table)))

    return jax.shard_map(
        shards,
        mesh=mesh,
        in_specs=(P(None, "gx", "gy", None), P("gx", "gy", None), P()),
        out_specs=P(None, "gx", "gy", None),
        check_vma=False,
    )
```

```python
import functools

import jax
import jax.numpy as jnp
from jax import lax
from jax.experimental import pallas as pl
from jax.experimental.pallas import tpu as pltpu
from jax.sharding import PartitionSpec as P

MESH = pl.DeviceIdType.MESH
ROWS = 48


def coefficients(top, ratio, count):
    low = top / ratio
    center = 0.5 * (top + low)
    radius = 0.5 * (top - low)
    sharp = center / radius
    rho = 1.0 / sharp
    steps = []
    for _ in range(1, count):
        rho_next = 1.0 / (2.0 * sharp - rho)
        steps.append((rho_next * rho, 2.0 * rho_next / radius))
        rho = rho_next
    return 1.0 / center, steps


def roll(value, shift, axis):
    return pltpu.roll(value, shift % value.shape[axis], axis)


def kernel(nx, ny, rhs, classes, table, out, base, kinds, sig, upd, upd_next, drop, res, acc,
           pack_dn, pack_up, got_dn, got_up, turn_pack, turn_got, nod, node_sum, red, cs_main, cs_pack, cs_got, cs_far,
           cf_main, cf_pack, cf_got, cf_far, values_in, cm_one, g_one, g_two, s_one, s_two, s_back, fine,
           sem_in, send, recv, far_send, far_recv, x2_send, x2_recv, cs_send, cs_recv, x3_send, x3_recv):
    gx, gy = lax.axis_index("gx"), lax.axis_index("gy")
    first_x, last_x, first_y, last_y = gx == 0, gx == nx - 1, gy == 0, gy == ny - 1

    def at(dx, dy):
        return (lax.rem(gx + dx + nx, nx), lax.rem(gy + dy + ny, ny))

    near = [(1, 1), (1, -1), (-1, 1), (-1, -1), (1, 0), (-1, 0), (0, 1), (0, -1)]

    def remote(source, target, sems, index, where):
        return pltpu.make_async_remote_copy(
            src_ref=source, dst_ref=target, send_sem=sems[0].at[index], recv_sem=sems[1].at[index],
            device_id=at(*where), device_id_type=MESH)

    barrier = pltpu.get_barrier_semaphore()
    for where in near:
        pl.semaphore_signal(barrier, inc=1, device_id=at(*where), device_id_type=MESH)
    loads = [
        pltpu.make_async_copy(table, values_in, sem_in.at[2]),
        pltpu.make_async_copy(classes, kinds, sem_in.at[1]),
        pltpu.make_async_copy(rhs, base.at[:, 3:11, 0:32], sem_in.at[0]),
    ]
    for copy in loads:
        copy.start()

    pl.semaphore_wait(barrier, len(near))
    x1 = (send, recv)
    first = [
        remote(rhs.at[1:3, 0:3], base.at[1:3, 11:14, 0:32], x1, 1, (-1, 0)),
        remote(rhs.at[1:3, 5:8], base.at[1:3, 0:3, 0:32], x1, 0, (1, 0)),
        remote(rhs.at[0:1, 0:2], base.at[0:1, 11:13, 0:32], x1, 10, (-1, 0)),
        remote(rhs.at[0:1, 5:8], base.at[0:1, 0:3, 0:32], x1, 11, (1, 0)),
    ]
    for copy in first:
        copy.start()
    for copy in loads:
        copy.wait()

    values = [values_in[k] for k in range(16)]
    for x in range(8):
        code = kinds[x]
        level = values
        for bit in range(4):
            flag = (code & (1 << bit)) != 0
            level = [jnp.where(flag, level[2 * i + 1], level[2 * i]) for i in range(len(level) // 2)]
        sig[x + 4, 0:32] = level[0]

    sub = lax.broadcasted_iota(jnp.int32, (8, 128), 0)
    lower = sub < 4
    for x in range(8):
        ux, uy, uz = (base[c, x + 3, 0:8] for c in range(3))
        sg = sig[x + 4, 0:8]
        pack_dn[x, 0] = jnp.where(lower, ux, roll(uy, 4, 0))
        pack_dn[x, 1] = jnp.where(lower, uz, roll(sg, 4, 0))
        ux, uy, uz = (base[c, x + 3, 24:32] for c in range(3))
        sg = sig[x + 4, 24:32]
        pack_up[x, 0] = jnp.where(lower, roll(uy, 4, 0), ux)
        pack_up[x, 1] = jnp.where(lower, roll(sg, 4, 0), uz)
    for x in range(8):
        pack_up[8, 0, x:x + 1] = sig[x + 4, 27:28]
    pack_up[8, 1] = jnp.zeros((8, 128), jnp.float32)

    second = [
        remote(pack_dn.at[0:2], got_dn.at[12:14], x1, 2, (-1, -1)),
        remote(pack_up.at[0:3], got_up.at[13:16], x1, 3, (-1, 1)),
        remote(pack_dn.at[5:8], got_dn.at[9:12], x1, 4, (1, -1)),
        remote(pack_up.at[4:8], got_up.at[9:13], x1, 5, (1, 1)),
        remote(pack_dn, got_dn.at[0:8], x1, 6, (0, -1)),
        remote(pack_up, got_up.at[0:9], x1, 7, (0, 1)),
        remote(sig.at[10:12, 0:32], sig.at[2:4, 0:32], x1, 8, (1, 0)),
        remote(sig.at[4:6, 0:32], sig.at[12:14, 0:32], x1, 9, (-1, 0)),
    ]
    for copy in second[0:4] + second[6:8] + second[4:6]:
        copy.start()
    far = (far_send, far_recv)
    later = [
        remote(sig.at[8:10, 0:32], sig.at[0:2, 0:32], far, 0, (1, 0)),
        remote(sig.at[6:7, 0:32], sig.at[14:15, 0:32], far, 1, (-1, 0)),
    ]

    lane = lax.broadcasted_iota(jnp.int32, (ROWS, 128), 1)
    row = lax.broadcasted_iota(jnp.int32, (ROWS, 128), 0)
    lane_end, lane_start = lane == 127, lane == 0
    f32 = lambda flag: flag.astype(jnp.float32)
    keep_hi, keep_lo = 1.0 - f32(last_y), 1.0 - f32(first_y)
    row_mask = jnp.where(row < 32, 1.0, jnp.where(row < 40, keep_hi, keep_lo))
    row_zero = (row[0:8] == 0) & first_y

    def next_z(f):
        return jnp.where(lane_end, 0.0, roll(f, -1, 1))

    def prev_z(f):
        return jnp.where(lane_start, 0.0, roll(f, 1, 1))

    def next_y(f):
        return roll(f, -1, 0)

    def prev_y(f):
        return roll(f, 1, 0)

    def prev_y_inside(f):
        moved = roll(f, 1, 0)
        return jnp.concatenate([jnp.where(row_zero, 0.0, moved[0:8]), moved[8:]], axis=0)

    fine_z = lax.broadcasted_iota(jnp.int32, (256, 128), 0)
    packed_z = lax.broadcasted_iota(jnp.int32, (256, 128), 1)
    half = fine_z // 128 == packed_z // 64
    apart = (fine_z % 128) - 2 * (packed_z % 64)
    mean_z = jnp.where(half & ((apart == 0) | (apart == 1)), 0.125, 0.0)
    rest_z = jnp.where(half, jnp.where(apart == 0, 1.0, jnp.where(jnp.abs(apart) == 1, 0.5, 0.0)), 0.0)

    def dot(value, weights):
        weights = weights.astype(jnp.bfloat16)
        total = None
        for _ in range(3):
            part = value.astype(jnp.bfloat16)
            value = value - part.astype(jnp.float32)
            product = jnp.dot(part, weights, preferred_element_type=jnp.float32)
            total = product if total is None else total + product
        return total

    for x in range(4):
        red[x, 8:40] = sig[2 * x + 4, 0:32] + sig[2 * x + 5, 0:32]
    pairs = [red[x, pl.ds(8, 16, stride=2)] + red[x, pl.ds(9, 16, stride=2)] for x in range(4)]
    wide = jnp.concatenate(
        [jnp.concatenate([p[0:8] for p in pairs], axis=0), jnp.concatenate([p[8:16] for p in pairs], axis=0)], axis=1)
    coarse = 2.0 * dot(wide, mean_z)
    for x in range(4):
        cs_main[7 + x] = coarse[8 * x:8 * x + 8]

    plane_x = lax.broadcasted_iota(jnp.int32, (19, 8, 128), 0) - 7 + 4 * gx
    plane_ok = (plane_x >= 0) & (plane_x < 4 * nx)
    left3 = lax.broadcasted_iota(jnp.int32, (19, 8, 128), 2) < 64
    cm_one[0] = jnp.where(plane_ok, 1.0, 0.0)
    cm_one[1] = jnp.where(plane_ok, jnp.where(left3, keep_hi, keep_lo), 0.0)

    left = lax.broadcasted_iota(jnp.int32, (8, 128), 1) < 64

    def flip(tile):
        return roll(tile, 64, 1)

    def halves(a, b):
        if b is None:
            return a, flip(a)
        return jnp.where(left, a, flip(b)), jnp.where(left, flip(a), b)

    def unhalve(dn, up):
        return jnp.where(left, dn, flip(up)), jnp.where(left, flip(dn), up)

    def spread(main, pack, got, far_got, sems, own, count):
        tiles = [main[own + i] for i in range(count)] + [None]
        pairs = [halves(tiles[0], tiles[1]), halves(tiles[2], tiles[3])]
        odd = [halves(tiles[1], tiles[2]), halves(tiles[3], tiles[4])]
        if count == 5:
            pairs.append(halves(tiles[4], None))
        number = len(pairs)
        for i, (dn, up) in enumerate(pairs):
            pack[0, i] = dn
            pack[1, i] = up
        for i, (one, two) in enumerate((odd, pairs[:2])):
            pack[0, 3 + i] = jnp.where(lower, one[0], roll(two[0], 4, 0))
            pack[1, 3 + i] = jnp.where(lower, roll(one[1], 4, 0), two[1])
        block = main.at[own:own + count]
        size, end = count - 1, own + 2 * count
        reach = 4 if count == 5 else 3
        distant = [
            remote(main.at[own + 1:own + count], main.at[0:size], sems, 0, (2, 0)),
            remote(main.at[own:own + reach], main.at[end:end + reach], sems, 1, (-2, 0)),
        ]
        for i, dx in enumerate((2, -2)):
            for j, dy in enumerate((-1, 1)):
                distant.append(remote(pack.at[j, 3 + i], far_got.at[i, j], sems, 2 + 2 * i + j, (dx, dy)))
        close = []
        for i, dx in enumerate((1, -1, 0)):
            for j, dy in enumerate((-1, 1)):
                close.append(remote(pack.at[j, 0:number], got.at[i, j, 0:number], sems, 6 + 2 * i + j, (dx, dy)))
        close.append(remote(block, main.at[own - count:own], sems, 12, (1, 0)))
        close.append(remote(block, main.at[own + count:own + 2 * count], sems, 13, (-1, 0)))
        return distant, close

    def received(got, far_got, number):
        planes = []
        for spot in (0, 2, 1):
            block = []
            for i in range(number):
                block += list(unhalve(got[spot, 0, i], got[spot, 1, i]))
            planes.append(block[:5] if number == 3 else block)
        sides = []
        for i in range(2):
            dn, up = far_got[i, 0], far_got[i, 1]
            sides.append(list(unhalve(dn, roll(up, 4, 0))) + list(unhalve(roll(dn, 4, 0), up)))
        return sides[0], planes[0], planes[1], planes[2], sides[1]

    cs_distant, cs_close = spread(cs_main, cs_pack, cs_got, cs_far, (cs_send, cs_recv), 7, 4)

    def spot_dn(x):
        return x if 0 <= x < 8 else (12 + x if x < 0 else 4 + x)

    def spot_up(x):
        return x if 0 <= x < 8 else (13 + x if x < 0 else 5 + x)

    zero_tile = jnp.zeros((8, 128), jnp.float32)

    def unpack(planes):
        for x in planes:
            if x == 10:
                for c in range(3):
                    base[c, x + 3, 32:40] = zero_tile
                sig[x + 4, 32:40] = zero_tile
            elif x > -4:
                a, b = got_dn[spot_dn(x), 0], got_dn[spot_dn(x), 1]
                base[0, x + 3, 32:40] = a * keep_hi
                base[1, x + 3, 32:40] = roll(a, 4, 0) * keep_hi
                base[2, x + 3, 32:40] = b * keep_hi
                sig[x + 4, 32:40] = roll(b, 4, 0) * keep_hi
            else:
                sig[x + 4, 32:40] = zero_tile
            a, b = got_up[spot_up(x), 0], got_up[spot_up(x), 1]
            if x > -4:
                base[0, x + 3, 40:48] = a * keep_lo
                base[1, x + 3, 40:48] = roll(a, 4, 0) * keep_lo
                base[2, x + 3, 40:48] = b * keep_lo
            sg = roll(b, 4, 0)
            if 0 <= x < 8:
                sg = jnp.where(sub == 3, got_up[8, 0, x:x + 1], sg)
            sig[x + 4, 40:48] = sg * keep_lo

    keep_left, keep_right = 1.0 - f32(first_x), 1.0 - f32(last_x)

    def side(x):
        return keep_left if x < 0 else (keep_right if x > 7 else None)

    inv, edge_steps = coefficients(20.0, 30.0, 4)

    def edge_turn(turn, lo, hi):
        c_old, c_res = edge_steps[turn]
        source, target = ((base, upd), (upd, upd_next), (upd_next, None))[turn]
        shift = 3 if turn == 0 else 2
        scaled = row_mask * c_res
        before = None
        here = [source[c, lo - 1 + shift] for c in range(3)]
        for x in range(lo - 1, hi + 1):
            after = [None if (c == 0 and x == hi) else source[c, x + 1 + shift] for c in range(3)]
            ux, uy, uz = here
            cy = (next_z(ux) - ux) - (after[2] - uz)
            cz = (after[1] - uy) - (next_y(ux) - ux)
            if x == -1:
                cy, cz = cy * keep_left, cz * keep_left
            if x >= lo:
                cx = (next_y(uz) - uz) - (next_z(uy) - uy)
                sg = sig[x + 4]
                applied = [
                    (prev_y_inside(cz) - cz) - (prev_z(cy) - cy) + sg * ux,
                    (prev_z(cx) - cx) - (before[1] - cz) + sg * uy,
                    (before[0] - cy) - (prev_y_inside(cx) - cx) + sg * uz,
                ]
                weight = scaled if side(x) is None else scaled * side(x)
                rest = []
                for c in range(3):
                    if turn == 0:
                        u = here[c] * inv
                        r = here[c] - applied[c] * inv
                    else:
                        u = here[c]
                        r = res[c, x + 2] - applied[c]
                    new = c_old * u + weight * r
                    if turn < 2:
                        target[c, x + 2] = new
                        res[c, x + 2] = r
                        if 0 <= x < 8:
                            acc[c, x] = u + new if turn == 0 else acc[c, x] + new
                    else:
                        answer = acc[c, x] + new
                        acc[c, x] = answer
                        rest.append(base[c, x + 3] - sg * answer)
                if turn == 2:
                    rx, ry, rz = rest
                    total = (ry - prev_y(ry)) + (rz - prev_z(rz)) + rx
                    if x not in (0, lo) or x == 5:
                        total = total - drop[x - 1]
                    nod[x + 5, 0:32] = total[0:32]
                    drop[x] = rx
            before = (cy, cz)
            here = after

    for copy in (second[4], second[5]):
        copy.wait()
    unpack(range(8))
    edge_turn(0, 1, 6)
    edge_turn(1, 2, 5)
    edge_turn(2, 3, 4)
    for copy in later:
        copy.start()

    for copy in (first[0], first[2], second[0], second[1], second[7]):
        copy.wait()
    unpack(range(8, 11))

    @pl.when(last_x)
    def _():
        base[:, 11:14] = jnp.zeros((3, 3, ROWS, 128), jnp.float32)
        sig[12:14] = jnp.zeros((2, ROWS, 128), jnp.float32)

    edge_turn(0, 7, 9)
    edge_turn(1, 6, 8)
    edge_turn(2, 5, 7)
    nod[13, 0:32] = drop[7, 0:32]

    x2 = (x2_send, x2_recv)
    swap = [
        remote(nod.at[9:14, 0:32], nod.at[0:5, 0:32], x2, 0, (1, 0)),
        remote(nod.at[5:9, 0:32], nod.at[14:18, 0:32], x2, 1, (-1, 0)),
        remote(turn_pack.at[0:2], turn_got.at[0:2], x2, 2, (1, 1)),
        remote(turn_pack.at[2:4], turn_got.at[2:4], x2, 3, (1, -1)),
        remote(turn_pack.at[4:6], turn_got.at[4:6], x2, 4, (-1, 1)),
        remote(turn_pack.at[6], turn_got.at[6], x2, 5, (-1, -1)),
        remote(nod.at[5:14, 24:32], nod.at[5:14, 40:48], x2, 6, (0, 1)),
        remote(nod.at[5:14, 0:8], nod.at[5:14, 32:40], x2, 7, (0, -1)),
    ]
    up = [nod[9 + i, 24:32] for i in range(5)]
    turn_pack[0] = jnp.where(sub >= 3, up[4], jnp.where(sub == 0, roll(up[0], 1, 0), roll(up[1], 3, 0)))
    turn_pack[1] = jnp.where(lower, roll(up[2], 4, 0), up[3])
    dn = [nod[9 + i, 0:8] for i in range(5)]
    turn_pack[2] = jnp.where(lower, dn[4], roll(dn[3], 4, 0))
    turn_pack[3] = jnp.where(lower, dn[2], roll(dn[1], 4, 0))
    for copy in (swap[2], swap[3], swap[0]):
        copy.start()

    for copy in (first[1], first[3], second[2], second[3], second[6]):
        copy.wait()
    unpack(range(-4, 0))

    @pl.when(first_x)
    def _():
        base[:, 0:3] = jnp.zeros((3, 3, ROWS, 128), jnp.float32)
        sig[2:4] = jnp.zeros((2, ROWS, 128), jnp.float32)

    edge_turn(0, -2, 0)
    edge_turn(1, -1, 1)
    edge_turn(2, 0, 2)
    nod[8, 0:32] = nod[8, 0:32] - drop[2, 0:32]
    up = [nod[5 + i, 24:32] for i in range(4)]
    turn_pack[4] = jnp.where(lower, roll(up[1], 4, 0), up[0])
    turn_pack[5] = jnp.where(lower, roll(up[3], 4, 0), up[2])
    dn = [nod[5 + i, 0:8] for i in range(3)]
    turn_pack[6] = jnp.where(lower, dn[0], jnp.where(sub < 6, roll(dn[1], 4, 0), roll(dn[2], 6, 0)))
    for copy in (swap[4], swap[5], swap[6], swap[7], swap[1]):
        copy.start()
    for copy in cs_close + cs_distant:
        copy.start()

    for copy in later + swap:
        copy.wait()
    one, two = turn_got[0], turn_got[1]
    for spot, tile in enumerate((roll(one, 7, 0), roll(one, 5, 0), roll(two, 4, 0), two, one)):
        nod[spot, 40:48] = tile
    one, two = turn_got[2], turn_got[3]
    for spot, tile in enumerate((zero_tile, roll(two, 4, 0), two, roll(one, 4, 0), one)):
        nod[spot, 32:40] = tile
    one, two = turn_got[4], turn_got[5]
    for spot, tile in enumerate((one, roll(one, 4, 0), two, roll(two, 4, 0))):
        nod[14 + spot, 40:48] = tile
    one = turn_got[6]
    for spot, tile in enumerate((one, roll(one, 4, 0), roll(one, 2, 0), zero_tile)):
        nod[14 + spot, 32:40] = tile

    @pl.when(first_x)
    def _():
        nod[0:5] = jnp.zeros((5, ROWS, 128), jnp.float32)
        sig[0:2] = jnp.zeros((2, ROWS, 128), jnp.float32)

    @pl.when(last_x)
    def _():
        sig[14:15] = jnp.zeros((1, ROWS, 128), jnp.float32)

    nod[5] = nod[5] - nod[4]
    nod[14] = nod[14] - nod[13]

    @pl.when(last_x)
    def _():
        nod[14:18] = jnp.zeros((4, ROWS, 128), jnp.float32)

    @pl.when(first_y)
    def _():
        nod[:, 40:48] = jnp.zeros((18, 8, 128), jnp.float32)

    @pl.when(last_y)
    def _():
        nod[:, 32:40] = jnp.zeros((18, 8, 128), jnp.float32)

    def place(x):
        return x + 4 if x < 0 else (x + 5 if x < 8 else x + 6)

    inv, steps = coefficients(48.0, 30.0, 4)
    steps = steps + [None]
    nupd, nres = upd.at[0], res.at[0]
    planes = []
    for turn, step in enumerate(steps):
        lo, hi = -3 + turn, 10 - turn
        get = (lambda x: nod[place(x)]) if turn == 0 else (lambda x: nupd[x + 3])
        here = get(lo - 1)
        before = None
        for x in range(lo - 1, hi + 1):
            after = get(x + 1)
            sg = sig[x + 4]
            flux_x = sg * (after - here)
            if x >= lo:
                flux_y = sg * (next_y(here) - here)
                flux_z = sg * (next_z(here) - here)
                applied = (flux_x - before) + (flux_y - prev_y(flux_y)) + (flux_z - prev_z(flux_z))
                if turn == 0:
                    u = here * inv
                    r = here - applied * inv
                else:
                    u = here
                    r = nres[x + 3] - applied
                if step is not None:
                    weight = row_mask * step[1]
                    weight = weight if side(x) is None else weight * side(x)
                    new = step[0] * u + weight * r
                    nupd[x + 3] = new
                    nres[x + 3] = r
                    if 0 <= x < 9:
                        node_sum[x] = u + new if turn == 0 else node_sum[x] + new
                else:
                    planes.append(r)
                    if x % 2 == 1:
                        total = planes[x - 1] + 0.5 * planes[x]
                        if x > 1:
                            total = total + 0.5 * planes[x - 2]
                        red[x // 2, 8:40] = total[0:32]
                        red[x // 2, 0:8] = total[40:48] * keep_lo
                    if x == 7:
                        red[4, 8:40] = 0.5 * r[0:32]
                        red[4, 0:8] = 0.5 * r[40:48] * keep_lo
            before = flux_x
            here = after

    thin = [red[x, pl.ds(8, 16, stride=2)] + 0.5 * (red[x, pl.ds(9, 16, stride=2)] + red[x, pl.ds(7, 16, stride=2)])
            for x in range(5)]
    wide = jnp.concatenate(
        [jnp.concatenate([p[0:8] for p in thin], axis=0), jnp.concatenate([p[8:16] for p in thin], axis=0)], axis=1)
    coarse = dot(wide, rest_z)
    for x in range(5):
        cf_main[9 + x] = coarse[8 * x:8 * x + 8]
    cf_distant, cf_close = spread(cf_main, cf_pack, cf_got, cf_far, (x3_send, x3_recv), 9, 5)
    for copy in cf_distant[2:] + cf_close[:4] + cf_distant[:2] + cf_close[6:] + cf_close[4:6]:
        copy.start()
    for copy in cs_distant + cs_close:
        copy.wait()

    far_low, low_block, own_block, high_block, far_high = received(cs_got, cs_far, 2)
    halo = far_low[:3] + low_block + own_block + high_block + far_high
    for x in range(18):
        s_one[x] = cs_main[x] * cm_one[0, x]
        s_two[x] = halo[x] * cm_one[1, x]
    s_one[18], s_two[18] = zero_tile, zero_tile

    def lanes3(n):
        return lax.broadcasted_iota(jnp.int32, (n, 8, 128), 2)

    def coarse_both_y(one, two, ahead=True):
        turn_one, turn_two = roll(one, 64, 2), roll(two, 64, 2)
        pick = lanes3(one.shape[0]) < 64
        mixed, other = jnp.where(pick, turn_one, turn_two), jnp.where(pick, turn_two, turn_one)
        rows = lax.broadcasted_iota(jnp.int32, one.shape, 1)
        behind = (roll(jnp.where(rows == 7, other, one), 1, 1), roll(jnp.where(rows == 7, mixed, two), 1, 1))
        if not ahead:
            return None, behind
        return (roll(jnp.where(rows == 0, mixed, one), -1, 1), roll(jnp.where(rows == 0, other, two), -1, 1)), behind

    def coarse_next_z(f):
        return jnp.where(lanes3(f.shape[0]) % 64 == 63, 0.0, roll(f, -1, 2))

    def coarse_prev_z(f):
        return jnp.where(lanes3(f.shape[0]) % 64 == 0, 0.0, roll(f, 1, 2))

    _, (back_one, back_two) = coarse_both_y(s_one[...], s_two[...], False)
    s_back[0, 0], s_back[0, 1] = back_one, back_two
    s_back[1, 0], s_back[1, 1] = coarse_prev_z(s_one[...]), coarse_prev_z(s_two[...])

    for copy in cf_distant + cf_close:
        copy.wait()

    far_low, low_block, own_block, high_block, far_high = received(cf_got, cf_far, 3)
    halo = far_low + low_block + own_block + high_block + far_high
    where_plane = [0, 1, 2, 4, 5, 6, 7, 9, 10, 11, 12, 14, 15, 16, 17, 19, 20, 21, 22]
    extra = {-4: (3, gx > 1), 0: (8, gx > 0), 4: (13, None), 8: (18, None)}
    for x in range(-7, 12):
        one, two = cf_main[where_plane[x + 7]], halo[where_plane[x + 7]]
        if x in extra:
            spot, valid = extra[x]
            add_one, add_two = cf_main[spot], halo[spot]
            if valid is not None:
                add_one, add_two = add_one * f32(valid), add_two * f32(valid)
            one, two = one + add_one, two + add_two
        g_one[x + 7] = one * cm_one[0, x + 7]
        g_two[x + 7] = two * cm_one[1, x + 7]

    inv, steps = coefficients(96.0, 100.0, 8)
    f_one, f_two = g_one[...], g_two[...]
    r_one = r_two = None
    answer = None
    low = -7
    for turn, (c_old, c_res) in enumerate(steps):
        n = f_one.shape[0]
        sg_one, sg_two = s_one[low + 7:low + 7 + n], s_two[low + 7:low + 7 + n]
        x_one = sg_one[:-1] * (f_one[1:] - f_one[:-1])
        x_two = sg_two[:-1] * (f_two[1:] - f_two[:-1])
        mid_one, mid_two = f_one[1:-1], f_two[1:-1]
        inner = slice(low + 8, low + 6 + n)
        ahead_y, behind_y = coarse_both_y(mid_one, mid_two)
        results = []
        for k, (f, x_flux, s) in enumerate(((mid_one, x_one, sg_one[1:-1]), (mid_two, x_two, sg_two[1:-1]))):
            ahead = s * ((ahead_y[k] - f) + (coarse_next_z(f) - f))
            behind = s_back[0, k, inner] * (behind_y[k] - f) + s_back[1, k, inner] * (roll(f, 1, 2) - f)
            results.append((x_flux[1:] - x_flux[:-1]) + (ahead + behind))
        low += 1
        if turn == 0:
            r_one, r_two = mid_one - results[0] * inv, mid_two - results[1] * inv
            mid_one, mid_two = mid_one * inv, mid_two * inv
            answer = [mid_one[6:11], mid_two[6:11]]
        else:
            r_one, r_two = r_one[1:-1] - results[0], r_two[1:-1] - results[1]
        n -= 2
        f_one = c_old * mid_one + c_res * (cm_one[0, low + 7:low + 7 + n] * r_one)
        f_two = c_old * mid_two + c_res * (cm_one[1, low + 7:low + 7 + n] * r_two)
        answer = [answer[0] + f_one[-low:5 - low], answer[1] + f_two[-low:5 - low]]

    coarse_k = lax.broadcasted_iota(jnp.int32, (128, 256), 0)
    fine_k = lax.broadcasted_iota(jnp.int32, (128, 256), 1)
    same = coarse_k // 64 == fine_k // 128
    apart = (fine_k % 128) - 2 * (coarse_k % 64)
    grow = jnp.where(same, jnp.where(apart == 0, 1.0, jnp.where(jnp.abs(apart) == 1, 0.5, 0.0)), 0.0)
    body = dot(answer[0].reshape(40, 128), grow)
    edge = dot(answer[1].reshape(40, 128), grow[:, 0:128])
    for x in range(5):
        fine[x, 0:8] = body[8 * x:8 * x + 8, 0:128]
        fine[x, 8:16] = body[8 * x:8 * x + 8, 128:256]
        fine[x, 16:24] = edge[8 * x:8 * x + 8]

    own, nxt = None, None
    half_rows = []
    for x in range(5):
        a, b = fine[x, 0:16], fine[x, 1:17]
        red[x, pl.ds(0, 16, stride=2)] = a
        red[x, pl.ds(1, 16, stride=2)] = 0.5 * (a + b)
        red[x, 32:40] = fine[x, 16:24]
    for x in range(9):
        value = red[x // 2] if x % 2 == 0 else 0.5 * (red[x // 2] + red[x // 2 + 1])
        node_sum[x, 0:40] = node_sum[x, 0:40] + value
    keep_next = [keep_hi, keep_right]
    for x in range(8):
        here = node_sum[x, 0:32]
        after = node_sum[x + 1, 0:32]
        if x == 7:
            after = after * keep_right
        shifted = roll(node_sum[x], -1, 0)[0:32]
        last = (row[0:32] == 31) & last_y
        shifted = jnp.where(last, 0.0, shifted)
        out[0, x] = acc[0, x, 0:32] + (after - here)
        out[1, x] = acc[1, x, 0:32] + (shifted - here)
        out[2, x] = acc[2, x, 0:32] + (jnp.where(lane_end[0:32], 0.0, roll(here, -1, 1)) - here)


def solution(mesh):
    nx, ny = mesh.shape["gx"], mesh.shape["gy"]
    f32 = jnp.float32
    dma = pltpu.SemaphoreType.DMA

    def shards(right_side, classes, table):
        return pl.pallas_call(
            functools.partial(kernel, nx, ny),
            out_shape=jax.ShapeDtypeStruct(right_side.shape, f32),
            in_specs=[pl.BlockSpec(memory_space=pltpu.HBM)] * 3,
            out_specs=pl.BlockSpec(memory_space=pltpu.VMEM),
            scratch_shapes=[
                pltpu.VMEM((3, 14, ROWS, 128), f32),
                pltpu.VMEM((8, 32, 128), jnp.int32),
                pltpu.VMEM((16, ROWS, 128), f32),
                pltpu.VMEM((3, 14, ROWS, 128), f32),
                pltpu.VMEM((3, 14, ROWS, 128), f32),
                pltpu.VMEM((8, ROWS, 128), f32),
                pltpu.VMEM((3, 14, ROWS, 128), f32),
                pltpu.VMEM((3, 8, ROWS, 128), f32),
                pltpu.VMEM((8, 2, 8, 128), f32),
                pltpu.VMEM((9, 2, 8, 128), f32),
                pltpu.VMEM((15, 2, 8, 128), f32),
                pltpu.VMEM((16, 2, 8, 128), f32),
                pltpu.VMEM((7, 8, 128), f32),
                pltpu.VMEM((7, 8, 128), f32),
                pltpu.VMEM((18, ROWS, 128), f32),
                pltpu.VMEM((9, ROWS, 128), f32),
                pltpu.VMEM((6, 40, 128), f32),
                pltpu.VMEM((19, 8, 128), f32),
                pltpu.VMEM((2, 5, 8, 128), f32),
                pltpu.VMEM((3, 2, 2, 8, 128), f32),
                pltpu.VMEM((2, 2, 8, 128), f32),
                pltpu.VMEM((23, 8, 128), f32),
                pltpu.VMEM((2, 5, 8, 128), f32),
                pltpu.VMEM((3, 2, 3, 8, 128), f32),
                pltpu.VMEM((2, 2, 8, 128), f32),
                pltpu.SMEM((16,), f32),
                pltpu.VMEM((2, 19, 8, 128), f32),
                pltpu.VMEM((19, 8, 128), f32),
                pltpu.VMEM((19, 8, 128), f32),
                pltpu.VMEM((19, 8, 128), f32),
                pltpu.VMEM((19, 8, 128), f32),
                pltpu.VMEM((2, 2, 19, 8, 128), f32),
                pltpu.VMEM((5, 24, 128), f32),
                dma((3,)), dma((12,)), dma((12,)), dma((2,)), dma((2,)), dma((8,)), dma((8,)),
                dma((14,)), dma((14,)), dma((14,)), dma((14,)),
            ],
            compiler_params=pltpu.CompilerParams(
                collective_id=0, has_side_effects=True, vmem_limit_bytes=40 * 2**20),
            name="cycle",
        )(*(pltpu.with_memory_space_constraint(a, pltpu.HBM) for a in (right_side, classes, table)))

    return jax.shard_map(
        shards,
        mesh=mesh,
        in_specs=(P(None, "gx", "gy", None), P("gx", "gy", None), P()),
        out_specs=P(None, "gx", "gy", None),
        check_vma=False,
    )
```
